128 devices in a mesh: dp: 16 (over z_hi, y, core), tensor: 8 (over z_lo, x).
Axes of the slice: x: 4, y: 4, z: 4 (z_hi: 2, z_lo: 2; z = z_hi * 2 + z_lo), core: 2. Of those that a mesh axis runs over, the one named last changes fastest.
Arguments:
- train_inputs: bfloat16 [32, 512, 4096], P('dp', None, 'tensor'), may hold values from -100 to 100
- train_grads: bfloat16 [32, 2, 512, 14336], P('dp', None, None, 'tensor'), may hold values from -100 to 100
- train_lengths: int32 [32], P('dp'), may hold values from 64 to 512, as said below
- query_inputs: bfloat16 [256, 128, 4096], P('dp', None, 'tensor'), may hold values from -100 to 100
- query_grads: bfloat16 [256, 2, 128, 14336], P('dp', None, None, 'tensor'), may hold values from -100 to 100
- query_lengths: int32 [256], P('dp'), may hold values from 16 to 128, as said below
- proj_in: bfloat16 [4096, 64], P('tensor'), may hold values from -0.09375 to 0.09375
- proj_out: bfloat16 [2, 14336, 64], P(None, 'tensor'), may hold values from -0.046875 to 0.046875
Outputs:
- scores: float32 [32, 256], P('dp')
The draws below stay inside these ranges and needn't reach their ends.
Inputs may be any that keep to these rules, and one draw needn't show every extreme that they name: `train_lengths`: some training sequence has exactly 512 live positions. `query_lengths`: some query generation has exactly 128 live positions.
All inputs are finite; a program needn't handle non-finite values.
Results may differ from the reference program's by a relative error of at most 0.0061.
Values sent between devices are 32-bit elements; how exact they have to be, the bound alone decides.
A program may use at most 128 MiB of HBM per device.

```python
import math
import jax
import jax.numpy as jnp
from jax import lax

D = 4096
FF = 14336
RANK = 64
LAYERS = 2
SEQ = 512
QLEN = 128
TRAIN = 32
QUERIES = 256


def shaped_field(key, noise_field, rise_factor, scale_low, scale_high):
    extent = noise_field.shape
    subkeys = jax.random.split(key, 2)
    row_shape = extent[:-1]
    row_scale = jnp.exp(jax.random.uniform(subkeys[0], row_shape, jnp.float32, math.log(scale_low), math.log(scale_high)))
    column_scale = jnp.exp(jax.random.uniform(subkeys[1], (extent[-1],), jnp.float32, math.log(scale_low), math.log(scale_high)))
    ramp_scale = jnp.exp(math.log(rise_factor) * (jnp.arange(extent[0], dtype=jnp.float32) / max(extent[0] - 1, 1) - 0.5))
    ramp_scale = ramp_scale.reshape((extent[0],) + (1,) * (len(extent) - 1))
    field_value = noise_field * row_scale[..., None] * column_scale
    return field_value * ramp_scale


def ragged(key, count_rows, longest):
    first_key, second_key = jax.random.split(key)
    place = jnp.arange(count_rows, dtype=jnp.int32)
    span_rows = max(count_rows - 1, 1)
    lower = longest // 8 + longest // 2 * place // span_rows
    upper = longest // 4 + (longest - longest // 4) * place // span_rows
    drawn = jax.random.randint(first_key, (count_rows,), lower, upper + 1, dtype=jnp.int32)
    chosen = jax.random.randint(second_key, (), 0, count_rows, dtype=jnp.int32)
    return jnp.where(place == chosen, longest, drawn).astype(jnp.int32)


def draw_train_inputs(key, part):
    key = jax.random.fold_in(key, 11)
    noise_key = jax.random.fold_in(key, 1)
    extent = (TRAIN, SEQ, D)
    noise_field = jax.random.truncated_normal(noise_key, -4.0, 4.0, extent, jnp.float32)
    return shaped_field(jax.random.fold_in(key, 2), noise_field, 3.0, 0.3, 3.0).astype(jnp.bfloat16)


def draw_train_grads(key, part):
    key = jax.random.fold_in(key, 12)
    noise_key = jax.random.fold_in(key, 1)
    extent = (TRAIN, LAYERS, SEQ, FF)
    noise_field = jax.random.truncated_normal(noise_key, -4.0, 4.0, extent, jnp.float32)
    return shaped_field(jax.random.fold_in(key, 2), noise_field, 3.0, 0.3, 3.0).astype(jnp.bfloat16)


def draw_query_inputs(key, part):
    key = jax.random.fold_in(key, 13)
    noise_key = jax.random.fold_in(key, 1)
    extent = (QUERIES, QLEN, D)
    noise_field = jax.random.truncated_normal(noise_key, -4.0, 4.0, extent, jnp.float32)
    return shaped_field(jax.random.fold_in(key, 2), noise_field, 1.0, 0.3, 3.0).astype(jnp.bfloat16)


def draw_query_grads(key, part):
    key = jax.random.fold_in(key, 14)
    noise_key = jax.random.fold_in(key, 1)
    extent = (QUERIES, LAYERS, QLEN, FF)
    noise_field = jax.random.truncated_normal(noise_key, -4.0, 4.0, extent, jnp.float32)
    return shaped_field(jax.random.fold_in(key, 2), noise_field, 1.0, 0.3, 3.0).astype(jnp.bfloat16)


def draw_train_lengths(key, part):
    key = jax.random.fold_in(key, 15)
    return ragged(key, TRAIN, SEQ)


def draw_query_lengths(key, part):
    key = jax.random.fold_in(key, 16)
    return ragged(key, QUERIES, QLEN)


def levels(own_key, dims, pieces, low, largest):
    factor_of = 1.0
    for dim, parts in pieces:
        draws = jax.random.uniform(jax.random.fold_in(jax.random.fold_in(own_key, 6), dim), (parts,), jnp.float32, low / len(pieces), largest / len(pieces))
        factor_of = factor_of * jnp.repeat(jnp.exp(draws), dims[dim] // parts).reshape((-1,) + (1,) * (len(dims) - 1 - dim))
    return factor_of


def bell_draw(stream_key, shape, spread, most, pieces=(), held_as=jnp.bfloat16):
    factor_of = levels(stream_key, shape, pieces, -0.22, 0.18) if pieces else 1.0
    values = jax.random.normal(stream_key, shape, jnp.float32) * spread * factor_of
    return jnp.minimum(jnp.maximum(values, -most), most).astype(held_as)


def setup_inputs(seed: int = 0) -> dict:
    arg_keys = jax.random.split(jax.random.key(seed), 9)
    train_inputs = draw_train_inputs(jax.random.fold_in(arg_keys[8], 71), 0)
    train_grads = draw_train_grads(jax.random.fold_in(arg_keys[8], 71), 0)
    train_lengths = draw_train_lengths(jax.random.fold_in(arg_keys[8], 71), 0)
    query_inputs = draw_query_inputs(jax.random.fold_in(arg_keys[8], 71), 0)
    query_grads = draw_query_grads(jax.random.fold_in(arg_keys[8], 71), 0)
    query_lengths = draw_query_lengths(jax.random.fold_in(arg_keys[8], 71), 0)
    proj_in = bell_draw(arg_keys[6], (D, RANK), D ** -0.5, 0.09375, ((0, 8),))
    proj_out = bell_draw(arg_keys[7], (LAYERS, FF, RANK), FF ** -0.5, 0.046875, ((1, 8),))
    return {"train_inputs": train_inputs, "train_grads": train_grads, "train_lengths": train_lengths, "query_inputs": query_inputs, "query_grads": query_grads, "query_lengths": query_lengths, "proj_in": proj_in, "proj_out": proj_out}


damping = 0.1

def damped(moment):
    size_r = moment.shape[-1]
    return moment + damping * jnp.trace(moment) / size_r * jnp.eye(size_r, dtype=jnp.float32)

def condition_one(sketch, chol_out, chol_in):
    left_solve = jax.scipy.linalg.cho_solve((chol_out, True), sketch)
    return jax.scipy.linalg.cho_solve((chol_in, True), left_solve.T).T

def sketch_example(inputs, gradient, length, proj_in, proj_out):
    seq_len = inputs.shape[0]
    keeper = (jnp.arange(seq_len, dtype=jnp.int32) < length).astype(jnp.float32)[:, None]
    input_proj = (jnp.dot(inputs.astype(jnp.float32), proj_in.astype(jnp.float32), preferred_element_type=jnp.float32) * keeper).astype(jnp.bfloat16)
    output_proj = jnp.concatenate([jnp.dot(gradient[layer].astype(jnp.float32), proj_out[layer].astype(jnp.float32), preferred_element_type=jnp.float32) for layer in range(LAYERS)], axis=1)
    output_proj = (output_proj * keeper).astype(jnp.bfloat16)
    wide_in = input_proj.astype(jnp.float32)
    wide_out = output_proj.astype(jnp.float32)
    sketch = jnp.dot(wide_out.T, wide_in, precision=lax.Precision.HIGHEST)
    in_moment = jnp.dot(wide_in.T, wide_in, precision=lax.Precision.HIGHEST)
    grouped = wide_out.reshape(seq_len, LAYERS, RANK)
    out_moment = jnp.einsum('skr,skq->krq', grouped, grouped, precision=lax.Precision.HIGHEST)
    return (sketch, in_moment, out_moment, jnp.sum(keeper))

def reference(train_inputs, train_grads, train_lengths, query_inputs, query_grads, query_lengths, proj_in, proj_out):

    def train_item(items):
        return sketch_example(items[0], items[1], items[2], proj_in, proj_out)

    def query_item(items):
        return sketch_example(items[0], items[1], items[2], proj_in, proj_out)[0]
    train_sketch, in_parts, out_parts, live_parts = lax.map(train_item, (train_inputs, train_grads, train_lengths))
    query_sketch = lax.map(query_item, (query_inputs, query_grads, query_lengths))
    total_live = jnp.sum(live_parts)
    in_moment = lax.optimization_barrier(jnp.sum(in_parts, axis=0)) / total_live
    out_moment = lax.optimization_barrier(jnp.sum(out_parts, axis=0)) / total_live
    chol_in = jnp.linalg.cholesky(damped(in_moment))
    chol_out = jax.vmap(lambda moment: jnp.linalg.cholesky(damped(moment)))(out_moment)
    conditioned = jax.vmap(jax.vmap(condition_one, in_axes=(0, 0, None)), in_axes=(0, None, None))(train_sketch.reshape(TRAIN, LAYERS, RANK, RANK), chol_out, chol_in)
    score_scale = 1.0 / (RANK * math.sqrt(SEQ * QLEN))
    return jnp.dot(conditioned.reshape(TRAIN, -1), query_sketch.reshape(QUERIES, -1).T, precision=lax.Precision.HIGHEST) * score_scale
```

```python
import functools
import math

import jax
import jax.numpy as jnp
from jax import lax
from jax.experimental import pallas as pl
from jax.experimental.pallas import tpu as pltpu
from jax.sharding import PartitionSpec as P

MESH = pl.DeviceIdType.MESH
F32 = jnp.float32
BF16 = jnp.bfloat16
DAMPING = 0.1
RANK = 64
BLOCK = 128
HALF = 64
TENSOR = 8
DP = 16
GENS = ((1, 3, 4), (3, 4, 1), (4, 1, 3))
DOUBLINGS = 7


def chebyshev():
    low = DAMPING / RANK
    high = 1.0 + low
    angle = math.acosh((high + low) / (high - low))
    gains = []
    n = 1
    for _ in range(DOUBLINGS):
        gains.append(2.0 * math.cosh(n * angle) ** 2 / math.cosh(2 * n * angle))
        n *= 2
    return 2.0 / (high + low), gains


def rem(a, b):
    return lax.rem(a, jnp.int32(b))


def div(a, b):
    return lax.div(a, jnp.int32(b))


def split(v):
    high = v.astype(BF16)
    return high, (v - high.astype(F32)).astype(BF16)


def kernel(
    tlen, qlen, tin, tgr, qin, qgr, pin, pout, out_ref,
    xin, xgr, win, wout, wip, wop,
    acc, recv1, recv2, recv3,
    mloc, mrecv1, msum, mrecv2, mfull,
    bloc, brecv1, bsum, ball,
    qall, msg, fin,
    lsem, wsem, s1, r1, s2, r2, s3, r3,
    ms1, mr1, ms2, mr2, ms3, mr3,
    bs1, br1, bs2, br2, qs, qr, fs, fr,
):
    d = lax.axis_index("dp").astype(jnp.int32)
    t = lax.axis_index("tensor").astype(jnp.int32)
    z, x = div(t, 4), rem(t, 4)

    def flip(m):
        m = jnp.int32(m)
        mx, mz = rem(m, 4), div(m, 4)
        low = rem(x + mx, 2)
        high = rem(div(x, 2) + div(mx, 2), 2)
        return rem(z + mz, 2) * 4 + high * 2 + low

    def remote(src, dst, ssem, rsem, dd, tt):
        return pltpu.make_async_remote_copy(
            src_ref=src, dst_ref=dst, send_sem=ssem, recv_sem=rsem,
            device_id=(dd, tt), device_id_type=MESH,
        )

    def load(r, j):
        item = flip(7 - j)
        slot = r * 8 + j
        if r == 0:
            e, p = div(item, 4), rem(item, 4)
            rows = pl.ds(pl.multiple_of(p * BLOCK, BLOCK), BLOCK)
            a, b = tin.at[e, rows, :], tgr.at[e, :, rows, :]
        else:
            q = item * 2 + (r - 1)
            a, b = qin.at[q], qgr.at[q]
        return (
            pltpu.make_async_copy(a, xin.at[slot], lsem.at[0, slot]),
            pltpu.make_async_copy(b, xgr.at[slot], lsem.at[1, slot]),
        )

    def start_load(r, j):
        for c in load(r, j):
            c.start()

    wcopies = (
        pltpu.make_async_copy(pin, win, wsem.at[0]),
        pltpu.make_async_copy(pout, wout, wsem.at[1]),
    )
    for c in wcopies:
        c.start()

    @pl.loop(0, 8)
    def _(j):
        start_load(0, j)

    barrier = pltpu.get_barrier_semaphore()

    def greet(dd, tt):
        pl.semaphore_signal(barrier, inc=1, device_id=(dd, tt), device_id_type=MESH)

    def is_me(dd, tt):
        return jnp.logical_and(dd == d, tt == t)

    @pl.loop(1, 8)
    def _(m):
        greet(d, flip(m))

    @pl.loop(1, 16)
    def _(j):
        greet(rem(d + j, DP), t)

    @pl.loop(0, 16)
    def _(j):
        dd, tt = t * 2 + div(j, 8), rem(j, 8)

        @pl.when(jnp.logical_not(is_me(dd, tt)))
        def _():
            greet(dd, tt)

        column = div(d, 2)

        @pl.when(jnp.logical_not(is_me(j, column)))
        def _():
            greet(j, column)

    for c in wcopies:
        c.wait()
    zero_in = jnp.zeros((pin.shape[0], RANK), BF16)
    w = win[...]
    wip[0] = jnp.concatenate([w, zero_in], axis=1)
    wip[1] = jnp.concatenate([zero_in, w], axis=1)
    zero_out = jnp.zeros((pout.shape[1], RANK), BF16)
    wop[0] = jnp.concatenate([wout[0], zero_out], axis=1)
    wop[1] = jnp.concatenate([zero_out, wout[1]], axis=1)

    on_diagonal = div(d, 2) == t

    @pl.when(on_diagonal)
    def _():
        pl.semaphore_wait(barrier, 52)

    @pl.when(jnp.logical_not(on_diagonal))
    def _():
        pl.semaphore_wait(barrier, 54)

    def step1(r, p, m):
        g = GENS[p][0]
        s = (m + g) % 8 if g == 4 else (
            m + 1 - 2 * (m % 2) if g == 1 else (m // 4) * 4 + 3 - m % 4
        ) if isinstance(m, int) else (
            rem(m + 4, 8) if g == 4 else m + 1 - 2 * rem(m, 2) if g == 1
            else div(m, 4) * 4 + 3 - rem(m, 4)
        )
        return remote(
            acc.at[r, p, m], recv1.at[r, p, s], s1.at[r, p, s], r1.at[r, p, s],
            d, flip(g),
        )

    def span1(p):
        _, g2, g3 = GENS[p]
        return (g2, g2 ^ g3, g3, 0)

    def step2(r, p, k):
        _, g2, g3 = GENS[p]
        return remote(
            acc.at[r, p, (g2, g2 ^ g3)[k]], recv2.at[r, p, k],
            s2.at[r, p, k], r2.at[r, p, k], d, flip(g2),
        )

    def step3(r, p):
        g3 = GENS[p][2]
        return remote(
            acc.at[r, p, g3], recv3.at[r, p], s3.at[r, p], r3.at[r, p], d, flip(g3)
        )

    def sends1(p):
        g1 = GENS[p][0]
        return tuple(s ^ g1 for s in span1(p))

    def begin1(r):
        for k in range(4):
            for p in range(3):
                step1(r, p, sends1(p)[k]).start()

    def begin2(r):
        for p in range(3):
            for k, s in enumerate(span1(p)):
                step1(r, p, s ^ GENS[p][0]).wait_recv()
                acc[r, p, s] = acc[r, p, s] + recv1[r, p, s]
                if k == 1:
                    step2(r, p, 1).start()
                if k == 0:
                    step2(r, p, 0).start()

    def begin3(r):
        for p in range(3):
            g3 = GENS[p][2]
            step2(r, p, 1).wait_recv()
            acc[r, p, g3] = acc[r, p, g3] + recv2[r, p, 1]
            step3(r, p).start()
            step2(r, p, 0).wait_recv()
            acc[r, p, 0] = acc[r, p, 0] + recv2[r, p, 0]

    def end3(r):
        parts = []
        for p in range(3):
            step3(r, p).wait_recv()
            parts.append(acc[r, p, 0] + recv3[r, p])
        return parts

    def drain(r):
        for p in range(3):
            for m in sends1(p):
                step1(r, p, m).wait_send()
            for k in range(2):
                step2(r, p, k).wait_send()
            step3(r, p).wait_send()

    def project(r, j):
        slot = r * 8 + j
        m = 7 - j
        for c in load(r, j):
            c.wait()
        acc[r, 0, m] = jnp.dot(
            xin[slot, :HALF], wip[0], preferred_element_type=F32
        ) + jnp.dot(xin[slot, HALF:], wip[1], preferred_element_type=F32)
        rows = jnp.dot(xgr[slot, 0], wop[0], preferred_element_type=F32) + jnp.dot(
            xgr[slot, 1], wop[1], preferred_element_type=F32
        )
        acc[r, 1, m] = rows[:HALF]
        acc[r, 2, m] = rows[HALF:]

    @pl.loop(0, 8)
    def _(j):
        start_load(1, j)
        project(0, j)
        m = 7 - j
        low = rem(m, 4)

        @pl.when(jnp.logical_or(low == 1, low == 2))
        def _():
            step1(0, 0, m).start()

        @pl.when(low >= 2)
        def _():
            step1(0, 1, m).start()

        @pl.when(m >= 4)
        def _():
            step1(0, 2, m).start()

    def project_some(r, low, high):
        @pl.loop(low, high)
        def _(j):
            if r == 1:
                start_load(2, j)
            project(r, j)

    row64 = lax.broadcasted_iota(jnp.int32, (HALF, BLOCK), 0)
    lane64 = lax.broadcasted_iota(jnp.int32, (HALF, BLOCK), 1)
    left = lane64 < HALF

    def finished(parts, length):
        position = jnp.where(left, row64, row64 + HALF)
        inputs = jnp.where(position < length, parts[0], 0.0)
        turned = pltpu.roll(inputs, HALF, 1)
        twice = jnp.concatenate(
            [jnp.where(left, inputs, turned), jnp.where(left, turned, inputs)], axis=0
        ).astype(BF16)
        outputs = jnp.concatenate(
            [
                jnp.where(row64 < length, parts[1], 0.0),
                jnp.where(row64 + HALF < length, parts[2], 0.0),
            ],
            axis=0,
        )
        return twice, outputs.astype(BF16), outputs.T.astype(BF16)

    def fold(full):
        return jnp.where(left, full[:HALF], full[HALF:])

    def query_sketch(r):
        length = qlen[t * 2 + (r - 1)]
        twice, _, turned = finished(end3(r), length)
        return fold(jnp.dot(turned, twice, preferred_element_type=F32))

    def share(r, m):
        return remote(
            qall.at[r - 1, t], qall.at[r - 1, t], qs.at[r - 1, m], qr.at[r - 1, m], d, flip(m)
        )

    def share_sketch(r):
        qall[r - 1, t] = query_sketch(r)
        for m in range(1, 8):
            share(r, m).start()

    def moment1(m):
        return remote(mloc.at[flip(m)], mrecv1.at[m], ms1.at[m], mr1.at[m], d, flip(m))

    def moment2(j):
        return remote(msum, mrecv2.at[d], ms2.at[j], mr2.at[j], rem(d + j, DP), t)

    def moment3(m):
        return remote(mfull.at[t], mfull.at[t], ms3.at[m], mr3.at[m], d, flip(m))

    def sketch1(m):
        return remote(
            bloc.at[rem(flip(m), 4)], brecv1.at[m], bs1.at[m], br1.at[m], d, flip(m)
        )

    mine = 2 * rem(d, 2) + z

    def sketch2(j):
        return remote(
            bsum, ball.at[mine, x], bs2.at[j], br2.at[mine, x], j, div(d, 2)
        )

    def train_finish():
        length = tlen[z] - x * BLOCK
        twice, outputs, turned = finished(end3(0), length)
        products = jnp.dot(
            turned, jnp.concatenate([outputs, twice], axis=1), preferred_element_type=F32
        )
        ins = lax.dot_general(
            twice, twice, (((0,), (0,)), ((), ())), preferred_element_type=F32
        )
        live = jnp.minimum(jnp.maximum(length, 0), BLOCK).astype(F32)
        mloc[0:4] = fold(products[:, :BLOCK]).reshape(4, 16, BLOCK)
        mloc[4:8] = jnp.where(left, ins[:HALF], live).reshape(4, 16, BLOCK)
        for m in range(1, 8):
            moment1(m).start()
        bloc[...] = fold(products[:, BLOCK:]).reshape(4, 16, BLOCK)
        for m in range(1, 4):
            sketch1(m).start()

    def moments_over_dp():
        total = mloc[t]
        for m in range(1, 8):
            moment1(m).wait_recv()
            total = total + mrecv1[m]
        msum[...] = total
        mrecv2[d] = total

        @pl.loop(1, 16)
        def _(j):
            moment2(j).start()

    def sketches_out():
        total = bloc[x]
        for m in range(1, 4):
            sketch1(m).wait_recv()
            total = total + brecv1[m]
        bsum[...] = total

        @pl.loop(0, 16)
        def _(j):
            me = is_me(j, div(d, 2))

            @pl.when(jnp.logical_not(me))
            def _():
                sketch2(j).start()

            @pl.when(me)
            def _():
                ball[mine, x] = total

    def moments_back():
        @pl.loop(1, 16)
        def _(j):
            moment2(j).wait_recv()

        total = mrecv2[0]
        for j in range(1, 16):
            total = total + mrecv2[j]
        mfull[t] = total
        for m in range(1, 8):
            moment3(m).start()

    def wide(v):
        zero = jnp.zeros_like(v)
        return jnp.concatenate(
            [jnp.where(left, v, zero), jnp.where(left, zero, v)], axis=0
        )

    def product(lhs, rhs):
        lh, ll = split(lhs)
        rh, rl = split(rhs)
        both = jnp.dot(
            jnp.concatenate([lh, ll], axis=1),
            jnp.concatenate(
                [
                    jnp.concatenate([rh, rl], axis=1),
                    jnp.concatenate([rh, jnp.zeros_like(rl)], axis=1),
                ],
                axis=0,
            ),
            preferred_element_type=F32,
        )
        return both[:, :BLOCK] + both[:, BLOCK:]

    exact = functools.partial(
        jnp.dot, precision=lax.Precision.HIGHEST, preferred_element_type=F32
    )

    def invert(matrices):
        eye = jnp.where(rem(lane64, HALF) == row64, 1.0, 0.0).astype(F32)
        first, gains = chebyshev()
        state = [(eye - first * a, first * eye) for a in matrices]
        for g in gains:
            following = []
            for left_over, inverse in state:
                both = product(
                    jnp.concatenate([left_over, inverse], axis=0), wide(left_over)
                )
                following.append(
                    (g * both[:HALF] - (g - 1.0) * eye, g * (inverse + both[HALF:]))
                )
            state = following
        results = []
        for a, (_, inverse) in zip(matrices, state):
            error = exact(a, wide(inverse))
            results.append(2.0 * inverse - exact(inverse, wide(error)))
        return results

    def conditioned():
        for m in range(1, 8):
            moment3(m).wait_recv()
        whole = mfull[...].reshape(2 * HALF, BLOCK)
        outs, ins = whole[:HALF], whole[HALF:]
        live = jnp.max(jnp.where(left, 0.0, ins))
        ins = jnp.where(left, ins, pltpu.roll(ins, HALF, 1))
        diagonal = rem(lane64, HALF) == row64
        left_row = left[0:1]

        def traces(v):
            on = jnp.sum(jnp.where(diagonal, v, 0.0), axis=0, keepdims=True)
            a = jnp.sum(jnp.where(left_row, on, 0.0), axis=1, keepdims=True)
            b = jnp.sum(jnp.where(left_row, 0.0, on), axis=1, keepdims=True)
            return jnp.where(left_row, a, b)

        trace_out, trace_in = traces(outs), traces(ins)
        added = jnp.where(diagonal, DAMPING / RANK, 0.0).astype(F32)
        inv_out, inv_in = invert([outs / trace_out + added, ins / trace_in + added])
        inv_out = inv_out * (live / trace_out)
        inv_in = inv_in * (live / trace_in)

        @pl.loop(0, 16)
        def _(j):
            a, tt = div(j, 8), rem(j, 8)

            @pl.when(jnp.logical_not(is_me(2 * t + a, tt)))
            def _():
                k = 2 * a + div(tt, 4)
                xx = rem(tt, 4)
                remote(
                    bsum, ball.at[k, xx], bs2.at[0], br2.at[k, xx], d, t
                ).wait_recv()

        sketches = jnp.concatenate(
            [ball[e].reshape(HALF, BLOCK) for e in range(4)], axis=1
        )
        wide_out = wide(inv_out)
        twice = jnp.concatenate([sketches, sketches], axis=0)
        solved = []
        for e in range(4):
            solved.append(
                fold(product(wide_out, twice[:, e * BLOCK : (e + 1) * BLOCK]))
            )
        return product(jnp.concatenate(solved, axis=0), wide(inv_in))

    def final(a, tt):
        return remote(
            msg.at[a], fin.at[d], fs.at[a, tt], fr.at[d], 2 * t + a, tt
        )

    def score(weights, scale):
        for r in (1, 2):
            for m in range(1, 8):
                share(r, m).wait_recv()
        queries = qall[...].reshape(16, HALF, BLOCK)
        rows = []
        for e in range(4):
            rows.append(
                jnp.sum(queries * weights[e * HALF : (e + 1) * HALF][None], axis=1)
            )
        rows = jnp.concatenate(rows, axis=0)
        ones = jnp.ones((16, BLOCK), F32)
        sums = lax.dot_general(
            ones, rows, (((1,), (1,)), ((), ())),
            precision=lax.Precision.HIGHEST, preferred_element_type=F32,
        )
        row = lax.broadcasted_iota(jnp.int32, (16, HALF), 0)
        column = lax.broadcasted_iota(jnp.int32, (16, HALF), 1)
        example = div(column, 16)
        kept = jnp.logical_and(
            rem(row, 8) < 2, example == 2 * div(row, 8) + rem(row, 8)
        )
        sums = jnp.where(kept, sums * scale, 0.0)
        at_row = lax.broadcasted_iota(jnp.int32, (HALF, BLOCK), 0)
        at_lane = lax.broadcasted_iota(jnp.int32, (HALF, BLOCK), 1)
        query = 2 * rem(at_row, 8) + rem(div(at_row, 8), 2)
        place = jnp.where(at_lane == rem(d, 8) * 16 + query, 1.0, 0.0).astype(F32)
        msg[...] = exact(sums, place).reshape(2, 8, BLOCK)

        @pl.loop(0, 16)
        def _(j):
            aa, tt = div(j, 8), rem(j, 8)
            me = is_me(2 * t + aa, tt)

            @pl.when(jnp.logical_not(me))
            def _():
                final(aa, tt).start()

            @pl.when(me)
            def _():
                fin[d] = msg[aa]

    project_some(1, 0, 4)
    begin2(0)
    project_some(1, 4, 8)
    begin3(0)
    project_some(2, 0, 4)
    train_finish()
    begin1(1)
    project_some(2, 4, 8)
    moments_over_dp()
    sketches_out()
    begin1(2)
    begin2(1)
    moments_back()
    begin3(1)
    weights = conditioned()
    begin2(2)
    share_sketch(1)
    begin3(2)
    share_sketch(2)
    drain(0)
    drain(1)
    drain(2)
    train_positions, query_positions = tin.shape[1], qin.shape[1]
    score(weights, 1.0 / (RANK * math.sqrt(train_positions * query_positions)))

    for m in range(1, 8):
        moment1(m).wait_send()
        moment3(m).wait_send()
        share(1, m).wait_send()
        share(2, m).wait_send()
    for m in range(1, 4):
        sketch1(m).wait_send()

    @pl.loop(1, 16)
    def _(j):
        moment2(j).wait_send()

    @pl.loop(0, 16)
    def _(j):
        @pl.when(jnp.logical_not(is_me(j, div(d, 2))))
        def _():
            sketch2(j).wait_send()

        aa, tt = div(j, 8), rem(j, 8)

        @pl.when(jnp.logical_not(is_me(2 * t + aa, tt)))
        def _():
            final(aa, tt).wait_send()

        @pl.when(jnp.logical_not(is_me(j, div(d, 2))))
        def _():
            remote(msg.at[0], fin.at[j], fs.at[0, 0], fr.at[j], d, t).wait_recv()

    low, high = fin[0], fin[8]
    for j in range(1, 8):
        low = low + fin[j]
        high = high + fin[j + 8]
    out_ref[:, :BLOCK] = low[:2]
    out_ref[:, BLOCK:] = high[:2]


def on_device(tin, tgr, tlen, qin, qgr, qlen, pin, pout):
    smem = pl.BlockSpec(memory_space=pltpu.SMEM)
    hbm = pl.BlockSpec(memory_space=pl.ANY)
    features, units = pin.shape[0], pout.shape[1]
    piece = (HALF, BLOCK)
    part = (16, BLOCK)
    dma = pltpu.SemaphoreType.DMA
    return pl.pallas_call(
        kernel,
        out_shape=jax.ShapeDtypeStruct((tin.shape[0], DP * qin.shape[0]), F32),
        in_specs=[smem, smem] + [hbm] * 6,
        out_specs=pl.BlockSpec(memory_space=pltpu.VMEM),
        scratch_shapes=[
            pltpu.VMEM((24, BLOCK, features), BF16),
            pltpu.VMEM((24, 2, BLOCK, units), BF16),
            pltpu.VMEM(pin.shape, BF16),
            pltpu.VMEM(pout.shape, BF16),
            pltpu.VMEM((2, features, BLOCK), BF16),
            pltpu.VMEM((2, units, BLOCK), BF16),
            pltpu.VMEM((3, 3, 8) + piece, F32),
            pltpu.VMEM((3, 3, 8) + piece, F32),
            pltpu.VMEM((3, 3, 2) + piece, F32),
            pltpu.VMEM((3, 3) + piece, F32),
            pltpu.VMEM((8,) + part, F32),
            pltpu.VMEM((8,) + part, F32),
            pltpu.VMEM(part, F32),
            pltpu.VMEM((16,) + part, F32),
            pltpu.VMEM((8,) + part, F32),
            pltpu.VMEM((4,) + part, F32),
            pltpu.VMEM((4,) + part, F32),
            pltpu.VMEM(part, F32),
            pltpu.VMEM((4, 4) + part, F32),
            pltpu.VMEM((2, 8) + piece, F32),
            pltpu.VMEM((2, 8, BLOCK), F32),
            pltpu.VMEM((16, 8, BLOCK), F32),
            dma((2, 24)), dma((2,)),
            dma((3, 3, 8)), dma((3, 3, 8)),
            dma((3, 3, 2)), dma((3, 3, 2)),
            dma((3, 3)), dma((3, 3)),
            dma((8,)), dma((8,)), dma((16,)), dma((16,)), dma((8,)), dma((8,)),
            dma((4,)), dma((4,)), dma((16,)), dma((4, 4)),
            dma((2, 8)), dma((2, 8)), dma((2, 8)), dma((16,)),
        ],
        compiler_params=pltpu.CompilerParams(
            collective_id=0, has_side_effects=True, vmem_limit_bytes=48 * 1024 * 1024
        ),
    )(tlen, qlen, tin, tgr, qin, qgr, pin, pout)


def solution(mesh):
    placed = (
        P("dp", None, "tensor"),
        P("dp", None, None, "tensor"),
        P("dp"),
        P("dp", None, "tensor"),
        P("dp", None, None, "tensor"),
        P("dp"),
        P("tensor", None),
        P(None, "tensor", None),
    )
    return jax.shard_map(
        on_device, mesh=mesh, in_specs=placed, out_specs=P("dp", None), check_vma=False
    )
```

```python
import contextlib
import functools
import math

import jax
import jax.numpy as jnp
from jax import lax
from jax.experimental import pallas as pl
from jax.experimental.pallas import tpu as pltpu
from jax.sharding import PartitionSpec as P

MESH = pl.DeviceIdType.MESH
SCOPES = False


def scope(name):
    return jax.named_scope(name) if SCOPES else contextlib.nullcontext()


F32 = jnp.float32
BF16 = jnp.bfloat16
DAMPING = 0.1
RANK = 64
BLOCK = 128
HALF = 64
DP = 16
DOUBLINGS = 7
GENS = ((1, 3, 4), (3, 4, 1), (4, 1, 3))


def chebyshev():
    low = DAMPING / RANK
    high = 1.0 + low
    angle = math.acosh((high + low) / (high - low))
    gains = []
    n = 1
    for _ in range(DOUBLINGS):
        gains.append(2.0 * math.cosh(n * angle) ** 2 / math.cosh(2 * n * angle))
        n *= 2
    return 2.0 / (high + low), gains


def rem(a, b):
    return lax.rem(a, jnp.int32(b))


def div(a, b):
    return lax.div(a, jnp.int32(b))


def split(v):
    high = v.astype(BF16)
    return high, (v - high.astype(F32)).astype(BF16)


def kernel(
    tlen_hbm, qlen_hbm, tin, tgr, qin, qgr, pin, pout, out_ref,
    tlen, qlen, xin, xgr, wip, wop, acc, got, got2, got3, part, msum, bsum, qall, msg, fin,
    wsem, isem, gsem, send, recv1, recv2, recv3, msend, mrecv, bsend, brecv, qsend, qrecv, fsend, frecv,
):
    d = lax.axis_index("dp").astype(jnp.int32)
    t = lax.axis_index("tensor").astype(jnp.int32)
    z, x = div(t, 4), rem(t, 4)
    column = div(d, 2)
    on_diagonal = column == t

    def flip(m):
        m = jnp.int32(m)
        mx, mz = rem(m, 4), div(m, 4)
        low = rem(x + mx, 2)
        high = rem(div(x, 2) + div(mx, 2), 2)
        return rem(z + mz, 2) * 4 + high * 2 + low

    def remote(src, dst, ssem, rsem, dd, tt):
        return pltpu.make_async_remote_copy(
            src_ref=src, dst_ref=dst, send_sem=ssem, recv_sem=rsem,
            device_id=(dd, tt), device_id_type=MESH,
        )

    def wait(ref, sem):
        pltpu.make_async_copy(ref, ref, sem).wait()

    def is_me(dd, tt):
        return jnp.logical_and(dd == d, tt == t)

    def unless(condition):
        return pl.when(jnp.logical_not(condition))

    def load(pair, query):
        sem = rem(pair, 4)
        m = 7 - 2 * sem
        for h in range(2):
            item = flip(m - h)
            if query:
                q = item * 2 + (div(pair, 4) - 1)
                a, b = qin.at[q], qgr.at[q]
            else:
                rows = pl.ds(pl.multiple_of(rem(item, 4) * BLOCK, BLOCK), BLOCK)
                e = div(item, 4)
                a, b = tin.at[e, rows, :], tgr.at[e, :, rows, :]
            to = pl.ds(h * BLOCK, BLOCK)
            pltpu.make_async_copy(a, xin.at[pair, to], isem.at[sem]).start()
            pltpu.make_async_copy(b, xgr.at[pair, :, to], gsem.at[sem]).start()

    with scope("start_loads"):
        pltpu.make_async_copy(pin, wip.at[0, :RANK], wsem.at[0]).start()
        pltpu.make_async_copy(pin, wip.at[1, RANK:], wsem.at[0]).start()
        pltpu.make_async_copy(pout.at[0], wop.at[0, :RANK], wsem.at[1]).start()
        pltpu.make_async_copy(pout.at[1], wop.at[1, RANK:], wsem.at[1]).start()

        @pl.loop(0, 4)
        def _(pair):
            load(pair, False)

        lengths = (
            pltpu.make_async_copy(tlen_hbm, tlen, wsem.at[2]),
            pltpu.make_async_copy(qlen_hbm, qlen, wsem.at[3]),
        )
        for c in lengths:
            c.start()

    barrier = pltpu.get_barrier_semaphore()

    def greet(dd, tt):
        pl.semaphore_signal(barrier, inc=1, device_id=(dd, tt), device_id_type=MESH)

    with scope("greet"):

        @pl.loop(1, 8)
        def _(m):
            greet(d, flip(m))

        @pl.loop(1, 16)
        def _(j):
            greet(rem(d + j, DP), t)

        @pl.loop(0, 16)
        def _(j):
            dd, tt = t * 2 + div(j, 8), rem(j, 8)

            @unless(is_me(dd, tt))
            def _():
                greet(dd, tt)

            @unless(is_me(j, column))
            def _():
                greet(j, column)

    with scope("weights"):
        wip[0, RANK:] = jnp.zeros(pin.shape, BF16)
        wip[1, :RANK] = jnp.zeros(pin.shape, BF16)
        wop[0, RANK:] = jnp.zeros(pout.shape[1:], BF16)
        wop[1, :RANK] = jnp.zeros(pout.shape[1:], BF16)
        wait(wip.at[0], wsem.at[0])
        wait(wop.at[0], wsem.at[1])
        for c in lengths:
            c.wait()

    with scope("barrier_wait"):

        @pl.when(on_diagonal)
        def _():
            pl.semaphore_wait(barrier, 52)

        @unless(on_diagonal)
        def _():
            pl.semaphore_wait(barrier, 54)

    def rows_of(p):
        return slice(HALF * p, HALF * (p + 1))

    def piece(r, p, m):
        return acc.at[r * 8 + m, rows_of(p)]

    def first(r, p, m, s):
        return remote(
            piece(r, p, m), got.at[r * 8 + s, rows_of(p)],
            send, recv1.at[r, p], d, flip(GENS[p][0]),
        )

    def times(rows, turned):
        return lax.dot_general(
            rows, turned, (((1,), (1,)), ((), ())), preferred_element_type=F32
        )

    def project(pair):
        r, sem = div(pair, 4), rem(pair, 4)
        m = 7 - 2 * sem
        wait(xin.at[pair], isem.at[sem])
        wait(xgr.at[pair], gsem.at[sem])

        @pl.when(pair < 8)
        def _():
            load(pair + 4, True)

        rows = xin[pair]
        low = jnp.concatenate([rows[:HALF], rows[BLOCK : BLOCK + HALF]], axis=0)
        high = jnp.concatenate([rows[HALF:BLOCK], rows[BLOCK + HALF :]], axis=0)
        ins = times(low, wip[0]) + times(high, wip[1])
        outs = times(xgr[pair, 0], wop[0]) + times(xgr[pair, 1], wop[1])
        for h in range(2):
            slot = r * 8 + m - h
            acc[slot, :HALF] = ins[h * HALF : (h + 1) * HALF]
            acc[slot, HALF:] = outs[h * BLOCK : (h + 1) * BLOCK]

        @pl.when(r == 0)
        def _():
            for h in range(2):
                item = m - h
                low = rem(item, 4)
                sent = (jnp.logical_or(low == 1, low == 2), low >= 2, item >= 4)
                after = (
                    item + 1 - 2 * rem(item, 2),
                    item - low + 3 - low,
                    item - 4,
                )
                for p in range(3):

                    @pl.when(sent[p])
                    def _(p=p):
                        first(0, p, item, after[p]).start()

    def project_pairs(low, high):
        pl.loop(low, high)(project)

    def halve1(r):
        for k in range(4):
            for p, (g1, g2, g3) in enumerate(GENS):
                s = (g2, g2 ^ g3, g3, 0)[k]
                first(r, p, s ^ g1, s).start()

    def add(r, p, s, ref):
        rows = rows_of(p)
        acc[r * 8 + s, rows] = acc[r * 8 + s, rows] + ref[...]

    def halve2(r):
        for p, (_, g2, g3) in enumerate(GENS):
            wait(qall.at[pl.ds(0, 4)], recv1.at[r, p])
            for k, s in enumerate((g2, g2 ^ g3)):
                add(r, p, s, got.at[r * 8 + s, rows_of(p)])
                remote(
                    piece(r, p, s), got2.at[r, p, k],
                    send, recv2.at[r, p], d, flip(g2),
                ).start()
        for p, (_, _, g3) in enumerate(GENS):
            for s in (g3, 0):
                add(r, p, s, got.at[r * 8 + s, rows_of(p)])

    def halve3(r):
        for p, (_, _, g3) in enumerate(GENS):
            wait(qall.at[pl.ds(0, 2)], recv2.at[r, p])
            add(r, p, g3, got2.at[r, p, 1])
            remote(
                piece(r, p, g3), got3.at[r, p], send, recv3.at[r, p], d, flip(g3)
            ).start()
        for p in range(3):
            add(r, p, 0, got2.at[r, p, 0])

    def halved(r):
        for p in range(3):
            wait(qall.at[0], recv3.at[r, p])
        return acc[r * 8] + jnp.concatenate([got3[r, p] for p in range(3)], axis=0)

    row64 = lax.broadcasted_iota(jnp.int32, (HALF, BLOCK), 0)
    lane64 = lax.broadcasted_iota(jnp.int32, (HALF, BLOCK), 1)
    left = lane64 < HALF

    def finished(total, length):
        position = jnp.where(left, row64, row64 + HALF)
        inputs = jnp.where(position < length, total[:HALF], 0.0)
        turned = pltpu.roll(inputs, HALF, 1)
        twice = jnp.concatenate(
            [jnp.where(left, inputs, turned), jnp.where(left, turned, inputs)], axis=0
        ).astype(BF16)
        outputs = jnp.concatenate(
            [
                jnp.where(row64 < length, total[HALF:BLOCK], 0.0),
                jnp.where(row64 + HALF < length, total[BLOCK:], 0.0),
            ],
            axis=0,
        )
        return twice, outputs.astype(BF16), outputs.T.astype(BF16)

    def fold(full):
        return jnp.where(left, full[:HALF], full[HALF:])

    def query_sketch(total, r):
        length = qlen[t * 2 + (r - 1)]
        twice, _, turned = finished(total, length)
        return fold(jnp.dot(turned, twice, preferred_element_type=F32))

    def share(r, m):
        mine = qall.at[(r - 1) * 8 + t]
        return remote(mine, mine, qsend, qrecv.at[r - 1], d, flip(m))

    def share_sketch(r):
        with scope("halved"):
            total = halved(r)
        qall[(r - 1) * 8 + t] = query_sketch(total, r)
        for m in range(1, 8):
            share(r, m).start()

    def moment1(m):
        return remote(part.at[flip(m)], part.at[8 + m], msend, mrecv.at[0], d, flip(m))

    def moment2(j):
        return remote(msum, part.at[16 + d], msend, mrecv.at[1], rem(d + j, DP), t)

    def moment3(m):
        return remote(
            part.at[32 + t], part.at[32 + t], msend, mrecv.at[2], d, flip(m)
        )

    def sketch1(m):
        return remote(
            part.at[40 + rem(flip(m), 4)], part.at[44 + m], bsend, brecv.at[0], d, flip(m)
        )

    my_quarter = 48 + 4 * (2 * rem(d, 2) + z) + x

    def sketch2(j):
        return remote(bsum, part.at[my_quarter], bsend, brecv.at[1], j, column)

    def train_finish():
        with scope("halved"):
            total = halved(0)
        length = tlen[z] - x * BLOCK
        twice, outputs, turned = finished(total, length)
        products = jnp.dot(
            turned, jnp.concatenate([outputs, twice], axis=1), preferred_element_type=F32
        )
        ins = lax.dot_general(
            twice, twice, (((0,), (0,)), ((), ())), preferred_element_type=F32
        )
        live = jnp.minimum(jnp.maximum(length, 0), BLOCK).astype(F32)
        part[0:4] = fold(products[:, :BLOCK]).reshape(4, 16, BLOCK)
        part[4:8] = jnp.where(left, ins[:HALF], live).reshape(4, 16, BLOCK)
        for m in range(7, 0, -1):
            moment1(m).start()
        part[40:44] = fold(products[:, BLOCK:]).reshape(4, 16, BLOCK)
        for m in range(1, 4):
            sketch1(m).start()

    def moments_over_dp():
        wait(part.at[pl.ds(9, 7)], mrecv.at[0])
        total = part[t]
        for m in range(1, 8):
            total = total + part[8 + m]
        msum[...] = total
        part[16 + d] = total

        @pl.loop(1, 16)
        def _(j):
            moment2(j).start()

    def sketches_out():
        wait(part.at[pl.ds(45, 3)], brecv.at[0])
        total = part[40 + x]
        for m in range(1, 4):
            total = total + part[44 + m]
        bsum[...] = total

        @pl.loop(0, 16)
        def _(j):
            me = is_me(j, column)

            @unless(me)
            def _():
                sketch2(j).start()

            @pl.when(me)
            def _():
                part[my_quarter] = total

    def moments_back():
        wait(part.at[pl.ds(16, 15)], mrecv.at[1])
        total = part[16]
        for j in range(1, 16):
            total = total + part[16 + j]
        part[32 + t] = total
        for m in range(7, 0, -1):
            moment3(m).start()

    def wide(v):
        zero = jnp.zeros_like(v)
        return jnp.concatenate(
            [jnp.where(left, v, zero), jnp.where(left, zero, v)], axis=0
        )

    def product(lhs, rhs):
        lh, ll = split(lhs)
        rh, rl = split(rhs)
        both = jnp.dot(
            jnp.concatenate([lh, ll], axis=1),
            jnp.concatenate(
                [
                    jnp.concatenate([rh, rl], axis=1),
                    jnp.concatenate([rh, jnp.zeros_like(rl)], axis=1),
                ],
                axis=0,
            ),
            preferred_element_type=F32,
        )
        return both[:, : rhs.shape[1]] + both[:, rhs.shape[1] :]

    exact = functools.partial(
        jnp.dot, precision=lax.Precision.HIGHEST, preferred_element_type=F32
    )

    def invert(matrices):
        eye = jnp.where(rem(lane64, HALF) == row64, 1.0, 0.0).astype(F32)
        first, gains = chebyshev()
        state = [(eye - first * a, first * eye) for a in matrices]
        for g in gains:
            following = []
            for left_over, inverse in state:
                both = product(
                    jnp.concatenate([left_over, inverse], axis=0), wide(left_over)
                )
                following.append(
                    (g * both[:HALF] - (g - 1.0) * eye, g * (inverse + both[HALF:]))
                )
            state = following
        results = []
        for a, (_, inverse) in zip(matrices, state):
            error = exact(a, wide(inverse))
            results.append(2.0 * inverse - exact(inverse, wide(error)))
        return results

    def inverses():
        with scope("wait_moment3"):
            wait(part.at[pl.ds(32, 7)], mrecv.at[2])
        whole = part[32:40].reshape(2 * HALF, BLOCK)
        outs, ins = whole[:HALF], whole[HALF:]
        live = jnp.max(jnp.where(left, 0.0, ins))
        ins = jnp.where(left, ins, pltpu.roll(ins, HALF, 1))
        diagonal = rem(lane64, HALF) == row64
        left_row = left[0:1]

        def traces(v):
            on = jnp.sum(jnp.where(diagonal, v, 0.0), axis=0, keepdims=True)
            a = jnp.sum(jnp.where(left_row, on, 0.0), axis=1, keepdims=True)
            b = jnp.sum(jnp.where(left_row, 0.0, on), axis=1, keepdims=True)
            return jnp.where(left_row, a, b)

        trace_out, trace_in = traces(outs), traces(ins)
        added = jnp.where(diagonal, DAMPING / RANK, 0.0).astype(F32)
        inv_out, inv_in = invert([outs / trace_out + added, ins / trace_in + added])
        return inv_out * (live / trace_out), inv_in * (live / trace_in)

    def diagonal_or_not(f):
        pl.when(on_diagonal)(functools.partial(f, 15))
        unless(on_diagonal)(functools.partial(f, 16))

    def solve(inv_out, inv_in):
        with scope("wait_sketches"):
            diagonal_or_not(lambda n: wait(part.at[pl.ds(48, n)], brecv.at[1]))
        wide_out = wide(inv_out)
        solved = []
        for e in range(4):
            sketch = part[48 + 4 * e : 52 + 4 * e].reshape(HALF, BLOCK)
            solved.append(
                fold(product(wide_out, jnp.concatenate([sketch, sketch], axis=0)))
            )
        return product(jnp.concatenate(solved, axis=0), wide(inv_in))

    def final(a, tt):
        return remote(msg.at[a], fin.at[d], fsend, frecv, 2 * t + a, tt)

    def score(weights, scale):
        with scope("wait_share"):
            for r in range(2):
                wait(qall.at[pl.ds(r * 8, 7)], qrecv.at[r])
        queries = qall[...]
        rows = []
        for e in range(4):
            rows.append(
                jnp.sum(queries * weights[e * HALF : (e + 1) * HALF][None], axis=1)
            )
        rows = jnp.concatenate(rows, axis=0)
        ones = jnp.ones((16, BLOCK), F32)
        sums = lax.dot_general(
            ones, rows, (((1,), (1,)), ((), ())),
            precision=lax.Precision.HIGHEST, preferred_element_type=F32,
        )
        row = lax.broadcasted_iota(jnp.int32, (16, HALF), 0)
        lane = lax.broadcasted_iota(jnp.int32, (16, HALF), 1)
        example = div(lane, 16)
        kept = jnp.logical_and(
            rem(row, 8) < 2, example == 2 * div(row, 8) + rem(row, 8)
        )
        sums = jnp.where(kept, sums * scale, 0.0)
        at_row = lax.broadcasted_iota(jnp.int32, (HALF, BLOCK), 0)
        at_lane = lax.broadcasted_iota(jnp.int32, (HALF, BLOCK), 1)
        query = 2 * rem(at_row, 8) + rem(div(at_row, 8), 2)
        place = jnp.where(at_lane == rem(d, 8) * 16 + query, 1.0, 0.0).astype(F32)
        msg[...] = exact(sums, place).reshape(2, 8, BLOCK)

        @pl.loop(0, 16)
        def _(j):
            a, tt = div(j, 8), rem(j, 8)
            me = is_me(2 * t + a, tt)

            @unless(me)
            def _():
                final(a, tt).start()

            @pl.when(me)
            def _():
                fin[d] = msg[a]

    def do(name, f, *args):
        with scope(name):
            return f(*args)

    do("project_0", project_pairs, 0, 4)
    do("project_1", project_pairs, 4, 8)
    do("halve2_0", halve2, 0)
    do("halve1_1", halve1, 1)
    do("project_2a", project_pairs, 8, 11)
    do("halve3_0", halve3, 0)
    do("project_2b", project_pairs, 11, 12)
    do("train_finish", train_finish)
    do("halve2_1", halve2, 1)
    do("halve1_2", halve1, 2)
    do("moments_over_dp", moments_over_dp)
    do("halve3_1", halve3, 1)
    do("halve2_2", halve2, 2)
    do("sketches_out", sketches_out)
    do("share_1", share_sketch, 1)
    do("moments_back", moments_back)
    do("halve3_2", halve3, 2)
    do("share_2", share_sketch, 2)
    inv_out, inv_in = do("inverses", inverses)
    weights = do("solve", solve, inv_out, inv_in)
    train_positions, query_positions = tin.shape[1], qin.shape[1]
    scale = 1.0 / (RANK * math.sqrt(train_positions * query_positions))
    do("score", score, weights, scale)

    with scope("drain"):
        wait(acc.at[pl.ds(0, 21)], send)
        wait(part.at[pl.ds(0, 29)], msend)
        diagonal_or_not(lambda n: wait(part.at[pl.ds(0, n + 3)], bsend))
        wait(qall.at[pl.ds(0, 14)], qsend)
    with scope("final_wait"):
        diagonal_or_not(lambda n: wait(fin.at[pl.ds(0, n)], frecv))
    with scope("final_drain"):
        diagonal_or_not(lambda n: wait(fin.at[pl.ds(0, n)], fsend))
    low, high = fin[0], fin[8]
    for j in range(1, 8):
        low = low + fin[j]
        high = high + fin[j + 8]
    out_ref[:, :BLOCK] = low[:2]
    out_ref[:, BLOCK:] = high[:2]


def on_device(tin, tgr, tlen, qin, qgr, qlen, pin, pout):
    hbm = pl.BlockSpec(memory_space=pltpu.HBM)
    features, units = pin.shape[0], pout.shape[1]
    dma = pltpu.SemaphoreType.DMA
    return pl.pallas_call(
        kernel,
        out_shape=jax.ShapeDtypeStruct((tin.shape[0], DP * qin.shape[0]), F32),
        in_specs=[hbm] * 8,
        out_specs=pl.BlockSpec(memory_space=pltpu.VMEM),
        scratch_shapes=[
            pltpu.SMEM(tlen.shape, jnp.int32),
            pltpu.SMEM(qlen.shape, jnp.int32),
            pltpu.VMEM((12, 2 * BLOCK, features), BF16),
            pltpu.VMEM((12, 2, 2 * BLOCK, units), BF16),
            pltpu.VMEM((2, BLOCK, features), BF16),
            pltpu.VMEM((2, BLOCK, units), BF16),
            pltpu.VMEM((24, HALF + BLOCK, BLOCK), F32),
            pltpu.VMEM((24, HALF + BLOCK, BLOCK), F32),
            pltpu.VMEM((3, 3, 2, HALF, BLOCK), F32),
            pltpu.VMEM((3, 3, HALF, BLOCK), F32),
            pltpu.VMEM((64, 16, BLOCK), F32),
            pltpu.VMEM((16, BLOCK), F32),
            pltpu.VMEM((16, BLOCK), F32),
            pltpu.VMEM((16, HALF, BLOCK), F32),
            pltpu.VMEM((2, 8, BLOCK), F32),
            pltpu.VMEM((16, 8, BLOCK), F32),
            dma((4,)), dma((4,)), dma((4,)),
            dma, dma((3, 3)), dma((3, 3)), dma((3, 3)), dma, dma((3,)), dma, dma((2,)), dma, dma((2,)), dma, dma,
        ],
        compiler_params=pltpu.CompilerParams(
            collective_id=0, has_side_effects=True, vmem_limit_bytes=56 * 1024 * 1024
        ),
    )(tlen, qlen, tin, tgr, qin, qgr, pin.T, pout.transpose(0, 2, 1))


def solution(mesh):
    placed = (
        P("dp", None, "tensor"),
        P("dp", None, None, "tensor"),
        P("dp"),
        P("dp", None, "tensor"),
        P("dp", None, None, "tensor"),
        P("dp"),
        P("tensor", None),
        P(None, "tensor", None),
    )
    return jax.shard_map(
        on_device, mesh=mesh, in_specs=placed, out_specs=P("dp", None), check_vma=False
    )
```

```python
import contextlib
import functools
import math

import jax
import jax.numpy as jnp
from jax import lax
from jax.experimental import pallas as pl
from jax.experimental.pallas import tpu as pltpu
from jax.sharding import PartitionSpec as P

MESH = pl.DeviceIdType.MESH
SCOPES = False


def scope(name):
    return jax.named_scope(name) if SCOPES else contextlib.nullcontext()


F32 = jnp.float32
BF16 = jnp.bfloat16
DAMPING = 0.1
RANK = 64
BLOCK = 128
HALF = 64
DP = 16
DOUBLINGS = 7
GENS = ((1, 3, 4), (3, 4, 1), (4, 1, 3))


def chebyshev():
    low = DAMPING / RANK
    high = 1.0 + low
    return 2.0 / (high + low), (high + low) / (high - low)


def rem(a, b):
    return lax.rem(a, jnp.int32(b))


def div(a, b):
    return lax.div(a, jnp.int32(b))


def split(v):
    high = v.astype(BF16)
    return high, (v - high.astype(F32)).astype(BF16)


def kernel(
    tlen_hbm, qlen_hbm, tin, tgr, qin, qgr, pin, pout, out_ref,
    tlen, qlen, xin, xgr, wip, wop, acc, got, got2, got3, part, msum, bsum, qall, msg, fin,
    wsem, isem, gsem, send, recv1, recv2, recv3, msend, mrecv, bsend, brecv, qsend, qrecv, fsend, frecv,
):
    d = lax.axis_index("dp").astype(jnp.int32)
    t = lax.axis_index("tensor").astype(jnp.int32)
    z, x = div(t, 4), rem(t, 4)
    column = div(d, 4)
    on_diagonal = column == x

    def flip(m):
        m = jnp.int32(m)
        mx, mz = rem(m, 4), div(m, 4)
        low = rem(x + mx, 2)
        high = rem(div(x, 2) + div(mx, 2), 2)
        return rem(z + mz, 2) * 4 + high * 2 + low

    def remote(src, dst, ssem, rsem, dd, tt):
        return pltpu.make_async_remote_copy(
            src_ref=src, dst_ref=dst, send_sem=ssem, recv_sem=rsem,
            device_id=(dd, tt), device_id_type=MESH,
        )

    def wait(ref, sem):
        pltpu.make_async_copy(ref, ref, sem).wait()

    def is_me(dd, tt):
        return jnp.logical_and(dd == d, tt == t)

    def unless(condition):
        return pl.when(jnp.logical_not(condition))

    def load(pair, query):
        sem = rem(pair, 4)
        m = 7 - 2 * sem
        for h in range(2):
            item = flip(m - h)
            if query:
                q = item * 2 + (div(pair, 4) - 1)
                a, b = qin.at[q], qgr.at[q]
            else:
                rows = pl.ds(pl.multiple_of(rem(item, 4) * BLOCK, BLOCK), BLOCK)
                e = div(item, 4)
                a, b = tin.at[e, rows, :], tgr.at[e, :, rows, :]
            to = pl.ds(h * BLOCK, BLOCK)
            pltpu.make_async_copy(a, xin.at[pair, to], isem.at[sem]).start()
            to = pl.ds((pair * 2 + h) * BLOCK, BLOCK)
            pltpu.make_async_copy(b, xgr.at[:, to], gsem.at[sem]).start()

    with scope("start_loads"):
        pltpu.make_async_copy(pin, wip.at[0, :RANK], wsem.at[0]).start()
        pltpu.make_async_copy(pin, wip.at[1, RANK:], wsem.at[0]).start()
        pltpu.make_async_copy(pout.at[0], wop.at[0, :RANK], wsem.at[1]).start()
        pltpu.make_async_copy(pout.at[1], wop.at[1, RANK:], wsem.at[1]).start()

        @pl.loop(0, 4)
        def _(pair):
            load(pair, False)

        lengths = (
            pltpu.make_async_copy(tlen_hbm, tlen, wsem.at[2]),
            pltpu.make_async_copy(qlen_hbm, qlen, wsem.at[3]),
        )
        for c in lengths:
            c.start()

    barrier = pltpu.get_barrier_semaphore()

    def greet(dd, tt):
        pl.semaphore_signal(barrier, inc=1, device_id=(dd, tt), device_id_type=MESH)

    with scope("greet"):

        @pl.loop(1, 8)
        def _(m):
            greet(d, flip(m))

        @pl.loop(1, 16)
        def _(j):
            greet(rem(d + j, DP), t)

        @pl.loop(0, 32)
        def _(j):
            dd, tt = div(j, 2), rem(j, 2) * 4 + column

            @unless(is_me(dd, tt))
            def _():
                greet(dd, tt)

    with scope("weights"):
        wip[0, RANK:] = jnp.zeros(pin.shape, BF16)
        wip[1, :RANK] = jnp.zeros(pin.shape, BF16)
        wop[0, RANK:] = jnp.zeros(pout.shape[1:], BF16)
        wop[1, :RANK] = jnp.zeros(pout.shape[1:], BF16)
        wait(wip.at[0], wsem.at[0])
        wait(wop.at[0], wsem.at[1])
        for c in lengths:
            c.wait()

    def rows_of(p):
        return slice(HALF * p, HALF * (p + 1))

    def piece(r, p, m):
        return acc.at[r * 8 + m, rows_of(p)]

    def first(r, p, m, s):
        return remote(
            piece(r, p, m), got.at[r * 8 + s, rows_of(p)],
            send, recv1.at[r, p], d, flip(GENS[p][0]),
        )

    def times(rows, turned):
        return lax.dot_general(
            rows, turned, (((1,), (1,)), ((), ())), preferred_element_type=F32
        )

    def project(four):
        pairs = (2 * four, 2 * four + 1)
        for pair in pairs:
            sem = rem(pair, 4)
            wait(xin.at[pair], isem.at[sem])
            wait(xgr.at[:, pl.ds(pair * 2 * BLOCK, 2 * BLOCK)], gsem.at[sem])

        @pl.when(four < 4)
        def _():
            for pair in pairs:
                load(pair + 4, True)

        def rows(start):
            return jnp.concatenate(
                [
                    xin[pair, h * BLOCK + start : h * BLOCK + start + HALF]
                    for pair in pairs
                    for h in range(2)
                ],
                axis=0,
            )

        ins = times(rows(0), wip[0]) + times(rows(HALF), wip[1])
        units = pl.ds(four * 4 * BLOCK, 4 * BLOCK)
        outs = times(xgr[0, units], wop[0]) + times(xgr[1, units], wop[1])
        for i in range(4):
            slot = div(four, 2) * 8 + 7 - 4 * rem(four, 2) - i
            acc[slot, :HALF] = ins[i * HALF : (i + 1) * HALF]
            acc[slot, HALF:] = outs[i * BLOCK : (i + 1) * BLOCK]

    def send_items(*which):
        for p, m in which:
            first(0, p, m, m ^ GENS[p][0]).start()

    def everyone_is_here():
        pl.when(on_diagonal)(lambda: pl.semaphore_wait(barrier, 53))
        unless(on_diagonal)(lambda: pl.semaphore_wait(barrier, 54))

    def halve1(r):
        for k in range(4):
            for p, (g1, g2, g3) in enumerate(GENS):
                s = (g2, g2 ^ g3, g3, 0)[k]
                first(r, p, s ^ g1, s).start()

    def add(r, p, s, ref):
        rows = rows_of(p)
        acc[r * 8 + s, rows] = acc[r * 8 + s, rows] + ref[...]

    def halve2(r):
        for p, (_, g2, g3) in enumerate(GENS):
            wait(qall.at[pl.ds(0, 4)], recv1.at[r, p])
            for k, s in enumerate((g2, g2 ^ g3)):
                add(r, p, s, got.at[r * 8 + s, rows_of(p)])
                remote(
                    piece(r, p, s), got2.at[r, p, k],
                    send, recv2.at[r % 2, p], d, flip(g2),
                ).start()
        for p, (_, _, g3) in enumerate(GENS):
            for s in (g3, 0):
                add(r, p, s, got.at[r * 8 + s, rows_of(p)])

    def halve3(r):
        for p, (_, _, g3) in enumerate(GENS):
            wait(qall.at[pl.ds(0, 2)], recv2.at[r % 2, p])
            add(r, p, g3, got2.at[r, p, 1])
            remote(
                piece(r, p, g3), got3.at[r, p], send, recv3.at[r % 2, p], d, flip(g3)
            ).start()
        for p in range(3):
            add(r, p, 0, got2.at[r, p, 0])

    def halved(r):
        for p in range(3):
            wait(qall.at[0], recv3.at[r % 2, p])
        return acc[r * 8] + jnp.concatenate([got3[r, p] for p in range(3)], axis=0)

    row64 = lax.broadcasted_iota(jnp.int32, (HALF, BLOCK), 0)
    lane64 = lax.broadcasted_iota(jnp.int32, (HALF, BLOCK), 1)
    left = lane64 < HALF

    def finished(total, length):
        position = jnp.where(left, row64, row64 + HALF)
        inputs = jnp.where(position < length, total[:HALF], 0.0)
        turned = pltpu.roll(inputs, HALF, 1)
        twice = jnp.concatenate(
            [jnp.where(left, inputs, turned), jnp.where(left, turned, inputs)], axis=0
        ).astype(BF16)
        outputs = jnp.concatenate(
            [
                jnp.where(row64 < length, total[HALF:BLOCK], 0.0),
                jnp.where(row64 + HALF < length, total[BLOCK:], 0.0),
            ],
            axis=0,
        )
        return twice, outputs.astype(BF16), outputs.T.astype(BF16)

    def fold(full):
        return jnp.where(left, full[:HALF], full[HALF:])

    def query_sketch(total, r):
        length = qlen[t * 2 + (r - 1)]
        twice, _, turned = finished(total, length)
        return fold(jnp.dot(turned, twice, preferred_element_type=F32))

    def share(r, m):
        mine = qall.at[(r - 1) * 4 + x]
        return remote(mine, mine, qsend, qrecv.at[r - 1], d, flip(m))

    def share_sketch(r):
        with scope("halved"):
            total = halved(r)
        qall[(r - 1) * 4 + x] = query_sketch(total, r)
        for m in (2, 1, 3):
            share(r, m).start()

    def moment1(m):
        return remote(part.at[flip(m)], part.at[8 + m], msend, mrecv.at[0], d, flip(m))

    def moment2(j):
        return remote(msum, part.at[16 + d], msend, mrecv.at[1], rem(d + j, DP), t)

    def moment3(m):
        return remote(
            part.at[32 + t], part.at[32 + t], msend, mrecv.at[2], d, flip(m)
        )

    def sketch1(m):
        return remote(
            part.at[40 + rem(flip(m), 4)], part.at[44 + m], bsend, brecv.at[0], d, flip(m)
        )

    def sketch2(j):
        return remote(bsum, part.at[48 + d], bsend, brecv.at[1], rem(d + j, DP), t)

    def sketch3(m):
        return remote(
            part.at[pl.ds(48 + 4 * rem(flip(m), 4), 4)], part.at[pl.ds(64 + 4 * t, 4)],
            bsend, brecv.at[2], d, flip(m),
        )

    def train_finish():
        with scope("halved"):
            total = halved(0)
        length = tlen[z] - x * BLOCK
        twice, outputs, turned = finished(total, length)
        products = jnp.dot(
            turned, jnp.concatenate([outputs, twice], axis=1), preferred_element_type=F32
        )
        ins = lax.dot_general(
            twice, twice, (((0,), (0,)), ((), ())), preferred_element_type=F32
        )
        live = jnp.minimum(jnp.maximum(length, 0), BLOCK).astype(F32)
        part[0:4] = fold(products[:, :BLOCK]).reshape(4, 16, BLOCK)
        part[4:8] = jnp.where(left, ins[:HALF], live).reshape(4, 16, BLOCK)
        for m in range(7, 0, -1):
            moment1(m).start()
        part[40:44] = fold(products[:, BLOCK:]).reshape(4, 16, BLOCK)
        for m in range(1, 4):
            sketch1(m).start()

    def moments_over_dp():
        wait(part.at[pl.ds(9, 7)], mrecv.at[0])
        total = part[t]
        for m in range(1, 8):
            total = total + part[8 + m]
        msum[...] = total
        part[16 + d] = total

        @pl.loop(1, 16)
        def _(j):
            moment2(j).start()

    def sketches_out():
        wait(part.at[pl.ds(45, 3)], brecv.at[0])
        total = part[40 + x]
        for m in range(1, 4):
            total = total + part[44 + m]
        bsum[...] = total
        part[48 + d] = total

        @pl.loop(1, 16)
        def _(j):
            sketch2(j).start()

    def sketches_across():
        wait(part.at[pl.ds(48, 15)], brecv.at[1])
        part[pl.ds(64 + 4 * t, 4)] = part[pl.ds(48 + 4 * x, 4)]
        for m in range(7, 0, -1):
            sketch3(m).start()

    def moments_back():
        wait(part.at[pl.ds(16, 15)], mrecv.at[1])
        total = part[16]
        for j in range(1, 16):
            total = total + part[16 + j]
        part[32 + t] = total
        for m in range(7, 0, -1):
            moment3(m).start()

    def wide(v):
        zero = jnp.zeros_like(v)
        return jnp.concatenate(
            [jnp.where(left, v, zero), jnp.where(left, zero, v)], axis=0
        )

    def product(lhs, rhs):
        lh, ll = split(lhs)
        rh, rl = split(rhs)
        both = jnp.dot(
            jnp.concatenate([lh, ll], axis=1),
            jnp.concatenate(
                [
                    jnp.concatenate([rh, rl], axis=1),
                    jnp.concatenate([rh, jnp.zeros_like(rl)], axis=1),
                ],
                axis=0,
            ),
            preferred_element_type=F32,
        )
        return both[:, : rhs.shape[1]] + both[:, rhs.shape[1] :]

    exact = functools.partial(
        jnp.dot, precision=lax.Precision.HIGHEST, preferred_element_type=F32
    )

    def invert(matrices):
        eye = jnp.where(rem(lane64, HALF) == row64, 1.0, 0.0).astype(F32)
        weight, start = chebyshev()

        def double(_, carry):
            value, state = carry
            following = 2.0 * value * value - 1.0
            g = 2.0 * value * value / following
            doubled = []
            for left_over, inverse in state:
                both = product(
                    jnp.concatenate([left_over, inverse], axis=0), wide(left_over)
                )
                doubled.append(
                    (g * both[:HALF] - (g - 1.0) * eye, g * (inverse + both[HALF:]))
                )
            return following, tuple(doubled)

        state = tuple((eye - weight * a, weight * eye) for a in matrices)
        _, state = lax.fori_loop(
            0, DOUBLINGS, double, (jnp.full((1, BLOCK), start, F32), state)
        )
        results = []
        for a, (_, inverse) in zip(matrices, state):
            error = exact(a, wide(inverse))
            results.append(2.0 * inverse - exact(inverse, wide(error)))
        return results

    def inverses():
        with scope("wait_moment3"):
            wait(part.at[pl.ds(32, 7)], mrecv.at[2])
        whole = part[32:40].reshape(2 * HALF, BLOCK)
        outs, ins = whole[:HALF], whole[HALF:]
        live = jnp.max(jnp.where(left, 0.0, ins))
        ins = jnp.where(left, ins, pltpu.roll(ins, HALF, 1))
        diagonal = rem(lane64, HALF) == row64
        left_row = left[0:1]

        def traces(v):
            on = jnp.sum(jnp.where(diagonal, v, 0.0), axis=0, keepdims=True)
            a = jnp.sum(jnp.where(left_row, on, 0.0), axis=1, keepdims=True)
            b = jnp.sum(jnp.where(left_row, 0.0, on), axis=1, keepdims=True)
            return jnp.where(left_row, a, b)

        trace_out, trace_in = traces(outs), traces(ins)
        added = jnp.where(diagonal, DAMPING / RANK, 0.0).astype(F32)
        inv_out, inv_in = invert([outs / trace_out + added, ins / trace_in + added])
        return inv_out * (live / trace_out), inv_in * (live / trace_in)

    def diagonal_or_not(f):
        pl.when(on_diagonal)(functools.partial(f, 31))
        unless(on_diagonal)(functools.partial(f, 32))

    def solve(inv_out, inv_in):
        with scope("wait_sketches"):
            wait(part.at[pl.ds(64, 28)], brecv.at[2])
        wide_out = wide(inv_out)
        solved = []
        for e in range(8):
            sketch = jnp.concatenate(
                [part[64 + 4 * (4 * (e % 2) + q) + e // 2] for q in range(4)], axis=0
            )
            solved.append(
                fold(product(wide_out, jnp.concatenate([sketch, sketch], axis=0)))
            )
        return product(jnp.concatenate(solved, axis=0), wide(inv_in))

    def final(a, tt):
        return remote(msg.at[a], fin.at[d * 2 + z], fsend, frecv, 4 * x + a, tt)

    def score(weights, scale):
        with scope("wait_share"):
            for r in range(2):
                wait(qall.at[pl.ds(0, 3)], qrecv.at[r])
        queries = qall[...]
        rows = []
        for e in range(8):
            rows.append(
                jnp.sum(queries * weights[e * HALF : (e + 1) * HALF][None], axis=1)
            )
        sums = exact(jnp.concatenate(rows, axis=0), jnp.ones((BLOCK, BLOCK), F32))
        row = lax.broadcasted_iota(jnp.int32, (HALF, BLOCK), 0)
        lane = lax.broadcasted_iota(jnp.int32, (HALF, BLOCK), 1)
        query = 8 * z + 2 * rem(row, 4) + rem(div(row, 4), 2)
        sums = jnp.where(lane == rem(d, 8) * 16 + query, sums * scale, 0.0)
        sums = [
            jnp.sum(sums[e * 8 : (e + 1) * 8], axis=0, keepdims=True) for e in range(8)
        ]
        for a in range(4):
            msg[a] = jnp.concatenate(sums[2 * a : 2 * a + 2], axis=0)

        @pl.loop(0, 32)
        def _(j):
            a, tt = div(j, 8), rem(j, 8)
            me = is_me(4 * x + a, tt)

            @unless(me)
            def _():
                final(a, tt).start()

            @pl.when(me)
            def _():
                fin[d * 2 + z] = msg[a]

    def do(name, f, *args):
        with scope(name):
            return f(*args)

    @pl.loop(0, 6)
    def _(four):
        do("project", project, four)

        @pl.when(four == 0)
        def _():
            do("barrier_wait", everyone_is_here)
            send_items((2, 7), (1, 7), (0, 6), (2, 6), (1, 6), (0, 5), (2, 5), (2, 4))

        @pl.when(four == 1)
        def _():
            send_items((1, 3), (0, 2), (1, 2), (0, 1))

        @pl.when(four == 3)
        def _():
            do("halve2_0", halve2, 0)
            do("halve1_1", halve1, 1)

        @pl.when(four == 4)
        def _():
            do("halve3_0", halve3, 0)

    do("halve1_2", halve1, 2)
    do("halve2_1", halve2, 1)
    do("train_finish", train_finish)
    do("halve3_1", halve3, 1)
    do("halve2_2", halve2, 2)
    do("moments_over_dp", moments_over_dp)
    do("sketches_out", sketches_out)
    do("share_1", share_sketch, 1)
    do("halve3_2", halve3, 2)
    do("moments_back", moments_back)
    do("sketches_across", sketches_across)
    do("share_2", share_sketch, 2)
    inv_out, inv_in = do("inverses", inverses)
    weights = do("solve", solve, inv_out, inv_in)
    train_positions, query_positions = tin.shape[1], qin.shape[1]
    scale = 1.0 / (RANK * math.sqrt(train_positions * query_positions))
    do("score", score, weights, scale)

    with scope("drain"):
        wait(acc.at[pl.ds(0, 21)], send)
        wait(part.at[pl.ds(0, 29)], msend)
        wait(part.at[pl.ds(0, 46)], bsend)
        wait(qall.at[pl.ds(0, 6)], qsend)
    with scope("final_wait"):
        diagonal_or_not(lambda n: wait(fin.at[pl.ds(0, n)], frecv))
    with scope("final_drain"):
        diagonal_or_not(lambda n: wait(fin.at[pl.ds(0, n)], fsend))
    low, high = fin[0], fin[16]
    for j in range(1, 16):
        low = low + fin[j]
        high = high + fin[j + 16]
    out_ref[:, :BLOCK] = low
    out_ref[:, BLOCK:] = high


def on_device(tin, tgr, tlen, qin, qgr, qlen, pin, pout):
    hbm = pl.BlockSpec(memory_space=pltpu.HBM)
    features, units = pin.shape[0], pout.shape[1]
    dma = pltpu.SemaphoreType.DMA
    return pl.pallas_call(
        kernel,
        out_shape=jax.ShapeDtypeStruct((tin.shape[0], DP * qin.shape[0]), F32),
        in_specs=[hbm] * 8,
        out_specs=pl.BlockSpec(memory_space=pltpu.VMEM),
        scratch_shapes=[
            pltpu.SMEM(tlen.shape, jnp.int32),
            pltpu.SMEM(qlen.shape, jnp.int32),
            pltpu.VMEM((12, 2 * BLOCK, features), BF16),
            pltpu.VMEM((2, 24 * BLOCK, units), BF16),
            pltpu.VMEM((2, BLOCK, features), BF16),
            pltpu.VMEM((2, BLOCK, units), BF16),
            pltpu.VMEM((24, HALF + BLOCK, BLOCK), F32),
            pltpu.VMEM((24, HALF + BLOCK, BLOCK), F32),
            pltpu.VMEM((3, 3, 2, HALF, BLOCK), F32),
            pltpu.VMEM((3, 3, HALF, BLOCK), F32),
            pltpu.VMEM((96, 16, BLOCK), F32),
            pltpu.VMEM((16, BLOCK), F32),
            pltpu.VMEM((16, BLOCK), F32),
            pltpu.VMEM((8, HALF, BLOCK), F32),
            pltpu.VMEM((4, 2, BLOCK), F32),
            pltpu.VMEM((32, 2, BLOCK), F32),
            dma((4,)), dma((4,)), dma((4,)),
            dma, dma((3, 3)), dma((2, 3)), dma((2, 3)), dma, dma((3,)), dma, dma((3,)), dma, dma((2,)), dma, dma,
        ],
        compiler_params=pltpu.CompilerParams(
            collective_id=0, has_side_effects=True, vmem_limit_bytes=56 * 1024 * 1024
        ),
    )(tlen, qlen, tin, tgr, qin, qgr, pin.T, pout.transpose(0, 2, 1))


def solution(mesh):
    placed = (
        P("dp", None, "tensor"),
        P("dp", None, None, "tensor"),
        P("dp"),
        P("dp", None, "tensor"),
        P("dp", None, None, "tensor"),
        P("dp"),
        P("tensor", None),
        P(None, "tensor", None),
    )
    return jax.shard_map(
        on_device, mesh=mesh, in_specs=placed, out_specs=P("dp", None), check_vma=False
    )
```

```python
import contextlib
import functools
import math

import jax
import jax.numpy as jnp
from jax import lax
from jax.experimental import pallas as pl
from jax.experimental.pallas import tpu as pltpu
from jax.sharding import PartitionSpec as P

MESH = pl.DeviceIdType.MESH
SCOPES = False


def scope(name):
    return jax.named_scope(name) if SCOPES else contextlib.nullcontext()


F32 = jnp.float32
BF16 = jnp.bfloat16
DAMPING = 0.1
RANK = 64
BLOCK = 128
HALF = 64
DP = 16
DOUBLINGS = 7
GENS = ((1, 3, 4), (3, 4, 1), (4, 1, 3))


def chebyshev():
    low = DAMPING / RANK
    high = 1.0 + low
    return 2.0 / (high + low), (high + low) / (high - low)


def rem(a, b):
    return lax.rem(a, jnp.int32(b))


def div(a, b):
    return lax.div(a, jnp.int32(b))


def split(v):
    high = v.astype(BF16)
    return high, (v - high.astype(F32)).astype(BF16)


def kernel(
    tlen_hbm, qlen_hbm, tin, tgr, qin, qgr, pin, pout, out_ref,
    tlen, qlen, xin, xgr, wip, wop, acc, got, got2, got3, part, msum, bsum, qall, msg, fin,
    wsem, isem, gsem, send, recv1, recv2, recv3, msend, mrecv, bsend, brecv, qsend, qrecv, fsend, frecv,
):
    d = lax.axis_index("dp").astype(jnp.int32)
    t = lax.axis_index("tensor").astype(jnp.int32)
    z, x = div(t, 4), rem(t, 4)
    column = div(d, 4)
    on_diagonal = column == x

    def flip(m):
        m = jnp.int32(m)
        mx, mz = rem(m, 4), div(m, 4)
        low = rem(x + mx, 2)
        high = rem(div(x, 2) + div(mx, 2), 2)
        return rem(z + mz, 2) * 4 + high * 2 + low

    def remote(src, dst, ssem, rsem, dd, tt):
        return pltpu.make_async_remote_copy(
            src_ref=src, dst_ref=dst, send_sem=ssem, recv_sem=rsem,
            device_id=(dd, tt), device_id_type=MESH,
        )

    def wait(ref, sem):
        pltpu.make_async_copy(ref, ref, sem).wait()

    def is_me(dd, tt):
        return jnp.logical_and(dd == d, tt == t)

    def unless(condition):
        return pl.when(jnp.logical_not(condition))

    def load(pair, query):
        sem = rem(pair, 4)
        m = 7 - 2 * sem
        for h in range(2):
            item = flip(m - h)
            if query:
                q = item * 2 + (div(pair, 4) - 1)
                a, b = qin.at[q], qgr.at[q]
            else:
                rows = pl.ds(pl.multiple_of(rem(item, 4) * BLOCK, BLOCK), BLOCK)
                e = div(item, 4)
                a, b = tin.at[e, rows, :], tgr.at[e, :, rows, :]
            to = pl.ds(h * BLOCK, BLOCK)
            pltpu.make_async_copy(a, xin.at[pair, to], isem.at[sem]).start()
            to = pl.ds((pair * 2 + h) * BLOCK, BLOCK)
            pltpu.make_async_copy(b, xgr.at[:, to], gsem.at[sem]).start()

    with scope("start_loads"):
        pltpu.make_async_copy(pin, wip.at[0, :RANK], wsem.at[0]).start()
        pltpu.make_async_copy(pin, wip.at[1, RANK:], wsem.at[0]).start()
        pltpu.make_async_copy(pout.at[0], wop.at[0, :RANK], wsem.at[1]).start()
        pltpu.make_async_copy(pout.at[1], wop.at[1, RANK:], wsem.at[1]).start()

        @pl.loop(0, 4)
        def _(pair):
            load(pair, False)

        lengths = (
            pltpu.make_async_copy(tlen_hbm, tlen, wsem.at[2]),
            pltpu.make_async_copy(qlen_hbm, qlen, wsem.at[3]),
        )
        for c in lengths:
            c.start()

    barrier = pltpu.get_barrier_semaphore()

    def greet(dd, tt):
        pl.semaphore_signal(barrier, inc=1, device_id=(dd, tt), device_id_type=MESH)

    with scope("greet"):

        @pl.loop(1, 16)
        def _(j):
            greet(rem(d + j, DP), t)

        @pl.loop(1, 8)
        def _(m):
            greet(d, flip(8 - m))

    with scope("weights"):
        wip[0, RANK:] = jnp.zeros(pin.shape, BF16)
        wip[1, :RANK] = jnp.zeros(pin.shape, BF16)
        wop[0, RANK:] = jnp.zeros(pout.shape[1:], BF16)
        wop[1, :RANK] = jnp.zeros(pout.shape[1:], BF16)
        wait(wip.at[0], wsem.at[0])
        wait(wop.at[0], wsem.at[1])
        for c in lengths:
            c.wait()

    def rows_of(p):
        return slice(HALF * p, HALF * (p + 1))

    def piece(r, p, m):
        return acc.at[r * 8 + m, rows_of(p)]

    def first(r, p, m, s):
        return remote(
            piece(r, p, m), got.at[r * 8 + s, rows_of(p)],
            send, recv1.at[r, p], d, flip(GENS[p][0]),
        )

    def times(rows, turned):
        return lax.dot_general(
            rows, turned, (((1,), (1,)), ((), ())), preferred_element_type=F32
        )

    def project(four):
        pairs = (2 * four, 2 * four + 1)
        for pair in pairs:
            sem = rem(pair, 4)
            wait(xin.at[pair], isem.at[sem])
            wait(xgr.at[:, pl.ds(pair * 2 * BLOCK, 2 * BLOCK)], gsem.at[sem])

        @pl.when(four < 4)
        def _():
            for pair in pairs:
                load(pair + 4, True)

        def rows(start):
            return jnp.concatenate(
                [
                    xin[pair, h * BLOCK + start : h * BLOCK + start + HALF]
                    for pair in pairs
                    for h in range(2)
                ],
                axis=0,
            )

        ins = times(rows(0), wip[0]) + times(rows(HALF), wip[1])
        units = pl.ds(four * 4 * BLOCK, 4 * BLOCK)
        outs = times(xgr[0, units], wop[0]) + times(xgr[1, units], wop[1])
        for i in range(4):
            slot = div(four, 2) * 8 + 7 - 4 * rem(four, 2) - i
            acc[slot, :HALF] = ins[i * HALF : (i + 1) * HALF]
            acc[slot, HALF:] = outs[i * BLOCK : (i + 1) * BLOCK]

    def send_items(*which):
        for p, m in which:
            first(0, p, m, m ^ GENS[p][0]).start()

    def everyone_is_here():
        pl.semaphore_wait(barrier, 22)

    def halve1(r):
        for k in range(4):
            for p, (g1, g2, g3) in enumerate(GENS):
                s = (g2, g2 ^ g3, g3, 0)[k]
                first(r, p, s ^ g1, s).start()

    def add(r, p, s, ref):
        rows = rows_of(p)
        acc[r * 8 + s, rows] = acc[r * 8 + s, rows] + ref[...]

    def halve2(r):
        for p, (_, g2, g3) in enumerate(GENS):
            wait(qall.at[pl.ds(0, 4)], recv1.at[r, p])
            for k, s in enumerate((g2, g2 ^ g3)):
                add(r, p, s, got.at[r * 8 + s, rows_of(p)])
                remote(
                    piece(r, p, s), got2.at[r, p, k],
                    send, recv2.at[r % 2, p], d, flip(g2),
                ).start()
        for p, (_, _, g3) in enumerate(GENS):
            for s in (g3, 0):
                add(r, p, s, got.at[r * 8 + s, rows_of(p)])

    def halve3(r):
        for p, (_, _, g3) in enumerate(GENS):
            wait(qall.at[pl.ds(0, 2)], recv2.at[r % 2, p])
            add(r, p, g3, got2.at[r, p, 1])
            remote(
                piece(r, p, g3), got3.at[r, p], send, recv3.at[r % 2, p], d, flip(g3)
            ).start()
        for p in range(3):
            add(r, p, 0, got2.at[r, p, 0])

    def halved(r):
        for p in range(3):
            wait(qall.at[0], recv3.at[r % 2, p])
        return acc[r * 8] + jnp.concatenate([got3[r, p] for p in range(3)], axis=0)

    row64 = lax.broadcasted_iota(jnp.int32, (HALF, BLOCK), 0)
    lane64 = lax.broadcasted_iota(jnp.int32, (HALF, BLOCK), 1)
    left = lane64 < HALF

    def finished(total, length):
        position = jnp.where(left, row64, row64 + HALF)
        inputs = jnp.where(position < length, total[:HALF], 0.0)
        turned = pltpu.roll(inputs, HALF, 1)
        twice = jnp.concatenate(
            [jnp.where(left, inputs, turned), jnp.where(left, turned, inputs)], axis=0
        ).astype(BF16)
        outputs = jnp.concatenate(
            [
                jnp.where(row64 < length, total[HALF:BLOCK], 0.0),
                jnp.where(row64 + HALF < length, total[BLOCK:], 0.0),
            ],
            axis=0,
        )
        return twice, outputs.astype(BF16), outputs.T.astype(BF16)

    def fold(full):
        return jnp.where(left, full[:HALF], full[HALF:])

    def query_sketch(total, r):
        length = qlen[t * 2 + (r - 1)]
        twice, _, turned = finished(total, length)
        return fold(jnp.dot(turned, twice, preferred_element_type=F32))

    def share(r, m):
        mine = qall.at[(r - 1) * 4 + x]
        return remote(mine, mine, qsend, qrecv.at[r - 1], d, flip(m))

    def share_sketch(r):
        with scope("halved"):
            total = halved(r)
        qall[(r - 1) * 4 + x] = query_sketch(total, r)
        for m in (2, 1, 3):
            share(r, m).start()

    def moment1(m):
        return remote(part.at[flip(m)], part.at[8 + m], msend, mrecv.at[0], d, flip(m))

    def moment2(j):
        return remote(msum, part.at[16 + d], msend, mrecv.at[1], rem(d + j, DP), t)

    def moment3(m):
        return remote(
            part.at[32 + t], part.at[32 + t], msend, mrecv.at[2], d, flip(m)
        )

    def sketch1(m):
        return remote(
            part.at[40 + rem(flip(m), 4)], part.at[44 + m], bsend, brecv.at[0], d, flip(m)
        )

    def sketch2(j):
        return remote(bsum, part.at[48 + d], bsend, brecv.at[1], rem(d + j, DP), t)

    def sketch3(m):
        return remote(
            part.at[pl.ds(48 + 4 * rem(flip(m), 4), 4)], part.at[pl.ds(64 + 4 * t, 4)],
            bsend, brecv.at[2], d, flip(m),
        )

    def train_finish():
        with scope("halved"):
            total = halved(0)
        length = tlen[z] - x * BLOCK
        twice, outputs, turned = finished(total, length)
        products = jnp.dot(
            turned, jnp.concatenate([outputs, twice], axis=1), preferred_element_type=F32
        )
        ins = lax.dot_general(
            twice, twice, (((0,), (0,)), ((), ())), preferred_element_type=F32
        )
        live = jnp.minimum(jnp.maximum(length, 0), BLOCK).astype(F32)
        part[0:4] = fold(products[:, :BLOCK]).reshape(4, 16, BLOCK)
        part[4:8] = jnp.where(left, ins[:HALF], live).reshape(4, 16, BLOCK)
        for m in range(7, 0, -1):
            moment1(m).start()
        part[40:44] = fold(products[:, BLOCK:]).reshape(4, 16, BLOCK)
        for m in range(1, 4):
            sketch1(m).start()

    def moments_over_dp():
        wait(part.at[pl.ds(9, 7)], mrecv.at[0])
        total = part[t]
        for m in range(1, 8):
            total = total + part[8 + m]
        msum[...] = total
        part[16 + d] = total

        @pl.loop(1, 16)
        def _(j):
            moment2(j).start()

    def sketches_out():
        wait(part.at[pl.ds(45, 3)], brecv.at[0])
        total = part[40 + x]
        for m in range(1, 4):
            total = total + part[44 + m]
        bsum[...] = total
        part[48 + d] = total

        @pl.loop(1, 16)
        def _(j):
            sketch2(j).start()

    def sketches_across():
        wait(part.at[pl.ds(48, 15)], brecv.at[1])
        part[pl.ds(64 + 4 * t, 4)] = part[pl.ds(48 + 4 * x, 4)]
        for m in range(7, 0, -1):
            sketch3(m).start()

    def moments_back():
        wait(part.at[pl.ds(16, 15)], mrecv.at[1])
        total = part[16]
        for j in range(1, 16):
            total = total + part[16 + j]
        part[32 + t] = total
        for m in range(7, 0, -1):
            moment3(m).start()

    def wide(v):
        zero = jnp.zeros_like(v)
        return jnp.concatenate(
            [jnp.where(left, v, zero), jnp.where(left, zero, v)], axis=0
        )

    def product(lhs, rhs):
        lh, ll = split(lhs)
        rh, rl = split(rhs)
        both = jnp.dot(
            jnp.concatenate([lh, ll], axis=1),
            jnp.concatenate(
                [
                    jnp.concatenate([rh, rl], axis=1),
                    jnp.concatenate([rh, jnp.zeros_like(rl)], axis=1),
                ],
                axis=0,
            ),
            preferred_element_type=F32,
        )
        return both[:, : rhs.shape[1]] + both[:, rhs.shape[1] :]

    exact = functools.partial(
        jnp.dot, precision=lax.Precision.HIGHEST, preferred_element_type=F32
    )

    def invert(matrices):
        eye = jnp.where(rem(lane64, HALF) == row64, 1.0, 0.0).astype(F32)
        weight, start = chebyshev()

        def double(_, carry):
            value, state = carry
            following = 2.0 * value * value - 1.0
            g = 2.0 * value * value / following
            doubled = []
            for left_over, inverse in state:
                both = product(
                    jnp.concatenate([left_over, inverse], axis=0), wide(left_over)
                )
                doubled.append(
                    (g * both[:HALF] - (g - 1.0) * eye, g * (inverse + both[HALF:]))
                )
            return following, tuple(doubled)

        state = tuple((eye - weight * a, weight * eye) for a in matrices)
        _, state = lax.fori_loop(
            0, DOUBLINGS, double, (jnp.full((1, BLOCK), start, F32), state)
        )
        results = []
        for a, (_, inverse) in zip(matrices, state):
            error = exact(a, wide(inverse))
            results.append(2.0 * inverse - exact(inverse, wide(error)))
        return results

    def inverses():
        with scope("wait_moment3"):
            wait(part.at[pl.ds(32, 7)], mrecv.at[2])
        whole = part[32:40].reshape(2 * HALF, BLOCK)
        outs, ins = whole[:HALF], whole[HALF:]
        live = jnp.max(jnp.where(left, 0.0, ins))
        ins = jnp.where(left, ins, pltpu.roll(ins, HALF, 1))
        diagonal = rem(lane64, HALF) == row64
        left_row = left[0:1]

        def traces(v):
            on = jnp.sum(jnp.where(diagonal, v, 0.0), axis=0, keepdims=True)
            a = jnp.sum(jnp.where(left_row, on, 0.0), axis=1, keepdims=True)
            b = jnp.sum(jnp.where(left_row, 0.0, on), axis=1, keepdims=True)
            return jnp.where(left_row, a, b)

        trace_out, trace_in = traces(outs), traces(ins)
        added = jnp.where(diagonal, DAMPING / RANK, 0.0).astype(F32)
        inv_out, inv_in = invert([outs / trace_out + added, ins / trace_in + added])
        return inv_out * (live / trace_out), inv_in * (live / trace_in)

    def diagonal_or_not(f):
        pl.when(on_diagonal)(functools.partial(f, 31))
        unless(on_diagonal)(functools.partial(f, 32))

    def solve(inv_out, inv_in):
        with scope("wait_sketches"):
            wait(part.at[pl.ds(64, 28)], brecv.at[2])
        wide_out = wide(inv_out)
        solved = []
        for e in range(8):
            sketch = jnp.concatenate(
                [part[64 + 4 * (4 * (e % 2) + q) + e // 2] for q in range(4)], axis=0
            )
            solved.append(
                fold(product(wide_out, jnp.concatenate([sketch, sketch], axis=0)))
            )
        return product(jnp.concatenate(solved, axis=0), wide(inv_in))

    def final(a, tt):
        return remote(msg.at[a], fin.at[d * 2 + z], fsend, frecv, 4 * x + a, tt)

    def score(weights, scale):
        with scope("wait_share"):
            for r in range(2):
                wait(qall.at[pl.ds(0, 3)], qrecv.at[r])
        queries = qall[...]
        rows = []
        for e in range(8):
            rows.append(
                jnp.sum(queries * weights[e * HALF : (e + 1) * HALF][None], axis=1)
            )
        sums = exact(jnp.concatenate(rows, axis=0), jnp.ones((BLOCK, BLOCK), F32))
        row = lax.broadcasted_iota(jnp.int32, (HALF, BLOCK), 0)
        lane = lax.broadcasted_iota(jnp.int32, (HALF, BLOCK), 1)
        query = 8 * z + 2 * rem(row, 4) + rem(div(row, 4), 2)
        sums = jnp.where(lane == rem(d, 8) * 16 + query, sums * scale, 0.0)
        sums = [
            jnp.sum(sums[e * 8 : (e + 1) * 8], axis=0, keepdims=True) for e in range(8)
        ]
        for a in range(4):
            msg[a] = jnp.concatenate(sums[2 * a : 2 * a + 2], axis=0)

        @pl.loop(0, 32)
        def _(j):
            a, tt = div(j, 8), rem(j, 8)
            me = is_me(4 * x + a, tt)

            @unless(me)
            def _():
                final(a, tt).start()

            @pl.when(me)
            def _():
                fin[d * 2 + z] = msg[a]

    def do(name, f, *args):
        with scope(name):
            return f(*args)

    @pl.loop(0, 6)
    def _(four):
        do("project", project, four)

        @pl.when(four == 0)
        def _():
            do("barrier_wait", everyone_is_here)
            send_items((2, 7), (1, 7), (0, 6), (2, 6), (1, 6), (0, 5), (2, 5), (2, 4))

        @pl.when(four == 1)
        def _():
            send_items((1, 3), (0, 2), (1, 2), (0, 1))

        @pl.when(four == 3)
        def _():
            do("halve2_0", halve2, 0)
            do("halve1_1", halve1, 1)

        @pl.when(four == 4)
        def _():
            do("halve3_0", halve3, 0)

    do("halve1_2", halve1, 2)
    do("halve2_1", halve2, 1)
    do("train_finish", train_finish)
    do("halve3_1", halve3, 1)
    do("halve2_2", halve2, 2)
    do("moments_over_dp", moments_over_dp)
    do("sketches_out", sketches_out)
    do("share_1", share_sketch, 1)
    do("halve3_2", halve3, 2)
    do("moments_back", moments_back)
    do("sketches_across", sketches_across)
    do("share_2", share_sketch, 2)
    inv_out, inv_in = do("inverses", inverses)
    weights = do("solve", solve, inv_out, inv_in)
    train_positions, query_positions = tin.shape[1], qin.shape[1]
    scale = 1.0 / (RANK * math.sqrt(train_positions * query_positions))
    do("score", score, weights, scale)

    with scope("drain"):
        wait(acc.at[pl.ds(0, 21)], send)
        wait(part.at[pl.ds(0, 29)], msend)
        wait(part.at[pl.ds(0, 46)], bsend)
        wait(qall.at[pl.ds(0, 6)], qsend)
    with scope("final_wait"):
        diagonal_or_not(lambda n: wait(fin.at[pl.ds(0, n)], frecv))
    with scope("final_drain"):
        diagonal_or_not(lambda n: wait(fin.at[pl.ds(0, n)], fsend))
    low, high = fin[0], fin[16]
    for j in range(1, 16):
        low = low + fin[j]
        high = high + fin[j + 16]
    out_ref[:, :BLOCK] = low
    out_ref[:, BLOCK:] = high


def on_device(tin, tgr, tlen, qin, qgr, qlen, pin, pout):
    hbm = pl.BlockSpec(memory_space=pltpu.HBM)
    features, units = pin.shape[0], pout.shape[1]
    dma = pltpu.SemaphoreType.DMA
    return pl.pallas_call(
        kernel,
        out_shape=jax.ShapeDtypeStruct((tin.shape[0], DP * qin.shape[0]), F32),
        in_specs=[hbm] * 8,
        out_specs=pl.BlockSpec(memory_space=pltpu.VMEM),
        scratch_shapes=[
            pltpu.SMEM(tlen.shape, jnp.int32),
            pltpu.SMEM(qlen.shape, jnp.int32),
            pltpu.VMEM((12, 2 * BLOCK, features), BF16),
            pltpu.VMEM((2, 24 * BLOCK, units), BF16),
            pltpu.VMEM((2, BLOCK, features), BF16),
            pltpu.VMEM((2, BLOCK, units), BF16),
            pltpu.VMEM((24, HALF + BLOCK, BLOCK), F32),
            pltpu.VMEM((24, HALF + BLOCK, BLOCK), F32),
            pltpu.VMEM((3, 3, 2, HALF, BLOCK), F32),
            pltpu.VMEM((3, 3, HALF, BLOCK), F32),
            pltpu.VMEM((96, 16, BLOCK), F32),
            pltpu.VMEM((16, BLOCK), F32),
            pltpu.VMEM((16, BLOCK), F32),
            pltpu.VMEM((8, HALF, BLOCK), F32),
            pltpu.VMEM((4, 2, BLOCK), F32),
            pltpu.VMEM((32, 2, BLOCK), F32),
            dma((4,)), dma((4,)), dma((4,)),
            dma, dma((3, 3)), dma((2, 3)), dma((2, 3)), dma, dma((3,)), dma, dma((3,)), dma, dma((2,)), dma, dma,
        ],
        compiler_params=pltpu.CompilerParams(
            collective_id=0, has_side_effects=True, vmem_limit_bytes=56 * 1024 * 1024
        ),
    )(tlen, qlen, tin, tgr, qin, qgr, pin.T, pout.transpose(0, 2, 1))


def solution(mesh):
    placed = (
        P("dp", None, "tensor"),
        P("dp", None, None, "tensor"),
        P("dp"),
        P("dp", None, "tensor"),
        P("dp", None, None, "tensor"),
        P("dp"),
        P("tensor", None),
        P(None, "tensor", None),
    )
    return jax.shard_map(
        on_device, mesh=mesh, in_specs=placed, out_specs=P("dp", None), check_vma=False
    )
```

```python
import contextlib
import functools
import math

import jax
import jax.numpy as jnp
from jax import lax
from jax.experimental import pallas as pl
from jax.experimental.pallas import tpu as pltpu
from jax.sharding import PartitionSpec as P

MESH = pl.DeviceIdType.MESH
SCOPES = False


def scope(name):
    return jax.named_scope(name) if SCOPES else contextlib.nullcontext()


F32 = jnp.float32
BF16 = jnp.bfloat16
DAMPING = 0.1
RANK = 64
BLOCK = 128
HALF = 64
DP = 16
DOUBLINGS = 7
ROUTES = ((1, 5, 4, 1), (3, 2, 1, 2), (4, 7, 3, 0))


def chebyshev():
    low = DAMPING / RANK
    high = 1.0 + low
    return 2.0 / (high + low), (high + low) / (high - low)


def rem(a, b):
    return lax.rem(a, jnp.int32(b))


def div(a, b):
    return lax.div(a, jnp.int32(b))


def split(v):
    high = v.astype(BF16)
    return high, (v - high.astype(F32)).astype(BF16)


def kernel(
    tlen_hbm, qlen_hbm, tin, tgr, qin, qgr, pin, pout, out_ref,
    tlen, qlen, xin, xgr, wip, wop, acc, far, near, last, part, msum, bsum, qall, msg, fin,
    wsem, isem, gsem, send, recv1, recv2, msend, mrecv, bsend, brecv, qsend, qrecv, fsend, frecv,
):
    d = lax.axis_index("dp").astype(jnp.int32)
    t = lax.axis_index("tensor").astype(jnp.int32)
    z, x = div(t, 4), rem(t, 4)
    column = div(d, 4)
    on_diagonal = column == x

    def flip(m):
        m = jnp.int32(m)
        mx, mz = rem(m, 4), div(m, 4)
        low = rem(x + mx, 2)
        high = rem(div(x, 2) + div(mx, 2), 2)
        return rem(z + mz, 2) * 4 + high * 2 + low

    def remote(src, dst, ssem, rsem, dd, tt):
        return pltpu.make_async_remote_copy(
            src_ref=src, dst_ref=dst, send_sem=ssem, recv_sem=rsem,
            device_id=(dd, tt), device_id_type=MESH,
        )

    def wait(ref, sem):
        pltpu.make_async_copy(ref, ref, sem).wait()

    def is_me(dd, tt):
        return jnp.logical_and(dd == d, tt == t)

    def unless(condition):
        return pl.when(jnp.logical_not(condition))

    def items(four):
        second = rem(four, 2)
        return (7 - 3 * second, 6 - 3 * second, 5 - 4 * second, 2 - 2 * second)

    def load(four, query):
        sem = rem(four, 2)
        for k, m in enumerate(items(four)):
            item = flip(m)
            if query:
                q = item * 2 + (div(four, 2) - 1)
                a, b = qin.at[q], qgr.at[q]
            else:
                rows = pl.ds(pl.multiple_of(rem(item, 4) * BLOCK, BLOCK), BLOCK)
                e = div(item, 4)
                a, b = tin.at[e, rows, :], tgr.at[e, :, rows, :]
            to = pl.ds((four * 4 + k) * BLOCK, BLOCK)
            pltpu.make_async_copy(a, xin.at[to], isem.at[sem]).start()
            pltpu.make_async_copy(b, xgr.at[:, to], gsem.at[sem]).start()

    with scope("start_loads"):
        pltpu.make_async_copy(pin, wip.at[0, :RANK], wsem.at[0]).start()
        pltpu.make_async_copy(pin, wip.at[1, RANK:], wsem.at[0]).start()
        pltpu.make_async_copy(pout.at[0], wop.at[0, :RANK], wsem.at[1]).start()
        pltpu.make_async_copy(pout.at[1], wop.at[1, RANK:], wsem.at[1]).start()

        @pl.loop(0, 2)
        def _(four):
            load(four, False)

        lengths = (
            pltpu.make_async_copy(tlen_hbm, tlen, wsem.at[2]),
            pltpu.make_async_copy(qlen_hbm, qlen, wsem.at[3]),
        )
        for c in lengths:
            c.start()

    barrier = pltpu.get_barrier_semaphore()

    def greet(dd, tt):
        pl.semaphore_signal(barrier, inc=1, device_id=(dd, tt), device_id_type=MESH)

    with scope("greet"):

        @pl.loop(1, 16)
        def _(j):
            greet(rem(d + j, DP), t)

        @pl.loop(1, 8)
        def _(m):
            greet(d, flip(8 - m))

    with scope("weights"):
        wip[0, RANK:] = jnp.zeros(pin.shape, BF16)
        wip[1, :RANK] = jnp.zeros(pin.shape, BF16)
        wop[0, RANK:] = jnp.zeros(pout.shape[1:], BF16)
        wop[1, :RANK] = jnp.zeros(pout.shape[1:], BF16)
        wait(wip.at[0], wsem.at[0])
        wait(wop.at[0], wsem.at[1])
        for c in lengths:
            c.wait()

    def times(rows, turned):
        return lax.dot_general(
            rows, turned, (((1,), (1,)), ((), ())), preferred_element_type=F32
        )

    def project(four):
        r, sem = div(four, 2), rem(four, 2)
        rows = pl.ds(four * 4 * BLOCK, 4 * BLOCK)
        wait(xin.at[rows], isem.at[sem])
        wait(xgr.at[:, rows], gsem.at[sem])

        @pl.when(four < 4)
        def _():
            load(four + 2, True)

        ins = xin[rows].reshape(4, 2, HALF, -1)
        ins = times(ins[:, 0].reshape(4 * HALF, -1), wip[0]) + times(
            ins[:, 1].reshape(4 * HALF, -1), wip[1]
        )
        outs = times(xgr[0, rows], wop[0]) + times(xgr[1, rows], wop[1])
        for k, m in enumerate(items(four)):
            slot = r * 8 + m
            acc[slot, :HALF] = ins[k * HALF : (k + 1) * HALF]
            acc[slot, HALF:] = outs[k * BLOCK : (k + 1) * BLOCK]

    def everyone_is_here():
        pl.semaphore_wait(barrier, 22)

    def phase1(r):
        for k, (g, _, _, p) in enumerate(ROUTES):
            remote(
                acc.at[r * 8 + 6, pl.ds(HALF * p, HALF)], far.at[r, k],
                send, recv1.at[r, k], d, flip(6 ^ g),
            ).start()
        for k, (_, item, via, _) in enumerate(ROUTES):
            remote(
                acc.at[r * 8 + item], near.at[r, k], send, recv1.at[r, k], d, flip(via)
            ).start()

    def phase2(r):
        for k, (g, _, _, p) in enumerate(ROUTES):
            wait(part.at[pl.ds(0, 16)], recv1.at[r, k])
            mine = r * 8 + g
            rows = slice(HALF * p, HALF * (p + 1))
            acc[mine] = acc[mine] + near[r, k]
            acc[mine, rows] = acc[mine, rows] + far[r, k]
            remote(
                acc.at[mine], last.at[r, k], send, recv2.at[r], d, flip(g)
            ).start()

    def summed(r):
        wait(last.at[r], recv2.at[r])
        return acc[r * 8] + last[r, 0] + last[r, 1] + last[r, 2]

    row64 = lax.broadcasted_iota(jnp.int32, (HALF, BLOCK), 0)
    lane64 = lax.broadcasted_iota(jnp.int32, (HALF, BLOCK), 1)
    left = lane64 < HALF

    def finished(total, length):
        position = jnp.where(left, row64, row64 + HALF)
        inputs = jnp.where(position < length, total[:HALF], 0.0)
        turned = pltpu.roll(inputs, HALF, 1)
        twice = jnp.concatenate(
            [jnp.where(left, inputs, turned), jnp.where(left, turned, inputs)], axis=0
        ).astype(BF16)
        outputs = jnp.concatenate(
            [
                jnp.where(row64 < length, total[HALF:BLOCK], 0.0),
                jnp.where(row64 + HALF < length, total[BLOCK:], 0.0),
            ],
            axis=0,
        )
        return twice, outputs.astype(BF16), outputs.T.astype(BF16)

    def fold(full):
        return jnp.where(left, full[:HALF], full[HALF:])

    def query_sketch(total, r):
        length = qlen[t * 2 + (r - 1)]
        twice, _, turned = finished(total, length)
        return fold(jnp.dot(turned, twice, preferred_element_type=F32))

    def share(r, m):
        mine = qall.at[(r - 1) * 4 + x]
        return remote(mine, mine, qsend, qrecv.at[r - 1], d, flip(m))

    def share_sketch(r):
        with scope("summed"):
            total = summed(r)
        qall[(r - 1) * 4 + x] = query_sketch(total, r)
        for m in (2, 1, 3):
            share(r, m).start()

    def moment1(m):
        return remote(part.at[flip(m)], part.at[8 + m], msend, mrecv.at[0], d, flip(m))

    def moment2(j):
        return remote(msum, part.at[16 + d], msend, mrecv.at[1], rem(d + j, DP), t)

    def moment3(m):
        return remote(
            part.at[32 + t], part.at[32 + t], msend, mrecv.at[2], d, flip(m)
        )

    def sketch1(m):
        return remote(
            part.at[40 + rem(flip(m), 4)], part.at[44 + m], bsend, brecv.at[0], d, flip(m)
        )

    def sketch2(j):
        return remote(bsum, part.at[48 + d], bsend, brecv.at[1], rem(d + j, DP), t)

    def sketch3(m):
        return remote(
            part.at[pl.ds(48 + 4 * rem(flip(m), 4), 4)], part.at[pl.ds(64 + 4 * t, 4)],
            bsend, brecv.at[2], d, flip(m),
        )

    def train_finish():
        with scope("summed"):
            total = summed(0)
        length = tlen[z] - x * BLOCK
        twice, outputs, turned = finished(total, length)
        products = jnp.dot(
            turned, jnp.concatenate([outputs, twice], axis=1), preferred_element_type=F32
        )
        ins = lax.dot_general(
            twice, twice, (((0,), (0,)), ((), ())), preferred_element_type=F32
        )
        live = jnp.minimum(jnp.maximum(length, 0), BLOCK).astype(F32)
        part[0:4] = fold(products[:, :BLOCK]).reshape(4, 16, BLOCK)
        part[4:8] = jnp.where(left, ins[:HALF], live).reshape(4, 16, BLOCK)
        for m in range(7, 0, -1):
            moment1(m).start()
        part[40:44] = fold(products[:, BLOCK:]).reshape(4, 16, BLOCK)
        for m in range(1, 4):
            sketch1(m).start()

    def moments_over_dp():
        wait(part.at[pl.ds(9, 7)], mrecv.at[0])
        total = part[t]
        for m in range(1, 8):
            total = total + part[8 + m]
        msum[...] = total
        part[16 + d] = total

        @pl.loop(1, 16)
        def _(j):
            moment2(j).start()

    def sketches_out():
        wait(part.at[pl.ds(45, 3)], brecv.at[0])
        total = part[40 + x]
        for m in range(1, 4):
            total = total + part[44 + m]
        bsum[...] = total
        part[48 + d] = total

        @pl.loop(1, 16)
        def _(j):
            sketch2(j).start()

    def sketches_across():
        wait(part.at[pl.ds(48, 15)], brecv.at[1])
        part[pl.ds(64 + 4 * t, 4)] = part[pl.ds(48 + 4 * x, 4)]
        for m in range(7, 0, -1):
            sketch3(m).start()

    def moments_back():
        wait(part.at[pl.ds(16, 15)], mrecv.at[1])
        total = part[16]
        for j in range(1, 16):
            total = total + part[16 + j]
        part[32 + t] = total
        for m in range(7, 0, -1):
            moment3(m).start()

    def wide(v):
        zero = jnp.zeros_like(v)
        return jnp.concatenate(
            [jnp.where(left, v, zero), jnp.where(left, zero, v)], axis=0
        )

    def product(lhs, rhs):
        lh, ll = split(lhs)
        rh, rl = split(rhs)
        both = jnp.dot(
            jnp.concatenate([lh, ll], axis=1),
            jnp.concatenate(
                [
                    jnp.concatenate([rh, rl], axis=1),
                    jnp.concatenate([rh, jnp.zeros_like(rl)], axis=1),
                ],
                axis=0,
            ),
            preferred_element_type=F32,
        )
        return both[:, : rhs.shape[1]] + both[:, rhs.shape[1] :]

    exact = functools.partial(
        jnp.dot, precision=lax.Precision.HIGHEST, preferred_element_type=F32
    )

    def invert(matrices):
        eye = jnp.where(rem(lane64, HALF) == row64, 1.0, 0.0).astype(F32)
        weight, start = chebyshev()

        def double(_, carry):
            value, state = carry
            following = 2.0 * value * value - 1.0
            g = 2.0 * value * value / following
            doubled = []
            for left_over, inverse in state:
                both = product(
                    jnp.concatenate([left_over, inverse], axis=0), wide(left_over)
                )
                doubled.append(
                    (g * both[:HALF] - (g - 1.0) * eye, g * (inverse + both[HALF:]))
                )
            return following, tuple(doubled)

        state = tuple((eye - weight * a, weight * eye) for a in matrices)
        _, state = lax.fori_loop(
            0, DOUBLINGS, double, (jnp.full((1, BLOCK), start, F32), state)
        )
        results = []
        for a, (_, inverse) in zip(matrices, state):
            error = exact(a, wide(inverse))
            results.append(2.0 * inverse - exact(inverse, wide(error)))
        return results

    def inverses():
        with scope("wait_moment3"):
            wait(part.at[pl.ds(32, 7)], mrecv.at[2])
        whole = part[32:40].reshape(2 * HALF, BLOCK)
        outs, ins = whole[:HALF], whole[HALF:]
        live = jnp.max(jnp.where(left, 0.0, ins))
        ins = jnp.where(left, ins, pltpu.roll(ins, HALF, 1))
        diagonal = rem(lane64, HALF) == row64
        left_row = left[0:1]

        def traces(v):
            on = jnp.sum(jnp.where(diagonal, v, 0.0), axis=0, keepdims=True)
            a = jnp.sum(jnp.where(left_row, on, 0.0), axis=1, keepdims=True)
            b = jnp.sum(jnp.where(left_row, 0.0, on), axis=1, keepdims=True)
            return jnp.where(left_row, a, b)

        trace_out, trace_in = traces(outs), traces(ins)
        added = jnp.where(diagonal, DAMPING / RANK, 0.0).astype(F32)
        inv_out, inv_in = invert([outs / trace_out + added, ins / trace_in + added])
        return inv_out * (live / trace_out), inv_in * (live / trace_in)

    def diagonal_or_not(f):
        pl.when(on_diagonal)(functools.partial(f, 31))
        unless(on_diagonal)(functools.partial(f, 32))

    def solve(inv_out, inv_in):
        with scope("wait_sketches"):
            wait(part.at[pl.ds(64, 28)], brecv.at[2])
        wide_out = wide(inv_out)
        solved = []
        for e in range(8):
            sketch = jnp.concatenate(
                [part[64 + 4 * (4 * (e % 2) + q) + e // 2] for q in range(4)], axis=0
            )
            solved.append(
                fold(product(wide_out, jnp.concatenate([sketch, sketch], axis=0)))
            )
        return product(jnp.concatenate(solved, axis=0), wide(inv_in))

    def final(a, tt):
        return remote(msg.at[a], fin.at[d * 2 + z], fsend, frecv, 4 * x + a, tt)

    def score(weights, scale):
        with scope("wait_share"):
            for r in range(2):
                wait(qall.at[pl.ds(0, 3)], qrecv.at[r])
        queries = qall[...]
        rows = []
        for e in range(8):
            rows.append(
                jnp.sum(queries * weights[e * HALF : (e + 1) * HALF][None], axis=1)
            )
        sums = exact(jnp.concatenate(rows, axis=0), jnp.ones((BLOCK, BLOCK), F32))
        row = lax.broadcasted_iota(jnp.int32, (HALF, BLOCK), 0)
        lane = lax.broadcasted_iota(jnp.int32, (HALF, BLOCK), 1)
        query = 8 * z + 2 * rem(row, 4) + rem(div(row, 4), 2)
        sums = jnp.where(lane == rem(d, 8) * 16 + query, sums * scale, 0.0)
        sums = [
            jnp.sum(sums[e * 8 : (e + 1) * 8], axis=0, keepdims=True) for e in range(8)
        ]
        for a in range(4):
            msg[a] = jnp.concatenate(sums[2 * a : 2 * a + 2], axis=0)

        @pl.loop(0, 32)
        def _(j):
            a, tt = div(j, 8), rem(j, 8)
            me = is_me(4 * x + a, tt)

            @unless(me)
            def _():
                final(a, tt).start()

            @pl.when(me)
            def _():
                fin[d * 2 + z] = msg[a]

    def do(name, f, *args):
        with scope(name):
            return f(*args)

    @pl.loop(0, 6)
    def _(four):
        do("project", project, four)

        @pl.when(four == 0)
        def _():
            do("barrier_wait", everyone_is_here)
            phase1(0)

        @pl.when(four == 2)
        def _():
            phase1(1)

        @pl.when(four == 3)
        def _():
            do("phase2_0", phase2, 0)

        @pl.when(four == 4)
        def _():
            phase1(2)

    do("train_finish", train_finish)
    do("phase2_1", phase2, 1)
    do("moments_over_dp", moments_over_dp)
    do("phase2_2", phase2, 2)
    do("sketches_out", sketches_out)
    do("share_1", share_sketch, 1)
    do("moments_back", moments_back)
    do("sketches_across", sketches_across)
    do("share_2", share_sketch, 2)
    inv_out, inv_in = do("inverses", inverses)
    weights = do("solve", solve, inv_out, inv_in)
    train_positions, query_positions = tin.shape[1], qin.shape[1]
    scale = 1.0 / (RANK * math.sqrt(train_positions * query_positions))
    do("score", score, weights, scale)

    with scope("drain"):
        wait(acc.at[pl.ds(0, 21)], send)
        wait(part.at[pl.ds(0, 29)], msend)
        wait(part.at[pl.ds(0, 46)], bsend)
        wait(qall.at[pl.ds(0, 6)], qsend)
    with scope("final_wait"):
        diagonal_or_not(lambda n: wait(fin.at[pl.ds(0, n)], frecv))
    with scope("final_drain"):
        diagonal_or_not(lambda n: wait(fin.at[pl.ds(0, n)], fsend))
    low, high = fin[0], fin[16]
    for j in range(1, 16):
        low = low + fin[j]
        high = high + fin[j + 16]
    out_ref[:, :BLOCK] = low
    out_ref[:, BLOCK:] = high


def on_device(tin, tgr, tlen, qin, qgr, qlen, pin, pout):
    hbm = pl.BlockSpec(memory_space=pltpu.HBM)
    features, units = pin.shape[0], pout.shape[1]
    dma = pltpu.SemaphoreType.DMA
    return pl.pallas_call(
        kernel,
        out_shape=jax.ShapeDtypeStruct((tin.shape[0], DP * qin.shape[0]), F32),
        in_specs=[hbm] * 8,
        out_specs=pl.BlockSpec(memory_space=pltpu.VMEM),
        scratch_shapes=[
            pltpu.SMEM(tlen.shape, jnp.int32),
            pltpu.SMEM(qlen.shape, jnp.int32),
            pltpu.VMEM((24 * BLOCK, features), BF16),
            pltpu.VMEM((2, 24 * BLOCK, units), BF16),
            pltpu.VMEM((2, BLOCK, features), BF16),
            pltpu.VMEM((2, BLOCK, units), BF16),
            pltpu.VMEM((24, HALF + BLOCK, BLOCK), F32),
            pltpu.VMEM((3, 3, HALF, BLOCK), F32),
            pltpu.VMEM((3, 3, HALF + BLOCK, BLOCK), F32),
            pltpu.VMEM((3, 3, HALF + BLOCK, BLOCK), F32),
            pltpu.VMEM((96, 16, BLOCK), F32),
            pltpu.VMEM((16, BLOCK), F32),
            pltpu.VMEM((16, BLOCK), F32),
            pltpu.VMEM((8, HALF, BLOCK), F32),
            pltpu.VMEM((4, 2, BLOCK), F32),
            pltpu.VMEM((32, 2, BLOCK), F32),
            dma((4,)), dma((2,)), dma((2,)),
            dma, dma((3, 3)), dma((3,)), dma, dma((3,)), dma, dma((3,)), dma, dma((2,)), dma, dma,
        ],
        compiler_params=pltpu.CompilerParams(
            collective_id=0, has_side_effects=True, vmem_limit_bytes=56 * 1024 * 1024
        ),
    )(tlen, qlen, tin, tgr, qin, qgr, pin.T, pout.transpose(0, 2, 1))


def solution(mesh):
    placed = (
        P("dp", None, "tensor"),
        P("dp", None, None, "tensor"),
        P("dp"),
        P("dp", None, "tensor"),
        P("dp", None, None, "tensor"),
        P("dp"),
        P("tensor", None),
        P(None, "tensor", None),
    )
    return jax.shard_map(
        on_device, mesh=mesh, in_specs=placed, out_specs=P("dp", None), check_vma=False
    )
```

```python
import contextlib
import functools
import math

import jax
import jax.numpy as jnp
from jax import lax
from jax.experimental import pallas as pl
from jax.experimental.pallas import tpu as pltpu
from jax.sharding import PartitionSpec as P

MESH = pl.DeviceIdType.MESH
SCOPES = False


def scope(name):
    return jax.named_scope(name) if SCOPES else contextlib.nullcontext()


F32 = jnp.float32
BF16 = jnp.bfloat16
DAMPING = 0.1
RANK = 64
BLOCK = 128
HALF = 64
DP = 16
DOUBLINGS = 7
ROUTES = ((1, 5, 4, 1), (3, 2, 1, 2), (4, 7, 3, 0))


def chebyshev():
    low = DAMPING / RANK
    high = 1.0 + low
    return 2.0 / (high + low), (high + low) / (high - low)


def rem(a, b):
    return lax.rem(a, jnp.int32(b))


def div(a, b):
    return lax.div(a, jnp.int32(b))


def split(v):
    high = v.astype(BF16)
    return high, (v - high.astype(F32)).astype(BF16)


def kernel(
    tlen_hbm, qlen_hbm, tin, tgr, qin, qgr, pin, pout, out_ref,
    tlen, qlen, xin, xgr, wip, wop, acc, far, near, last, part, msum, bsum, qall, msg, fin,
    wsem, isem, gsem, send, recv1, recv2, msend, mrecv, bsend, brecv, qsend, qrecv, fsend, frecv,
):
    d = lax.axis_index("dp").astype(jnp.int32)
    t = lax.axis_index("tensor").astype(jnp.int32)
    z, x = div(t, 4), rem(t, 4)
    column = div(d, 4)
    on_diagonal = column == x
    core, chip = rem(d, 2), div(d, 2)
    leads = core == 1

    def flip(m):
        m = jnp.int32(m)
        mx, mz = rem(m, 4), div(m, 4)
        low = rem(x + mx, 2)
        high = rem(div(x, 2) + div(mx, 2), 2)
        return rem(z + mz, 2) * 4 + high * 2 + low

    def remote(src, dst, ssem, rsem, dd, tt):
        return pltpu.make_async_remote_copy(
            src_ref=src, dst_ref=dst, send_sem=ssem, recv_sem=rsem,
            device_id=(dd, tt), device_id_type=MESH,
        )

    def wait(ref, sem):
        pltpu.make_async_copy(ref, ref, sem).wait()

    def is_me(dd, tt):
        return jnp.logical_and(dd == d, tt == t)

    def unless(condition):
        return pl.when(jnp.logical_not(condition))

    def items(four):
        second = rem(four, 2)
        return (7 - 3 * second, 6 - 3 * second, 5 - 4 * second, 2 - 2 * second)

    def load(four, query):
        sem = rem(four, 2)
        for k, m in enumerate(items(four)):
            item = flip(m)
            if query:
                q = item * 2 + (div(four, 2) - 1)
                a, b = qin.at[q], qgr.at[q]
            else:
                rows = pl.ds(pl.multiple_of(rem(item, 4) * BLOCK, BLOCK), BLOCK)
                e = div(item, 4)
                a, b = tin.at[e, rows, :], tgr.at[e, :, rows, :]
            to = pl.ds((four * 4 + k) * BLOCK, BLOCK)
            pltpu.make_async_copy(a, xin.at[to], isem.at[sem]).start()
            pltpu.make_async_copy(b, xgr.at[:, to], gsem.at[sem]).start()

    with scope("start_loads"):
        pltpu.make_async_copy(pin, wip.at[0, :RANK], wsem.at[0]).start()
        pltpu.make_async_copy(pin, wip.at[1, RANK:], wsem.at[0]).start()
        pltpu.make_async_copy(pout.at[0], wop.at[0, :RANK], wsem.at[1]).start()
        pltpu.make_async_copy(pout.at[1], wop.at[1, RANK:], wsem.at[1]).start()

        @pl.loop(0, 2)
        def _(four):
            load(four, False)

        lengths = (
            pltpu.make_async_copy(tlen_hbm, tlen, wsem.at[2]),
            pltpu.make_async_copy(qlen_hbm, qlen, wsem.at[3]),
        )
        for c in lengths:
            c.start()

    barrier = pltpu.get_barrier_semaphore()

    def greet(dd, tt):
        pl.semaphore_signal(barrier, inc=1, device_id=(dd, tt), device_id_type=MESH)

    with scope("greet"):

        @pl.loop(1, 16)
        def _(j):
            greet(rem(d + j, DP), t)

        @pl.loop(1, 8)
        def _(m):
            greet(d, flip(8 - m))

    with scope("weights"):
        wip[0, RANK:] = jnp.zeros(pin.shape, BF16)
        wip[1, :RANK] = jnp.zeros(pin.shape, BF16)
        wop[0, RANK:] = jnp.zeros(pout.shape[1:], BF16)
        wop[1, :RANK] = jnp.zeros(pout.shape[1:], BF16)
        wait(wip.at[0], wsem.at[0])
        wait(wop.at[0], wsem.at[1])
        for c in lengths:
            c.wait()

    def times(rows, turned):
        return lax.dot_general(
            rows, turned, (((1,), (1,)), ((), ())), preferred_element_type=F32
        )

    def project(four):
        r, sem = div(four, 2), rem(four, 2)
        rows = pl.ds(four * 4 * BLOCK, 4 * BLOCK)
        wait(xin.at[rows], isem.at[sem])
        wait(xgr.at[:, rows], gsem.at[sem])

        @pl.when(four < 4)
        def _():
            load(four + 2, True)

        ins = xin[rows].reshape(4, 2, HALF, -1)
        ins = times(ins[:, 0].reshape(4 * HALF, -1), wip[0]) + times(
            ins[:, 1].reshape(4 * HALF, -1), wip[1]
        )
        outs = times(xgr[0, rows], wop[0]) + times(xgr[1, rows], wop[1])
        for k, m in enumerate(items(four)):
            slot = r * 8 + m
            acc[slot, :HALF] = ins[k * HALF : (k + 1) * HALF]
            acc[slot, HALF:] = outs[k * BLOCK : (k + 1) * BLOCK]

    def everyone_is_here():
        pl.semaphore_wait(barrier, 22)

    def phase1(r):
        for k, (g, _, _, p) in enumerate(ROUTES):
            remote(
                acc.at[r * 8 + 6, pl.ds(HALF * p, HALF)], far.at[r, k],
                send, recv1.at[r, k], d, flip(6 ^ g),
            ).start()
        for k, (_, item, via, _) in enumerate(ROUTES):
            remote(
                acc.at[r * 8 + item], near.at[r, k], send, recv1.at[r, k], d, flip(via)
            ).start()

    def phase2(r):
        for k, (g, _, _, p) in enumerate(ROUTES):
            wait(part.at[pl.ds(0, 16)], recv1.at[r, k])
            mine = r * 8 + g
            rows = slice(HALF * p, HALF * (p + 1))
            acc[mine] = acc[mine] + near[r, k]
            acc[mine, rows] = acc[mine, rows] + far[r, k]
            remote(
                acc.at[mine], last.at[r, k], send, recv2.at[r], d, flip(g)
            ).start()

    def summed(r):
        wait(last.at[r], recv2.at[r])
        return acc[r * 8] + last[r, 0] + last[r, 1] + last[r, 2]

    row64 = lax.broadcasted_iota(jnp.int32, (HALF, BLOCK), 0)
    lane64 = lax.broadcasted_iota(jnp.int32, (HALF, BLOCK), 1)
    left = lane64 < HALF

    def finished(total, length):
        position = jnp.where(left, row64, row64 + HALF)
        inputs = jnp.where(position < length, total[:HALF], 0.0)
        turned = pltpu.roll(inputs, HALF, 1)
        twice = jnp.concatenate(
            [jnp.where(left, inputs, turned), jnp.where(left, turned, inputs)], axis=0
        ).astype(BF16)
        outputs = jnp.concatenate(
            [
                jnp.where(row64 < length, total[HALF:BLOCK], 0.0),
                jnp.where(row64 + HALF < length, total[BLOCK:], 0.0),
            ],
            axis=0,
        )
        return twice, outputs.astype(BF16), outputs.T.astype(BF16)

    def fold(full):
        return jnp.where(left, full[:HALF], full[HALF:])

    def query_sketch(total, r):
        length = qlen[t * 2 + (r - 1)]
        twice, _, turned = finished(total, length)
        return fold(jnp.dot(turned, twice, preferred_element_type=F32))

    def share(r, m):
        mine = qall.at[(r - 1) * 4 + x]
        return remote(mine, mine, qsend, qrecv.at[r - 1], d, flip(m))

    def share_sketch(r):
        with scope("summed"):
            total = summed(r)
        qall[(r - 1) * 4 + x] = query_sketch(total, r)
        for m in (2, 1, 3):
            share(r, m).start()

    def moment1(m):
        slot = 16 - 8 * core + m
        return remote(
            part.at[flip(m)], part.at[slot], msend, mrecv.at[0], 2 * chip + 1, flip(m)
        )

    def moment2(j):
        other = 2 * rem(chip + j, 8) + 1
        return remote(msum, part.at[24 + chip], msend, mrecv.at[1], other, t)

    def moment3(m, to):
        piece = part.at[32 + t]
        return remote(piece, piece, msend, mrecv.at[2], 2 * chip + to, flip(m))

    def sketch1(m):
        return remote(
            part.at[40 + rem(flip(m), 4)], part.at[44 + m], bsend, brecv.at[0], d, flip(m)
        )

    def sketch2(j):
        return remote(bsum, part.at[48 + d], bsend, brecv.at[1], rem(d + j, DP), t)

    def sketch3(m):
        return remote(
            part.at[pl.ds(48 + 4 * rem(flip(m), 4), 4)], part.at[pl.ds(64 + 4 * t, 4)],
            bsend, brecv.at[2], d, flip(m),
        )

    def train_finish():
        with scope("summed"):
            total = summed(0)
        length = tlen[z] - x * BLOCK
        twice, outputs, turned = finished(total, length)
        products = jnp.dot(
            turned, jnp.concatenate([outputs, twice], axis=1), preferred_element_type=F32
        )
        ins = lax.dot_general(
            twice, twice, (((0,), (0,)), ((), ())), preferred_element_type=F32
        )
        live = jnp.minimum(jnp.maximum(length, 0), BLOCK).astype(F32)
        part[0:4] = fold(products[:, :BLOCK]).reshape(4, 16, BLOCK)
        part[4:8] = jnp.where(left, ins[:HALF], live).reshape(4, 16, BLOCK)
        for m in range(7, 0, -1):
            moment1(m).start()
        unless(leads)(lambda: moment1(0).start())
        part[40:44] = fold(products[:, BLOCK:]).reshape(4, 16, BLOCK)
        for m in range(1, 4):
            sketch1(m).start()

    def moments_over_dp():
        @pl.when(leads)
        def _():
            wait(part.at[pl.ds(9, 15)], mrecv.at[0])
            total = part[t]
            for slot in range(9, 24):
                total = total + part[slot]
            msum[...] = total
            part[24 + chip] = total
            for j in range(1, 8):
                moment2(j).start()

    def sketches_out():
        wait(part.at[pl.ds(45, 3)], brecv.at[0])
        total = part[40 + x]
        for m in range(1, 4):
            total = total + part[44 + m]
        bsum[...] = total
        part[48 + d] = total

        @pl.loop(1, 16)
        def _(j):
            sketch2(j).start()

    def sketches_across():
        wait(part.at[pl.ds(48, 15)], brecv.at[1])
        part[pl.ds(64 + 4 * t, 4)] = part[pl.ds(48 + 4 * x, 4)]
        for m in range(7, 0, -1):
            sketch3(m).start()

    def moments_back():
        @pl.when(leads)
        def _():
            wait(part.at[pl.ds(24, 7)], mrecv.at[1])
            total = part[24]
            for slot in range(25, 32):
                total = total + part[slot]
            part[32 + t] = total
            for m in range(7, -1, -1):
                moment3(m, 0).start()
                if m:
                    moment3(m, 1).start()

    def wide(v):
        zero = jnp.zeros_like(v)
        return jnp.concatenate(
            [jnp.where(left, v, zero), jnp.where(left, zero, v)], axis=0
        )

    def product(lhs, rhs):
        lh, ll = split(lhs)
        rh, rl = split(rhs)
        both = jnp.dot(
            jnp.concatenate([lh, ll], axis=1),
            jnp.concatenate(
                [
                    jnp.concatenate([rh, rl], axis=1),
                    jnp.concatenate([rh, jnp.zeros_like(rl)], axis=1),
                ],
                axis=0,
            ),
            preferred_element_type=F32,
        )
        return both[:, : rhs.shape[1]] + both[:, rhs.shape[1] :]

    exact = functools.partial(
        jnp.dot, precision=lax.Precision.HIGHEST, preferred_element_type=F32
    )

    def invert(matrices):
        eye = jnp.where(rem(lane64, HALF) == row64, 1.0, 0.0).astype(F32)
        weight, start = chebyshev()

        def double(_, carry):
            value, state = carry
            following = 2.0 * value * value - 1.0
            g = 2.0 * value * value / following
            doubled = []
            for left_over, inverse in state:
                both = product(
                    jnp.concatenate([left_over, inverse], axis=0), wide(left_over)
                )
                doubled.append(
                    (g * both[:HALF] - (g - 1.0) * eye, g * (inverse + both[HALF:]))
                )
            return following, tuple(doubled)

        state = tuple((eye - weight * a, weight * eye) for a in matrices)
        _, state = lax.fori_loop(
            0, DOUBLINGS, double, (jnp.full((1, BLOCK), start, F32), state)
        )
        results = []
        for a, (_, inverse) in zip(matrices, state):
            error = exact(a, wide(inverse))
            results.append(2.0 * inverse - exact(inverse, wide(error)))
        return results

    def inverses():
        with scope("wait_moment3"):
            pl.when(leads)(lambda: wait(part.at[pl.ds(32, 7)], mrecv.at[2]))
            unless(leads)(lambda: wait(part.at[pl.ds(32, 8)], mrecv.at[2]))
        whole = part[32:40].reshape(2 * HALF, BLOCK)
        outs, ins = whole[:HALF], whole[HALF:]
        live = jnp.max(jnp.where(left, 0.0, ins))
        ins = jnp.where(left, ins, pltpu.roll(ins, HALF, 1))
        diagonal = rem(lane64, HALF) == row64
        left_row = left[0:1]

        def traces(v):
            on = jnp.sum(jnp.where(diagonal, v, 0.0), axis=0, keepdims=True)
            a = jnp.sum(jnp.where(left_row, on, 0.0), axis=1, keepdims=True)
            b = jnp.sum(jnp.where(left_row, 0.0, on), axis=1, keepdims=True)
            return jnp.where(left_row, a, b)

        trace_out, trace_in = traces(outs), traces(ins)
        added = jnp.where(diagonal, DAMPING / RANK, 0.0).astype(F32)
        inv_out, inv_in = invert([outs / trace_out + added, ins / trace_in + added])
        return inv_out * (live / trace_out), inv_in * (live / trace_in)

    def diagonal_or_not(f):
        pl.when(on_diagonal)(functools.partial(f, 31))
        unless(on_diagonal)(functools.partial(f, 32))

    def solve(inv_out, inv_in):
        with scope("wait_sketches"):
            wait(part.at[pl.ds(64, 28)], brecv.at[2])
        wide_out = wide(inv_out)
        solved = []
        for e in range(8):
            sketch = jnp.concatenate(
                [part[64 + 4 * (4 * (e % 2) + q) + e // 2] for q in range(4)], axis=0
            )
            solved.append(
                fold(product(wide_out, jnp.concatenate([sketch, sketch], axis=0)))
            )
        return product(jnp.concatenate(solved, axis=0), wide(inv_in))

    def final(a, tt):
        return remote(msg.at[a], fin.at[d * 2 + z], fsend, frecv, 4 * x + a, tt)

    def score(weights, scale):
        with scope("wait_share"):
            for r in range(2):
                wait(qall.at[pl.ds(0, 3)], qrecv.at[r])
        queries = qall[...]
        rows = []
        for e in range(8):
            rows.append(
                jnp.sum(queries * weights[e * HALF : (e + 1) * HALF][None], axis=1)
            )
        sums = exact(jnp.concatenate(rows, axis=0), jnp.ones((BLOCK, BLOCK), F32))
        row = lax.broadcasted_iota(jnp.int32, (HALF, BLOCK), 0)
        lane = lax.broadcasted_iota(jnp.int32, (HALF, BLOCK), 1)
        query = 8 * z + 2 * rem(row, 4) + rem(div(row, 4), 2)
        sums = jnp.where(lane == rem(d, 8) * 16 + query, sums * scale, 0.0)
        sums = [
            jnp.sum(sums[e * 8 : (e + 1) * 8], axis=0, keepdims=True) for e in range(8)
        ]
        for a in range(4):
            msg[a] = jnp.concatenate(sums[2 * a : 2 * a + 2], axis=0)

        @pl.loop(0, 32)
        def _(j):
            a, tt = div(j, 8), rem(j, 8)
            me = is_me(4 * x + a, tt)

            @unless(me)
            def _():
                final(a, tt).start()

            @pl.when(me)
            def _():
                fin[d * 2 + z] = msg[a]

    def do(name, f, *args):
        with scope(name):
            return f(*args)

    @pl.loop(0, 6)
    def _(four):
        do("project", project, four)

        @pl.when(four == 0)
        def _():
            do("barrier_wait", everyone_is_here)
            phase1(0)

        @pl.when(four == 2)
        def _():
            phase1(1)

        @pl.when(four == 3)
        def _():
            do("phase2_0", phase2, 0)

        @pl.when(four == 4)
        def _():
            phase1(2)

    do("train_finish", train_finish)
    do("phase2_1", phase2, 1)
    do("sketches_out", sketches_out)
    do("moments_over_dp", moments_over_dp)
    do("phase2_2", phase2, 2)
    do("share_1", share_sketch, 1)
    do("moments_back", moments_back)
    do("sketches_across", sketches_across)
    do("share_2", share_sketch, 2)
    inv_out, inv_in = do("inverses", inverses)
    weights = do("solve", solve, inv_out, inv_in)
    train_positions, query_positions = tin.shape[1], qin.shape[1]
    scale = 1.0 / (RANK * math.sqrt(train_positions * query_positions))
    do("score", score, weights, scale)

    with scope("drain"):
        wait(acc.at[pl.ds(0, 21)], send)
        pl.when(leads)(lambda: wait(part.at[pl.ds(0, 29)], msend))
        unless(leads)(lambda: wait(part.at[pl.ds(0, 8)], msend))
        wait(part.at[pl.ds(0, 46)], bsend)
        wait(qall.at[pl.ds(0, 6)], qsend)
    with scope("final_wait"):
        diagonal_or_not(lambda n: wait(fin.at[pl.ds(0, n)], frecv))
    with scope("final_drain"):
        diagonal_or_not(lambda n: wait(fin.at[pl.ds(0, n)], fsend))
    low, high = fin[0], fin[16]
    for j in range(1, 16):
        low = low + fin[j]
        high = high + fin[j + 16]
    out_ref[:, :BLOCK] = low
    out_ref[:, BLOCK:] = high


def on_device(tin, tgr, tlen, qin, qgr, qlen, pin, pout):
    hbm = pl.BlockSpec(memory_space=pltpu.HBM)
    features, units = pin.shape[0], pout.shape[1]
    dma = pltpu.SemaphoreType.DMA
    return pl.pallas_call(
        kernel,
        out_shape=jax.ShapeDtypeStruct((tin.shape[0], DP * qin.shape[0]), F32),
        in_specs=[hbm] * 8,
        out_specs=pl.BlockSpec(memory_space=pltpu.VMEM),
        scratch_shapes=[
            pltpu.SMEM(tlen.shape, jnp.int32),
            pltpu.SMEM(qlen.shape, jnp.int32),
            pltpu.VMEM((24 * BLOCK, features), BF16),
            pltpu.VMEM((2, 24 * BLOCK, units), BF16),
            pltpu.VMEM((2, BLOCK, features), BF16),
            pltpu.VMEM((2, BLOCK, units), BF16),
            pltpu.VMEM((24, HALF + BLOCK, BLOCK), F32),
            pltpu.VMEM((3, 3, HALF, BLOCK), F32),
            pltpu.VMEM((3, 3, HALF + BLOCK, BLOCK), F32),
            pltpu.VMEM((3, 3, HALF + BLOCK, BLOCK), F32),
            pltpu.VMEM((96, 16, BLOCK), F32),
            pltpu.VMEM((16, BLOCK), F32),
            pltpu.VMEM((16, BLOCK), F32),
            pltpu.VMEM((8, HALF, BLOCK), F32),
            pltpu.VMEM((4, 2, BLOCK), F32),
            pltpu.VMEM((32, 2, BLOCK), F32),
            dma((4,)), dma((2,)), dma((2,)),
            dma, dma((3, 3)), dma((3,)), dma, dma((3,)), dma, dma((3,)), dma, dma((2,)), dma, dma,
        ],
        compiler_params=pltpu.CompilerParams(
            collective_id=0, has_side_effects=True, vmem_limit_bytes=56 * 1024 * 1024
        ),
    )(tlen, qlen, tin, tgr, qin, qgr, pin.T, pout.transpose(0, 2, 1))


def solution(mesh):
    placed = (
        P("dp", None, "tensor"),
        P("dp", None, None, "tensor"),
        P("dp"),
        P("dp", None, "tensor"),
        P("dp", None, None, "tensor"),
        P("dp"),
        P("tensor", None),
        P(None, "tensor", None),
    )
    return jax.shard_map(
        on_device, mesh=mesh, in_specs=placed, out_specs=P("dp", None), check_vma=False
    )
```

```python
import contextlib
import functools
import math

import jax
import jax.numpy as jnp
from jax import lax
from jax.experimental import pallas as pl
from jax.experimental.pallas import tpu as pltpu
from jax.sharding import PartitionSpec as P

MESH = pl.DeviceIdType.MESH
SCOPES = False


def scope(name):
    return jax.named_scope(name) if SCOPES else contextlib.nullcontext()


F32 = jnp.float32
BF16 = jnp.bfloat16
DAMPING = 0.1
RANK = 64
BLOCK = 128
HALF = 64
DP = 16
DOUBLINGS = 7
ROUTES = ((1, 5, 4, 1), (3, 2, 1, 2), (4, 7, 3, 0))


def chebyshev():
    low = DAMPING / RANK
    high = 1.0 + low
    return 2.0 / (high + low), (high + low) / (high - low)


def rem(a, b):
    return lax.rem(a, jnp.int32(b))


def div(a, b):
    return lax.div(a, jnp.int32(b))


def split(v):
    high = v.astype(BF16)
    return high, (v - high.astype(F32)).astype(BF16)


def kernel(
    tlen_hbm, qlen_hbm, tin, tgr, qin, qgr, pin, pout, out_ref,
    tlen, qlen, xin, xgr, wip, wop, acc, far, near, last, part, msum, bsum, qall, msg, fin,
    wsem, isem, gsem, send, recv1, recv2, msend, mrecv, bsend, brecv, qsend, qrecv, fsend, frecv,
):
    d = lax.axis_index("dp").astype(jnp.int32)
    t = lax.axis_index("tensor").astype(jnp.int32)
    z, x = div(t, 4), rem(t, 4)
    column = div(d, 4)
    on_diagonal = column == x
    core, chip = rem(d, 2), div(d, 2)
    leads = core == 1

    def flip(m):
        m = jnp.int32(m)
        mx, mz = rem(m, 4), div(m, 4)
        low = rem(x + mx, 2)
        high = rem(div(x, 2) + div(mx, 2), 2)
        return rem(z + mz, 2) * 4 + high * 2 + low

    def remote(src, dst, ssem, rsem, dd, tt):
        return pltpu.make_async_remote_copy(
            src_ref=src, dst_ref=dst, send_sem=ssem, recv_sem=rsem,
            device_id=(dd, tt), device_id_type=MESH,
        )

    def wait(ref, sem):
        pltpu.make_async_copy(ref, ref, sem).wait()

    def is_me(dd, tt):
        return jnp.logical_and(dd == d, tt == t)

    def unless(condition):
        return pl.when(jnp.logical_not(condition))

    def items(four):
        second = rem(four, 2)
        return (7 - 3 * second, 6 - 3 * second, 5 - 4 * second, 2 - 2 * second)

    def load(four, query):
        sem = rem(four, 2)
        for k, m in enumerate(items(four)):
            item = flip(m)
            if query:
                q = item * 2 + (div(four, 2) - 1)
                a, b = qin.at[q], qgr.at[q]
            else:
                rows = pl.ds(pl.multiple_of(rem(item, 4) * BLOCK, BLOCK), BLOCK)
                e = div(item, 4)
                a, b = tin.at[e, rows, :], tgr.at[e, :, rows, :]
            to = pl.ds((four * 4 + k) * BLOCK, BLOCK)
            pltpu.make_async_copy(a, xin.at[to], isem.at[sem]).start()
            pltpu.make_async_copy(b, xgr.at[:, to], gsem.at[sem]).start()

    with scope("start_loads"):
        pltpu.make_async_copy(pin, wip.at[0, :RANK], wsem.at[0]).start()
        pltpu.make_async_copy(pin, wip.at[1, RANK:], wsem.at[0]).start()
        pltpu.make_async_copy(pout.at[0], wop.at[0, :RANK], wsem.at[1]).start()
        pltpu.make_async_copy(pout.at[1], wop.at[1, RANK:], wsem.at[1]).start()

        @pl.loop(0, 2)
        def _(four):
            load(four, False)

        lengths = (
            pltpu.make_async_copy(tlen_hbm, tlen, wsem.at[2]),
            pltpu.make_async_copy(qlen_hbm, qlen, wsem.at[3]),
        )
        for c in lengths:
            c.start()

    barrier = pltpu.get_barrier_semaphore()

    def greet(dd, tt):
        pl.semaphore_signal(barrier, inc=1, device_id=(dd, tt), device_id_type=MESH)

    with scope("greet"):

        @pl.loop(1, 16)
        def _(j):
            greet(rem(d + j, DP), t)

        @pl.loop(1, 8)
        def _(m):
            greet(d, flip(8 - m))

    with scope("weights"):
        wip[0, RANK:] = jnp.zeros(pin.shape, BF16)
        wip[1, :RANK] = jnp.zeros(pin.shape, BF16)
        wop[0, RANK:] = jnp.zeros(pout.shape[1:], BF16)
        wop[1, :RANK] = jnp.zeros(pout.shape[1:], BF16)
        wait(wip.at[0], wsem.at[0])
        wait(wop.at[0], wsem.at[1])
        for c in lengths:
            c.wait()

    def times(rows, turned):
        return lax.dot_general(
            rows, turned, (((1,), (1,)), ((), ())), preferred_element_type=F32
        )

    def project(four):
        r, sem = div(four, 2), rem(four, 2)
        rows = pl.ds(four * 4 * BLOCK, 4 * BLOCK)
        wait(xin.at[rows], isem.at[sem])
        wait(xgr.at[:, rows], gsem.at[sem])

        @pl.when(four < 4)
        def _():
            load(four + 2, True)

        ins = xin[rows].reshape(4, 2, HALF, -1)
        ins = times(ins[:, 0].reshape(4 * HALF, -1), wip[0]) + times(
            ins[:, 1].reshape(4 * HALF, -1), wip[1]
        )
        outs = times(xgr[0, rows], wop[0]) + times(xgr[1, rows], wop[1])
        for k, m in enumerate(items(four)):
            slot = r * 8 + m
            acc[slot, :HALF] = ins[k * HALF : (k + 1) * HALF]
            acc[slot, HALF:] = outs[k * BLOCK : (k + 1) * BLOCK]

    def everyone_is_here():
        pl.semaphore_wait(barrier, 22)

    def phase1(r):
        for k, (g, _, _, p) in enumerate(ROUTES):
            remote(
                acc.at[r * 8 + 6, pl.ds(HALF * p, HALF)], far.at[r, k],
                send, recv1.at[r, k], d, flip(6 ^ g),
            ).start()
        for k, (_, item, via, _) in enumerate(ROUTES):
            remote(
                acc.at[r * 8 + item], near.at[r, k], send, recv1.at[r, k], d, flip(via)
            ).start()

    def phase2(r):
        for k, (g, _, _, p) in enumerate(ROUTES):
            wait(part.at[pl.ds(0, 16)], recv1.at[r, k])
            mine = r * 8 + g
            rows = slice(HALF * p, HALF * (p + 1))
            acc[mine] = acc[mine] + near[r, k]
            acc[mine, rows] = acc[mine, rows] + far[r, k]
            remote(
                acc.at[mine], last.at[r, k], send, recv2.at[r], d, flip(g)
            ).start()

    def summed(r):
        wait(last.at[r], recv2.at[r])
        return acc[r * 8] + last[r, 0] + last[r, 1] + last[r, 2]

    row64 = lax.broadcasted_iota(jnp.int32, (HALF, BLOCK), 0)
    lane64 = lax.broadcasted_iota(jnp.int32, (HALF, BLOCK), 1)
    left = lane64 < HALF

    def finished(total, length):
        position = jnp.where(left, row64, row64 + HALF)
        inputs = jnp.where(position < length, total[:HALF], 0.0)
        turned = pltpu.roll(inputs, HALF, 1)
        twice = jnp.concatenate(
            [jnp.where(left, inputs, turned), jnp.where(left, turned, inputs)], axis=0
        ).astype(BF16)
        outputs = jnp.concatenate(
            [
                jnp.where(row64 < length, total[HALF:BLOCK], 0.0),
                jnp.where(row64 + HALF < length, total[BLOCK:], 0.0),
            ],
            axis=0,
        )
        return twice, outputs.astype(BF16), outputs.T.astype(BF16)

    def fold(full):
        return jnp.where(left, full[:HALF], full[HALF:])

    def query_sketch(total, r):
        length = qlen[t * 2 + (r - 1)]
        twice, _, turned = finished(total, length)
        return fold(jnp.dot(turned, twice, preferred_element_type=F32))

    def share(r, m):
        mine = qall.at[(r - 1) * 4 + x]
        return remote(mine, mine, qsend, qrecv.at[r - 1], d, flip(m))

    def share_sketch(r):
        with scope("summed"):
            total = summed(r)
        qall[(r - 1) * 4 + x] = query_sketch(total, r)
        for m in (2, 1, 3):
            share(r, m).start()

    def moment1(m):
        slot = 16 - 8 * core + m
        return remote(
            part.at[flip(m)], part.at[slot], msend, mrecv.at[0], 2 * chip + 1, flip(m)
        )

    def moment2(j):
        other = 2 * rem(chip + j, 8) + 1
        return remote(msum, part.at[24 + chip], msend, mrecv.at[1], other, t)

    def moment3(m, to):
        piece = part.at[32 + t]
        return remote(piece, piece, msend, mrecv.at[2], 2 * chip + to, flip(m))

    def sketch1(m):
        return remote(
            part.at[40 + rem(flip(m), 4)], part.at[44 + m], bsend, brecv.at[0], d, flip(m)
        )

    def sketch2(j):
        other = 2 * rem(chip + j, 8) + core
        return remote(bsum, part.at[48 + chip], bsend, brecv.at[1], other, t)

    scored = 64 + 16 * core

    def sketch3(m):
        return remote(
            part.at[pl.ds(48 + 2 * rem(flip(m), 4), 2)],
            part.at[pl.ds(scored + 2 * t, 2)],
            bsend, brecv.at[2], d, flip(m),
        )

    def sketch4():
        mine = part.at[pl.ds(scored, 16)]
        return remote(mine, mine, bsend, brecv.at[3], 2 * chip + 1 - core, t)

    def train_finish():
        with scope("summed"):
            total = summed(0)
        length = tlen[z] - x * BLOCK
        twice, outputs, turned = finished(total, length)
        products = jnp.dot(
            turned, jnp.concatenate([outputs, twice], axis=1), preferred_element_type=F32
        )
        ins = lax.dot_general(
            twice, twice, (((0,), (0,)), ((), ())), preferred_element_type=F32
        )
        live = jnp.minimum(jnp.maximum(length, 0), BLOCK).astype(F32)
        part[0:4] = fold(products[:, :BLOCK]).reshape(4, 16, BLOCK)
        part[4:8] = jnp.where(left, ins[:HALF], live).reshape(4, 16, BLOCK)
        for m in range(7, 0, -1):
            moment1(m).start()
        unless(leads)(lambda: moment1(0).start())
        part[40:44] = fold(products[:, BLOCK:]).reshape(4, 16, BLOCK)
        for m in range(1, 4):
            sketch1(m).start()

    def moments_over_dp():
        @pl.when(leads)
        def _():
            wait(part.at[pl.ds(9, 15)], mrecv.at[0])
            total = part[t]
            for slot in range(9, 24):
                total = total + part[slot]
            msum[...] = total
            part[24 + chip] = total
            for j in range(1, 8):
                moment2(j).start()

    def sketches_out():
        wait(part.at[pl.ds(45, 3)], brecv.at[0])
        total = part[40 + x]
        for m in range(1, 4):
            total = total + part[44 + m]
        bsum[...] = total
        part[48 + chip] = total
        for j in range(1, 8):
            sketch2(j).start()

    def sketches_across():
        wait(part.at[pl.ds(48, 7)], brecv.at[1])
        part[pl.ds(scored + 2 * t, 2)] = part[pl.ds(48 + 2 * x, 2)]
        for m in range(7, 0, -1):
            sketch3(m).start()

    def swap_sketches():
        with scope("wait_sketches"):
            wait(part.at[pl.ds(64, 14)], brecv.at[2])
        sketch4().start()

    def moments_back():
        @pl.when(leads)
        def _():
            wait(part.at[pl.ds(24, 7)], mrecv.at[1])
            total = part[24]
            for slot in range(25, 32):
                total = total + part[slot]
            part[32 + t] = total
            for m in range(7, -1, -1):
                moment3(m, 0).start()
                if m:
                    moment3(m, 1).start()

    def wide(v):
        zero = jnp.zeros_like(v)
        return jnp.concatenate(
            [jnp.where(left, v, zero), jnp.where(left, zero, v)], axis=0
        )

    def product(lhs, rhs):
        lh, ll = split(lhs)
        rh, rl = split(rhs)
        both = jnp.dot(
            jnp.concatenate([lh, ll], axis=1),
            jnp.concatenate(
                [
                    jnp.concatenate([rh, rl], axis=1),
                    jnp.concatenate([rh, jnp.zeros_like(rl)], axis=1),
                ],
                axis=0,
            ),
            preferred_element_type=F32,
        )
        return both[:, : rhs.shape[1]] + both[:, rhs.shape[1] :]

    exact = functools.partial(
        jnp.dot, precision=lax.Precision.HIGHEST, preferred_element_type=F32
    )

    def invert(matrices):
        eye = jnp.where(rem(lane64, HALF) == row64, 1.0, 0.0).astype(F32)
        weight, start = chebyshev()

        def double(i, carry):
            pl.when(i == 5)(swap_sketches)
            value, state = carry
            following = 2.0 * value * value - 1.0
            g = 2.0 * value * value / following
            doubled = []
            for left_over, inverse in state:
                both = product(
                    jnp.concatenate([left_over, inverse], axis=0), wide(left_over)
                )
                doubled.append(
                    (g * both[:HALF] - (g - 1.0) * eye, g * (inverse + both[HALF:]))
                )
            return following, tuple(doubled)

        state = tuple((eye - weight * a, weight * eye) for a in matrices)
        _, state = lax.fori_loop(
            0, DOUBLINGS, double, (jnp.full((1, BLOCK), start, F32), state)
        )
        results = []
        for a, (_, inverse) in zip(matrices, state):
            error = exact(a, wide(inverse))
            results.append(2.0 * inverse - exact(inverse, wide(error)))
        return results

    def inverses():
        with scope("wait_moment3"):
            pl.when(leads)(lambda: wait(part.at[pl.ds(32, 7)], mrecv.at[2]))
            unless(leads)(lambda: wait(part.at[pl.ds(32, 8)], mrecv.at[2]))
        whole = part[32:40].reshape(2 * HALF, BLOCK)
        outs, ins = whole[:HALF], whole[HALF:]
        live = jnp.max(jnp.where(left, 0.0, ins))
        ins = jnp.where(left, ins, pltpu.roll(ins, HALF, 1))
        diagonal = rem(lane64, HALF) == row64
        left_row = left[0:1]

        def traces(v):
            on = jnp.sum(jnp.where(diagonal, v, 0.0), axis=0, keepdims=True)
            a = jnp.sum(jnp.where(left_row, on, 0.0), axis=1, keepdims=True)
            b = jnp.sum(jnp.where(left_row, 0.0, on), axis=1, keepdims=True)
            return jnp.where(left_row, a, b)

        trace_out, trace_in = traces(outs), traces(ins)
        added = jnp.where(diagonal, DAMPING / RANK, 0.0).astype(F32)
        inv_out, inv_in = invert([outs / trace_out + added, ins / trace_in + added])
        return inv_out * (live / trace_out), inv_in * (live / trace_in)

    def diagonal_or_not(f):
        pl.when(on_diagonal)(functools.partial(f, 31))
        unless(on_diagonal)(functools.partial(f, 32))

    def solve(inv_out, inv_in):
        with scope("wait_swap"):
            wait(part.at[pl.ds(64, 16)], brecv.at[3])
        wide_out = wide(inv_out)
        solved = []
        for e in range(8):
            first = 64 + 16 * (e // 2 % 2) + 8 * (e % 2) + e // 4
            sketch = jnp.concatenate([part[first + 2 * q] for q in range(4)], axis=0)
            solved.append(
                fold(product(wide_out, jnp.concatenate([sketch, sketch], axis=0)))
            )
        return product(jnp.concatenate(solved, axis=0), wide(inv_in))

    def final(a, tt):
        return remote(msg.at[a], fin.at[d * 2 + z], fsend, frecv, 4 * x + a, tt)

    def score(weights, scale):
        with scope("wait_share"):
            for r in range(2):
                wait(qall.at[pl.ds(0, 3)], qrecv.at[r])
        queries = qall[...]
        rows = []
        for e in range(8):
            rows.append(
                jnp.sum(queries * weights[e * HALF : (e + 1) * HALF][None], axis=1)
            )
        sums = exact(jnp.concatenate(rows, axis=0), jnp.ones((BLOCK, BLOCK), F32))
        row = lax.broadcasted_iota(jnp.int32, (HALF, BLOCK), 0)
        lane = lax.broadcasted_iota(jnp.int32, (HALF, BLOCK), 1)
        query = 8 * z + 2 * rem(row, 4) + rem(div(row, 4), 2)
        sums = jnp.where(lane == rem(d, 8) * 16 + query, sums * scale, 0.0)
        sums = [
            jnp.sum(sums[e * 8 : (e + 1) * 8], axis=0, keepdims=True) for e in range(8)
        ]
        for a in range(4):
            msg[a] = jnp.concatenate(sums[2 * a : 2 * a + 2], axis=0)

        @pl.loop(0, 8)
        def _(j):
            tt = rem(t + 6 + j, 8)
            for a in range(4):

                @unless(is_me(4 * x + a, tt))
                def _(a=a):
                    final(a, tt).start()

        @pl.when(on_diagonal)
        def _():
            fin[d * 2 + z] = msg[rem(d, 4)]

    def do(name, f, *args):
        with scope(name):
            return f(*args)

    @pl.loop(0, 6)
    def _(four):
        do("project", project, four)

        @pl.when(four == 0)
        def _():
            do("barrier_wait", everyone_is_here)
            phase1(0)

        @pl.when(four == 2)
        def _():
            phase1(1)

        @pl.when(four == 3)
        def _():
            do("phase2_0", phase2, 0)

        @pl.when(four == 4)
        def _():
            phase1(2)

    do("train_finish", train_finish)
    do("phase2_1", phase2, 1)
    do("sketches_out", sketches_out)
    do("moments_over_dp", moments_over_dp)
    do("phase2_2", phase2, 2)
    do("share_1", share_sketch, 1)
    do("moments_back", moments_back)
    do("sketches_across", sketches_across)
    do("share_2", share_sketch, 2)
    inv_out, inv_in = do("inverses", inverses)
    weights = do("solve", solve, inv_out, inv_in)
    train_positions, query_positions = tin.shape[1], qin.shape[1]
    scale = 1.0 / (RANK * math.sqrt(train_positions * query_positions))
    do("score", score, weights, scale)

    with scope("drain"):
        wait(acc.at[pl.ds(0, 21)], send)
        pl.when(leads)(lambda: wait(part.at[pl.ds(0, 29)], msend))
        unless(leads)(lambda: wait(part.at[pl.ds(0, 8)], msend))
        wait(part.at[pl.ds(0, 40)], bsend)
        wait(qall.at[pl.ds(0, 6)], qsend)
    with scope("final_wait"):
        diagonal_or_not(lambda n: wait(fin.at[pl.ds(0, n)], frecv))
    with scope("final_drain"):
        diagonal_or_not(lambda n: wait(fin.at[pl.ds(0, n)], fsend))
    low, high = fin[0], fin[16]
    for j in range(1, 16):
        low = low + fin[j]
        high = high + fin[j + 16]
    out_ref[:, :BLOCK] = low
    out_ref[:, BLOCK:] = high


def on_device(tin, tgr, tlen, qin, qgr, qlen, pin, pout):
    hbm = pl.BlockSpec(memory_space=pltpu.HBM)
    features, units = pin.shape[0], pout.shape[1]
    dma = pltpu.SemaphoreType.DMA
    return pl.pallas_call(
        kernel,
        out_shape=jax.ShapeDtypeStruct((tin.shape[0], DP * qin.shape[0]), F32),
        in_specs=[hbm] * 8,
        out_specs=pl.BlockSpec(memory_space=pltpu.VMEM),
        scratch_shapes=[
            pltpu.SMEM(tlen.shape, jnp.int32),
            pltpu.SMEM(qlen.shape, jnp.int32),
            pltpu.VMEM((24 * BLOCK, features), BF16),
            pltpu.VMEM((2, 24 * BLOCK, units), BF16),
            pltpu.VMEM((2, BLOCK, features), BF16),
            pltpu.VMEM((2, BLOCK, units), BF16),
            pltpu.VMEM((24, HALF + BLOCK, BLOCK), F32),
            pltpu.VMEM((3, 3, HALF, BLOCK), F32),
            pltpu.VMEM((3, 3, HALF + BLOCK, BLOCK), F32),
            pltpu.VMEM((3, 3, HALF + BLOCK, BLOCK), F32),
            pltpu.VMEM((96, 16, BLOCK), F32),
            pltpu.VMEM((16, BLOCK), F32),
            pltpu.VMEM((16, BLOCK), F32),
            pltpu.VMEM((8, HALF, BLOCK), F32),
            pltpu.VMEM((4, 2, BLOCK), F32),
            pltpu.VMEM((32, 2, BLOCK), F32),
            dma((4,)), dma((2,)), dma((2,)),
            dma, dma((3, 3)), dma((3,)), dma, dma((3,)), dma, dma((4,)), dma, dma((2,)), dma, dma,
        ],
        compiler_params=pltpu.CompilerParams(
            collective_id=0, has_side_effects=True, vmem_limit_bytes=56 * 1024 * 1024
        ),
    )(tlen, qlen, tin, tgr, qin, qgr, pin.T, pout.transpose(0, 2, 1))


def solution(mesh):
    placed = (
        P("dp", None, "tensor"),
        P("dp", None, None, "tensor"),
        P("dp"),
        P("dp", None, "tensor"),
        P("dp", None, None, "tensor"),
        P("dp"),
        P("tensor", None),
        P(None, "tensor", None),
    )
    return jax.shard_map(
        on_device, mesh=mesh, in_specs=placed, out_specs=P("dp", None), check_vma=False
    )
```

```python
import contextlib
import functools
import math

import jax
import jax.numpy as jnp
from jax import lax
from jax.experimental import pallas as pl
from jax.experimental.pallas import tpu as pltpu
from jax.sharding import PartitionSpec as P

MESH = pl.DeviceIdType.MESH
SCOPES = False


def scope(name):
    return jax.named_scope(name) if SCOPES else contextlib.nullcontext()


F32 = jnp.float32
BF16 = jnp.bfloat16
DAMPING = 0.1
RANK = 64
BLOCK = 128
HALF = 64
DP = 16
DOUBLINGS = 7
ROUTES = ((1, 5, 4, 1), (3, 2, 1, 2), (4, 7, 3, 0))


def chebyshev():
    low = DAMPING / RANK
    high = 1.0 + low
    return 2.0 / (high + low), (high + low) / (high - low)


def rem(a, b):
    return lax.rem(a, jnp.int32(b))


def div(a, b):
    return lax.div(a, jnp.int32(b))


def split(v):
    high = v.astype(BF16)
    return high, (v - high.astype(F32)).astype(BF16)


def kernel(
    tlen_hbm, qlen_hbm, tin, tgr, qin, qgr, pin, pout, out_ref,
    tlen, qlen, xin, xgr, wip, wop, acc, far, near, last, part, msum, bsum, qall, msg, fin,
    wsem, isem, gsem, send, recv1, recv2, msend, mrecv, bsend, brecv, qsend, qrecv, fsend, frecv,
):
    d = lax.axis_index("dp").astype(jnp.int32)
    t = lax.axis_index("tensor").astype(jnp.int32)
    z, x = div(t, 4), rem(t, 4)
    column = div(d, 4)
    on_diagonal = column == x
    core, chip = rem(d, 2), div(d, 2)
    leads = core == 1

    def flip(m):
        m = jnp.int32(m)
        mx, mz = rem(m, 4), div(m, 4)
        low = rem(x + mx, 2)
        high = rem(div(x, 2) + div(mx, 2), 2)
        return rem(z + mz, 2) * 4 + high * 2 + low

    def remote(src, dst, ssem, rsem, dd, tt):
        return pltpu.make_async_remote_copy(
            src_ref=src, dst_ref=dst, send_sem=ssem, recv_sem=rsem,
            device_id=(dd, tt), device_id_type=MESH,
        )

    def wait(ref, sem):
        pltpu.make_async_copy(ref, ref, sem).wait()

    def is_me(dd, tt):
        return jnp.logical_and(dd == d, tt == t)

    def unless(condition):
        return pl.when(jnp.logical_not(condition))

    def items(four):
        second = rem(four, 2)
        return (7 - 3 * second, 6 - 3 * second, 5 - 4 * second, 2 - 2 * second)

    def load(four, query):
        sem = rem(four, 2)
        for k, m in enumerate(items(four)):
            item = flip(m)
            if query:
                q = item * 2 + (div(four, 2) - 1)
                a, b = qin.at[q], qgr.at[q]
            else:
                rows = pl.ds(pl.multiple_of(rem(item, 4) * BLOCK, BLOCK), BLOCK)
                e = div(item, 4)
                a, b = tin.at[e, rows, :], tgr.at[e, :, rows, :]
            to = pl.ds((four * 4 + k) * BLOCK, BLOCK)
            pltpu.make_async_copy(a, xin.at[to], isem.at[sem]).start()
            pltpu.make_async_copy(b, xgr.at[:, to], gsem.at[sem]).start()

    with scope("start_loads"):
        pltpu.make_async_copy(pin, wip.at[0, :RANK], wsem.at[0]).start()
        pltpu.make_async_copy(pin, wip.at[1, RANK:], wsem.at[0]).start()
        pltpu.make_async_copy(pout.at[0], wop.at[0, :RANK], wsem.at[1]).start()
        pltpu.make_async_copy(pout.at[1], wop.at[1, RANK:], wsem.at[1]).start()

        @pl.loop(0, 2)
        def _(four):
            load(four, False)

        lengths = (
            pltpu.make_async_copy(tlen_hbm, tlen, wsem.at[2]),
            pltpu.make_async_copy(qlen_hbm, qlen, wsem.at[3]),
        )
        for c in lengths:
            c.start()

    barrier = pltpu.get_barrier_semaphore()

    def greet(dd, tt):
        pl.semaphore_signal(barrier, inc=1, device_id=(dd, tt), device_id_type=MESH)

    with scope("greet"):

        @pl.loop(1, 16)
        def _(j):
            greet(rem(d + j, DP), t)

        @pl.loop(1, 8)
        def _(m):
            greet(d, flip(8 - m))

    with scope("weights"):
        wip[0, RANK:] = jnp.zeros(pin.shape, BF16)
        wip[1, :RANK] = jnp.zeros(pin.shape, BF16)
        wop[0, RANK:] = jnp.zeros(pout.shape[1:], BF16)
        wop[1, :RANK] = jnp.zeros(pout.shape[1:], BF16)
        wait(wip.at[0], wsem.at[0])
        wait(wop.at[0], wsem.at[1])
        for c in lengths:
            c.wait()

    def times(rows, turned):
        return lax.dot_general(
            rows, turned, (((1,), (1,)), ((), ())), preferred_element_type=F32
        )

    def project(four):
        r, sem = div(four, 2), rem(four, 2)
        rows = pl.ds(four * 4 * BLOCK, 4 * BLOCK)
        wait(xin.at[rows], isem.at[sem])
        wait(xgr.at[:, rows], gsem.at[sem])

        @pl.when(four < 4)
        def _():
            load(four + 2, True)

        ins = xin[rows].reshape(4, 2, HALF, -1)
        ins = times(ins[:, 0].reshape(4 * HALF, -1), wip[0]) + times(
            ins[:, 1].reshape(4 * HALF, -1), wip[1]
        )
        outs = times(xgr[0, rows], wop[0]) + times(xgr[1, rows], wop[1])
        for k, m in enumerate(items(four)):
            slot = r * 8 + m
            acc[slot, :HALF] = ins[k * HALF : (k + 1) * HALF]
            acc[slot, HALF:] = outs[k * BLOCK : (k + 1) * BLOCK]

    def everyone_is_here():
        pl.semaphore_wait(barrier, 22)

    def phase1(r):
        for k, (g, _, _, p) in enumerate(ROUTES):
            remote(
                acc.at[r * 8 + 6, pl.ds(HALF * p, HALF)], far.at[r, k],
                send, recv1.at[r, k], d, flip(6 ^ g),
            ).start()
        for k, (_, item, via, _) in enumerate(ROUTES):
            remote(
                acc.at[r * 8 + item], near.at[r, k], send, recv1.at[r, k], d, flip(via)
            ).start()

    def phase2(r):
        for k, (g, _, _, p) in enumerate(ROUTES):
            wait(part.at[pl.ds(0, 16)], recv1.at[r, k])
            mine = r * 8 + g
            rows = slice(HALF * p, HALF * (p + 1))
            acc[mine] = acc[mine] + near[r, k]
            acc[mine, rows] = acc[mine, rows] + far[r, k]
            remote(
                acc.at[mine], last.at[r, k], send, recv2.at[r], d, flip(g)
            ).start()

    def summed(r):
        wait(last.at[r], recv2.at[r])
        return acc[r * 8] + last[r, 0] + last[r, 1] + last[r, 2]

    row64 = lax.broadcasted_iota(jnp.int32, (HALF, BLOCK), 0)
    lane64 = lax.broadcasted_iota(jnp.int32, (HALF, BLOCK), 1)
    left = lane64 < HALF

    def finished(total, length):
        position = jnp.where(left, row64, row64 + HALF)
        inputs = jnp.where(position < length, total[:HALF], 0.0)
        turned = pltpu.roll(inputs, HALF, 1)
        twice = jnp.concatenate(
            [jnp.where(left, inputs, turned), jnp.where(left, turned, inputs)], axis=0
        ).astype(BF16)
        outputs = jnp.concatenate(
            [
                jnp.where(row64 < length, total[HALF:BLOCK], 0.0),
                jnp.where(row64 + HALF < length, total[BLOCK:], 0.0),
            ],
            axis=0,
        )
        return twice, outputs.astype(BF16), outputs.T.astype(BF16)

    def fold(full):
        return jnp.where(left, full[:HALF], full[HALF:])

    def query_sketch(total, r):
        length = qlen[t * 2 + (r - 1)]
        twice, _, turned = finished(total, length)
        return fold(jnp.dot(turned, twice, preferred_element_type=F32))

    def share(r, m):
        mine = qall.at[(r - 1) * 4 + x]
        return remote(mine, mine, qsend, qrecv.at[r - 1], d, flip(m))

    def share_sketch(r):
        with scope("summed"):
            total = summed(r)
        qall[(r - 1) * 4 + x] = query_sketch(total, r)
        for m in (2, 1, 3):
            share(r, m).start()

    def moment1(m):
        slot = 16 - 8 * core + m
        return remote(
            part.at[flip(m)], part.at[slot], msend, mrecv.at[0], 2 * chip + 1, flip(m)
        )

    def moment2(j):
        other = 2 * rem(chip + j, 8) + 1
        return remote(msum, part.at[24 + chip], msend, mrecv.at[1], other, t)

    def moment3(m, to):
        piece = part.at[32 + t]
        return remote(piece, piece, msend, mrecv.at[2], 2 * chip + to, flip(m))

    def sketch1(m):
        return remote(
            part.at[40 + rem(flip(m), 4)], part.at[44 + m], bsend, brecv.at[0], d, flip(m)
        )

    def sketch2(j):
        other = 2 * rem(chip + j, 8) + core
        return remote(bsum, part.at[48 + chip], bsend, brecv.at[1], other, t)

    scored = 64 + 16 * core

    def sketch3(m):
        return remote(
            part.at[pl.ds(48 + 2 * rem(flip(m), 4), 2)],
            part.at[pl.ds(scored + 2 * t, 2)],
            bsend, brecv.at[2], d, flip(m),
        )

    def sketch4():
        mine = part.at[pl.ds(scored, 16)]
        return remote(mine, mine, bsend, brecv.at[3], 2 * chip + 1 - core, t)

    def train_finish():
        with scope("summed"):
            total = summed(0)
        length = tlen[z] - x * BLOCK
        twice, outputs, turned = finished(total, length)
        outs = jnp.dot(turned, outputs, preferred_element_type=F32)
        ins = lax.dot_general(
            twice, twice, (((0,), (0,)), ((), ())), preferred_element_type=F32
        )
        live = jnp.minimum(jnp.maximum(length, 0), BLOCK).astype(F32)
        part[0:4] = fold(outs).reshape(4, 16, BLOCK)
        part[4:8] = jnp.where(left, ins[:HALF], live).reshape(4, 16, BLOCK)
        for m in range(7, 0, -1):
            moment1(m).start()
        unless(leads)(lambda: moment1(0).start())
        sketch = jnp.dot(turned, twice, preferred_element_type=F32)
        part[40:44] = fold(sketch).reshape(4, 16, BLOCK)
        for m in range(1, 4):
            sketch1(m).start()

    def moments_over_dp():
        @pl.when(leads)
        def _():
            wait(part.at[pl.ds(9, 15)], mrecv.at[0])
            total = part[t]
            for slot in range(9, 24):
                total = total + part[slot]
            msum[...] = total
            part[24 + chip] = total
            for j in range(1, 8):
                moment2(j).start()

    def sketches_out():
        wait(part.at[pl.ds(45, 3)], brecv.at[0])
        total = part[40 + x]
        for m in range(1, 4):
            total = total + part[44 + m]
        bsum[...] = total
        part[48 + chip] = total
        for j in range(1, 8):
            sketch2(j).start()

    def sketches_across():
        wait(part.at[pl.ds(48, 7)], brecv.at[1])
        part[pl.ds(scored + 2 * t, 2)] = part[pl.ds(48 + 2 * x, 2)]
        for m in range(7, 0, -1):
            sketch3(m).start()

    def swap_sketches():
        with scope("wait_sketches"):
            wait(part.at[pl.ds(64, 14)], brecv.at[2])
        sketch4().start()

    def moments_back():
        @pl.when(leads)
        def _():
            wait(part.at[pl.ds(24, 7)], mrecv.at[1])
            total = part[24]
            for slot in range(25, 32):
                total = total + part[slot]
            part[32 + t] = total
            for m in range(7, -1, -1):
                moment3(m, 0).start()
                if m:
                    moment3(m, 1).start()

    def wide(v):
        zero = jnp.zeros_like(v)
        return jnp.concatenate(
            [jnp.where(left, v, zero), jnp.where(left, zero, v)], axis=0
        )

    def product(lhs, rhs):
        lh, ll = split(lhs)
        rh, rl = split(rhs)
        both = jnp.dot(
            jnp.concatenate([lh, ll], axis=1),
            jnp.concatenate(
                [
                    jnp.concatenate([rh, rl], axis=1),
                    jnp.concatenate([rh, jnp.zeros_like(rl)], axis=1),
                ],
                axis=0,
            ),
            preferred_element_type=F32,
        )
        return both[:, : rhs.shape[1]] + both[:, rhs.shape[1] :]

    exact = functools.partial(
        jnp.dot, precision=lax.Precision.HIGHEST, preferred_element_type=F32
    )

    def invert(matrices):
        eye = jnp.where(rem(lane64, HALF) == row64, 1.0, 0.0).astype(F32)
        weight, start = chebyshev()

        def double(i, carry):
            pl.when(i == 5)(swap_sketches)
            value, state = carry
            following = 2.0 * value * value - 1.0
            g = 2.0 * value * value / following
            doubled = []
            for left_over, inverse in state:
                both = product(
                    jnp.concatenate([left_over, inverse], axis=0), wide(left_over)
                )
                doubled.append(
                    (g * both[:HALF] - (g - 1.0) * eye, g * (inverse + both[HALF:]))
                )
            return following, tuple(doubled)

        state = tuple((eye - weight * a, weight * eye) for a in matrices)
        _, state = lax.fori_loop(
            0, DOUBLINGS, double, (jnp.full((1, BLOCK), start, F32), state)
        )
        results = []
        for a, (_, inverse) in zip(matrices, state):
            error = exact(a, wide(inverse))
            results.append(2.0 * inverse - exact(inverse, wide(error)))
        return results

    def inverses():
        with scope("wait_moment3"):
            pl.when(leads)(lambda: wait(part.at[pl.ds(32, 7)], mrecv.at[2]))
            unless(leads)(lambda: wait(part.at[pl.ds(32, 8)], mrecv.at[2]))
        whole = part[32:40].reshape(2 * HALF, BLOCK)
        outs, ins = whole[:HALF], whole[HALF:]
        live = jnp.max(jnp.where(left, 0.0, ins))
        ins = jnp.where(left, ins, pltpu.roll(ins, HALF, 1))
        diagonal = rem(lane64, HALF) == row64
        left_row = left[0:1]

        def traces(v):
            on = jnp.sum(jnp.where(diagonal, v, 0.0), axis=0, keepdims=True)
            a = jnp.sum(jnp.where(left_row, on, 0.0), axis=1, keepdims=True)
            b = jnp.sum(jnp.where(left_row, 0.0, on), axis=1, keepdims=True)
            return jnp.where(left_row, a, b)

        trace_out, trace_in = traces(outs), traces(ins)
        added = jnp.where(diagonal, DAMPING / RANK, 0.0).astype(F32)
        inv_out, inv_in = invert([outs / trace_out + added, ins / trace_in + added])
        return inv_out * (live / trace_out), inv_in * (live / trace_in)

    def diagonal_or_not(f):
        pl.when(on_diagonal)(functools.partial(f, 31))
        unless(on_diagonal)(functools.partial(f, 32))

    def solve(inv_out, inv_in):
        with scope("wait_swap"):
            wait(part.at[pl.ds(64, 16)], brecv.at[3])
        wide_out = wide(inv_out)
        solved = []
        for e in range(8):
            first = 64 + 16 * (e // 2 % 2) + 8 * (e % 2) + e // 4
            sketch = jnp.concatenate([part[first + 2 * q] for q in range(4)], axis=0)
            solved.append(
                fold(product(wide_out, jnp.concatenate([sketch, sketch], axis=0)))
            )
        return product(jnp.concatenate(solved, axis=0), wide(inv_in))

    def final(a, tt):
        return remote(msg.at[a], fin.at[d * 2 + z], fsend, frecv, 4 * x + a, tt)

    def score(weights, scale):
        with scope("wait_share"):
            for r in range(2):
                wait(qall.at[pl.ds(0, 3)], qrecv.at[r])
        queries = qall[...]
        rows = []
        for e in range(8):
            rows.append(
                jnp.sum(queries * weights[e * HALF : (e + 1) * HALF][None], axis=1)
            )
        sums = exact(jnp.concatenate(rows, axis=0), jnp.ones((BLOCK, BLOCK), F32))
        row = lax.broadcasted_iota(jnp.int32, (HALF, BLOCK), 0)
        lane = lax.broadcasted_iota(jnp.int32, (HALF, BLOCK), 1)
        query = 8 * z + 2 * rem(row, 4) + rem(div(row, 4), 2)
        sums = jnp.where(lane == rem(d, 8) * 16 + query, sums * scale, 0.0)
        sums = [
            jnp.sum(sums[e * 8 : (e + 1) * 8], axis=0, keepdims=True) for e in range(8)
        ]
        for a in range(4):
            msg[a] = jnp.concatenate(sums[2 * a : 2 * a + 2], axis=0)

        @pl.loop(0, 8)
        def _(j):
            tt = rem(t + 6 + j, 8)
            for a in range(4):

                @unless(is_me(4 * x + a, tt))
                def _(a=a):
                    final(a, tt).start()

        @pl.when(on_diagonal)
        def _():
            fin[d * 2 + z] = msg[rem(d, 4)]

    def do(name, f, *args):
        with scope(name):
            return f(*args)

    @pl.loop(0, 6)
    def _(four):
        do("project", project, four)

        @pl.when(four == 0)
        def _():
            do("barrier_wait", everyone_is_here)
            phase1(0)

        @pl.when(four == 2)
        def _():
            phase1(1)

        @pl.when(four == 3)
        def _():
            do("phase2_0", phase2, 0)

        @pl.when(four == 5)
        def _():
            phase1(2)

    do("train_finish", train_finish)
    do("phase2_1", phase2, 1)
    do("sketches_out", sketches_out)
    do("moments_over_dp", moments_over_dp)
    do("phase2_2", phase2, 2)
    do("share_1", share_sketch, 1)
    do("moments_back", moments_back)
    do("sketches_across", sketches_across)
    do("share_2", share_sketch, 2)
    inv_out, inv_in = do("inverses", inverses)
    weights = do("solve", solve, inv_out, inv_in)
    train_positions, query_positions = tin.shape[1], qin.shape[1]
    scale = 1.0 / (RANK * math.sqrt(train_positions * query_positions))
    do("score", score, weights, scale)

    with scope("drain"):
        wait(acc.at[pl.ds(0, 21)], send)
        pl.when(leads)(lambda: wait(part.at[pl.ds(0, 29)], msend))
        unless(leads)(lambda: wait(part.at[pl.ds(0, 8)], msend))
        wait(part.at[pl.ds(0, 40)], bsend)
        wait(qall.at[pl.ds(0, 6)], qsend)
    with scope("final_wait"):
        diagonal_or_not(lambda n: wait(fin.at[pl.ds(0, n)], frecv))
    with scope("final_drain"):
        diagonal_or_not(lambda n: wait(fin.at[pl.ds(0, n)], fsend))
    low, high = fin[0], fin[16]
    for j in range(1, 16):
        low = low + fin[j]
        high = high + fin[j + 16]
    out_ref[:, :BLOCK] = low
    out_ref[:, BLOCK:] = high


def on_device(tin, tgr, tlen, qin, qgr, qlen, pin, pout):
    hbm = pl.BlockSpec(memory_space=pltpu.HBM)
    features, units = pin.shape[0], pout.shape[1]
    dma = pltpu.SemaphoreType.DMA
    return pl.pallas_call(
        kernel,
        out_shape=jax.ShapeDtypeStruct((tin.shape[0], DP * qin.shape[0]), F32),
        in_specs=[hbm] * 8,
        out_specs=pl.BlockSpec(memory_space=pltpu.VMEM),
        scratch_shapes=[
            pltpu.SMEM(tlen.shape, jnp.int32),
            pltpu.SMEM(qlen.shape, jnp.int32),
            pltpu.VMEM((24 * BLOCK, features), BF16),
            pltpu.VMEM((2, 24 * BLOCK, units), BF16),
            pltpu.VMEM((2, BLOCK, features), BF16),
            pltpu.VMEM((2, BLOCK, units), BF16),
            pltpu.VMEM((24, HALF + BLOCK, BLOCK), F32),
            pltpu.VMEM((3, 3, HALF, BLOCK), F32),
            pltpu.VMEM((3, 3, HALF + BLOCK, BLOCK), F32),
            pltpu.VMEM((3, 3, HALF + BLOCK, BLOCK), F32),
            pltpu.VMEM((96, 16, BLOCK), F32),
            pltpu.VMEM((16, BLOCK), F32),
            pltpu.VMEM((16, BLOCK), F32),
            pltpu.VMEM((8, HALF, BLOCK), F32),
            pltpu.VMEM((4, 2, BLOCK), F32),
            pltpu.VMEM((32, 2, BLOCK), F32),
            dma((4,)), dma((2,)), dma((2,)),
            dma, dma((3, 3)), dma((3,)), dma, dma((3,)), dma, dma((4,)), dma, dma((2,)), dma, dma,
        ],
        compiler_params=pltpu.CompilerParams(
            collective_id=0, has_side_effects=True, vmem_limit_bytes=56 * 1024 * 1024
        ),
    )(tlen, qlen, tin, tgr, qin, qgr, pin.T, pout.transpose(0, 2, 1))


def solution(mesh):
    placed = (
        P("dp", None, "tensor"),
        P("dp", None, None, "tensor"),
        P("dp"),
        P("dp", None, "tensor"),
        P("dp", None, None, "tensor"),
        P("dp"),
        P("tensor", None),
        P(None, "tensor", None),
    )
    return jax.shard_map(
        on_device, mesh=mesh, in_specs=placed, out_specs=P("dp", None), check_vma=False
    )
```

```python
import contextlib
import functools
import math

import jax
import jax.numpy as jnp
from jax import lax
from jax.experimental import pallas as pl
from jax.experimental.pallas import tpu as pltpu
from jax.sharding import PartitionSpec as P

MESH = pl.DeviceIdType.MESH
SCOPES = False


def scope(name):
    return jax.named_scope(name) if SCOPES else contextlib.nullcontext()


F32 = jnp.float32
BF16 = jnp.bfloat16
DAMPING = 0.1
RANK = 64
BLOCK = 128
HALF = 64
DP = 16
DOUBLINGS = 7
ROUTES = ((1, 5, 4, 1), (3, 2, 1, 2), (4, 7, 3, 0))


def chebyshev():
    low = DAMPING / RANK
    high = 1.0 + low
    return 2.0 / (high + low), (high + low) / (high - low)


def rem(a, b):
    return lax.rem(a, jnp.int32(b))


def div(a, b):
    return lax.div(a, jnp.int32(b))


def split(v):
    high = v.astype(BF16)
    return high, (v - high.astype(F32)).astype(BF16)


def kernel(
    tlen_hbm, qlen_hbm, tin, tgr, qin, qgr, pin, pout, out_ref,
    tlen, qlen, xin, xgr, wip, wop, acc, far, near, last, part, msum, bsum, qall, msg, fin,
    wsem, isem, gsem, send, recv1, recv2, msend, mrecv, bsend, brecv, qsend, qrecv, fsend, frecv,
):
    d = lax.axis_index("dp").astype(jnp.int32)
    t = lax.axis_index("tensor").astype(jnp.int32)
    z, x = div(t, 4), rem(t, 4)
    column = div(d, 4)
    on_diagonal = column == x
    core, chip = rem(d, 2), div(d, 2)
    leads = core == 1

    def flip(m):
        m = jnp.int32(m)
        mx, mz = rem(m, 4), div(m, 4)
        low = rem(x + mx, 2)
        high = rem(div(x, 2) + div(mx, 2), 2)
        return rem(z + mz, 2) * 4 + high * 2 + low

    def remote(src, dst, ssem, rsem, dd, tt):
        return pltpu.make_async_remote_copy(
            src_ref=src, dst_ref=dst, send_sem=ssem, recv_sem=rsem,
            device_id=(dd, tt), device_id_type=MESH,
        )

    def wait(ref, sem):
        pltpu.make_async_copy(ref, ref, sem).wait()

    def is_me(dd, tt):
        return jnp.logical_and(dd == d, tt == t)

    def unless(condition):
        return pl.when(jnp.logical_not(condition))

    def items(four):
        second = rem(four, 2)
        return (7 - 3 * second, 6 - 3 * second, 5 - 4 * second, 2 - 2 * second)

    def load(four, query):
        sem = rem(four, 2)
        for k, m in enumerate(items(four)):
            item = flip(m)
            if query:
                q = item * 2 + (div(four, 2) - 1)
                a, b = qin.at[q], qgr.at[q]
            else:
                rows = pl.ds(pl.multiple_of(rem(item, 4) * BLOCK, BLOCK), BLOCK)
                e = div(item, 4)
                a, b = tin.at[e, rows, :], tgr.at[e, :, rows, :]
            to = pl.ds((four * 4 + k) * BLOCK, BLOCK)
            pltpu.make_async_copy(a, xin.at[to], isem.at[sem]).start()
            pltpu.make_async_copy(b, xgr.at[:, to], gsem.at[sem]).start()

    with scope("start_loads"):
        pltpu.make_async_copy(pin, wip.at[0, :RANK], wsem.at[0]).start()
        pltpu.make_async_copy(pin, wip.at[1, RANK:], wsem.at[0]).start()
        pltpu.make_async_copy(pout.at[0], wop.at[0, :RANK], wsem.at[1]).start()
        pltpu.make_async_copy(pout.at[1], wop.at[1, RANK:], wsem.at[1]).start()

        @pl.loop(0, 2)
        def _(four):
            load(four, False)

        lengths = (
            pltpu.make_async_copy(tlen_hbm, tlen, wsem.at[2]),
            pltpu.make_async_copy(qlen_hbm, qlen, wsem.at[3]),
        )
        for c in lengths:
            c.start()

    barrier = pltpu.get_barrier_semaphore()

    def greet(dd, tt):
        pl.semaphore_signal(barrier, inc=1, device_id=(dd, tt), device_id_type=MESH)

    with scope("greet"):

        @pl.loop(1, 16)
        def _(j):
            greet(rem(d + j, DP), t)

        @pl.loop(1, 8)
        def _(m):
            greet(d, flip(8 - m))

    with scope("weights"):
        wip[0, RANK:] = jnp.zeros(pin.shape, BF16)
        wip[1, :RANK] = jnp.zeros(pin.shape, BF16)
        wop[0, RANK:] = jnp.zeros(pout.shape[1:], BF16)
        wop[1, :RANK] = jnp.zeros(pout.shape[1:], BF16)
        wait(wip.at[0], wsem.at[0])
        wait(wop.at[0], wsem.at[1])
        for c in lengths:
            c.wait()

    def times(rows, turned):
        return lax.dot_general(
            rows, turned, (((1,), (1,)), ((), ())), preferred_element_type=F32
        )

    def project(four):
        r, sem = div(four, 2), rem(four, 2)
        rows = pl.ds(four * 4 * BLOCK, 4 * BLOCK)
        wait(xin.at[rows], isem.at[sem])
        wait(xgr.at[:, rows], gsem.at[sem])

        @pl.when(four < 4)
        def _():
            load(four + 2, True)

        ins = xin[rows].reshape(4, 2, HALF, -1)
        ins = times(ins[:, 0].reshape(4 * HALF, -1), wip[0]) + times(
            ins[:, 1].reshape(4 * HALF, -1), wip[1]
        )
        outs = times(xgr[0, rows], wop[0]) + times(xgr[1, rows], wop[1])
        for k, m in enumerate(items(four)):
            slot = r * 8 + m
            acc[slot, :HALF] = ins[k * HALF : (k + 1) * HALF]
            acc[slot, HALF:] = outs[k * BLOCK : (k + 1) * BLOCK]

    def everyone_is_here():
        pl.semaphore_wait(barrier, 22)

    def phase1(r):
        for k, (g, _, _, p) in enumerate(ROUTES):
            remote(
                acc.at[r * 8 + 6, pl.ds(HALF * p, HALF)], far.at[r, k],
                send, recv1.at[r, k], d, flip(6 ^ g),
            ).start()
        for k, (_, item, via, _) in enumerate(ROUTES):
            remote(
                acc.at[r * 8 + item], near.at[r, k], send, recv1.at[r, k], d, flip(via)
            ).start()

    def phase2(r):
        for k, (g, _, _, p) in enumerate(ROUTES):
            wait(part.at[pl.ds(0, 16)], recv1.at[r, k])
            mine = r * 8 + g
            rows = slice(HALF * p, HALF * (p + 1))
            acc[mine] = acc[mine] + near[r, k]
            acc[mine, rows] = acc[mine, rows] + far[r, k]
            remote(
                acc.at[mine], last.at[r, k], send, recv2.at[r], d, flip(g)
            ).start()

    def summed(r):
        wait(last.at[r], recv2.at[r])
        return acc[r * 8] + last[r, 0] + last[r, 1] + last[r, 2]

    row64 = lax.broadcasted_iota(jnp.int32, (HALF, BLOCK), 0)
    lane64 = lax.broadcasted_iota(jnp.int32, (HALF, BLOCK), 1)
    left = lane64 < HALF

    def finished(total, length):
        position = jnp.where(left, row64, row64 + HALF)
        inputs = jnp.where(position < length, total[:HALF], 0.0)
        turned = pltpu.roll(inputs, HALF, 1)
        twice = jnp.concatenate(
            [jnp.where(left, inputs, turned), jnp.where(left, turned, inputs)], axis=0
        ).astype(BF16)
        outputs = jnp.concatenate(
            [
                jnp.where(row64 < length, total[HALF:BLOCK], 0.0),
                jnp.where(row64 + HALF < length, total[BLOCK:], 0.0),
            ],
            axis=0,
        )
        return twice, outputs.astype(BF16), outputs.T.astype(BF16)

    def fold(full):
        return jnp.where(left, full[:HALF], full[HALF:])

    def query_sketch(total, r):
        length = qlen[t * 2 + (r - 1)]
        twice, _, turned = finished(total, length)
        return fold(jnp.dot(turned, twice, preferred_element_type=F32))

    def share(r, m):
        mine = qall.at[(r - 1) * 4 + x]
        return remote(mine, mine, qsend, qrecv.at[r - 1], d, flip(m))

    def share_sketch(r):
        with scope("summed"):
            total = summed(r)
        qall[(r - 1) * 4 + x] = query_sketch(total, r)
        for m in (2, 1, 3):
            share(r, m).start()

    def moment1(m):
        slot = 16 - 8 * core + m
        return remote(
            part.at[flip(m)], part.at[slot], msend, mrecv.at[0], 2 * chip + 1, flip(m)
        )

    def moment2(j):
        other = 2 * rem(chip + j, 8) + 1
        return remote(msum, part.at[24 + chip], msend, mrecv.at[1], other, t)

    def moment3(m, to):
        piece = part.at[32 + t]
        return remote(piece, piece, msend, mrecv.at[2], 2 * chip + to, flip(m))

    def sketch1(m):
        return remote(
            part.at[40 + rem(flip(m), 4)], part.at[44 + m], bsend, brecv.at[0], d, flip(m)
        )

    def sketch2(j):
        other = 2 * rem(chip + j, 8) + core
        return remote(bsum, part.at[48 + chip], bsend, brecv.at[1], other, t)

    scored = 64 + 16 * core

    def sketch3(m):
        return remote(
            part.at[pl.ds(48 + 2 * rem(flip(m), 4), 2)],
            part.at[pl.ds(scored + 2 * t, 2)],
            bsend, brecv.at[2], d, flip(m),
        )

    def sketch4():
        mine = part.at[pl.ds(scored, 16)]
        return remote(mine, mine, bsend, brecv.at[3], 2 * chip + 1 - core, t)

    def train_finish():
        with scope("summed"):
            total = summed(0)
        length = tlen[z] - x * BLOCK
        twice, outputs, turned = finished(total, length)
        outs = jnp.dot(turned, outputs, preferred_element_type=F32)
        ins = lax.dot_general(
            twice, twice, (((0,), (0,)), ((), ())), preferred_element_type=F32
        )
        live = jnp.minimum(jnp.maximum(length, 0), BLOCK).astype(F32)
        part[0:4] = fold(outs).reshape(4, 16, BLOCK)
        part[4:8] = jnp.where(left, ins[:HALF], live).reshape(4, 16, BLOCK)
        for m in range(7, 0, -1):
            moment1(m).start()
        unless(leads)(lambda: moment1(0).start())
        sketch = jnp.dot(turned, twice, preferred_element_type=F32)
        part[40:44] = fold(sketch).reshape(4, 16, BLOCK)
        for m in range(1, 4):
            sketch1(m).start()

    def moments_over_dp():
        @pl.when(leads)
        def _():
            wait(part.at[pl.ds(9, 15)], mrecv.at[0])
            total = part[t]
            for slot in range(9, 24):
                total = total + part[slot]
            msum[...] = total
            part[24 + chip] = total
            for j in range(1, 8):
                moment2(j).start()

    def sketches_out():
        wait(part.at[pl.ds(45, 3)], brecv.at[0])
        total = part[40 + x]
        for m in range(1, 4):
            total = total + part[44 + m]
        bsum[...] = total
        part[48 + chip] = total
        for j in range(1, 8):
            sketch2(j).start()

    def sketches_across():
        wait(part.at[pl.ds(48, 7)], brecv.at[1])
        part[pl.ds(scored + 2 * t, 2)] = part[pl.ds(48 + 2 * x, 2)]
        for m in range(7, 0, -1):
            sketch3(m).start()

    def swap_sketches():
        with scope("wait_sketches"):
            wait(part.at[pl.ds(64, 14)], brecv.at[2])
        sketch4().start()

    def moments_back():
        @pl.when(leads)
        def _():
            wait(part.at[pl.ds(24, 7)], mrecv.at[1])
            total = part[24]
            for slot in range(25, 32):
                total = total + part[slot]
            part[32 + t] = total
            for m in range(7, -1, -1):
                moment3(m, 0).start()
                if m:
                    moment3(m, 1).start()

    def wide(v):
        zero = jnp.zeros_like(v)
        return jnp.concatenate(
            [jnp.where(left, v, zero), jnp.where(left, zero, v)], axis=0
        )

    def product(lhs, rhs):
        lh, ll = split(lhs)
        rh, rl = split(rhs)
        both = jnp.dot(
            jnp.concatenate([lh, ll], axis=1),
            jnp.concatenate(
                [
                    jnp.concatenate([rh, rl], axis=1),
                    jnp.concatenate([rh, jnp.zeros_like(rl)], axis=1),
                ],
                axis=0,
            ),
            preferred_element_type=F32,
        )
        return both[:, : rhs.shape[1]] + both[:, rhs.shape[1] :]

    exact = functools.partial(
        jnp.dot, precision=lax.Precision.HIGHEST, preferred_element_type=F32
    )

    def invert(matrices):
        eye = jnp.where(rem(lane64, HALF) == row64, 1.0, 0.0).astype(F32)
        weight, start = chebyshev()

        def double(i, carry):
            pl.when(i == 4)(swap_sketches)
            value, state = carry
            following = 2.0 * value * value - 1.0
            g = 2.0 * value * value / following
            doubled = []
            for left_over, inverse in state:
                both = product(
                    jnp.concatenate([left_over, inverse], axis=0), wide(left_over)
                )
                doubled.append(
                    (g * both[:HALF] - (g - 1.0) * eye, g * (inverse + both[HALF:]))
                )
            return following, tuple(doubled)

        state = tuple((eye - weight * a, weight * eye) for a in matrices)
        _, state = lax.fori_loop(
            0, DOUBLINGS, double, (jnp.full((1, BLOCK), start, F32), state)
        )
        results = []
        for a, (_, inverse) in zip(matrices, state):
            error = exact(a, wide(inverse))
            results.append(2.0 * inverse - exact(inverse, wide(error)))
        return results

    def inverses():
        with scope("wait_moment3"):
            pl.when(leads)(lambda: wait(part.at[pl.ds(32, 7)], mrecv.at[2]))
            unless(leads)(lambda: wait(part.at[pl.ds(32, 8)], mrecv.at[2]))
        whole = part[32:40].reshape(2 * HALF, BLOCK)
        outs, ins = whole[:HALF], whole[HALF:]
        live = jnp.max(jnp.where(left, 0.0, ins))
        ins = jnp.where(left, ins, pltpu.roll(ins, HALF, 1))
        diagonal = rem(lane64, HALF) == row64
        left_row = left[0:1]

        def traces(v):
            on = jnp.sum(jnp.where(diagonal, v, 0.0), axis=0, keepdims=True)
            a = jnp.sum(jnp.where(left_row, on, 0.0), axis=1, keepdims=True)
            b = jnp.sum(jnp.where(left_row, 0.0, on), axis=1, keepdims=True)
            return jnp.where(left_row, a, b)

        trace_out, trace_in = traces(outs), traces(ins)
        added = jnp.where(diagonal, DAMPING / RANK, 0.0).astype(F32)
        inv_out, inv_in = invert([outs / trace_out + added, ins / trace_in + added])
        return inv_out * (live / trace_out), inv_in * (live / trace_in)

    def diagonal_or_not(f):
        pl.when(on_diagonal)(functools.partial(f, 31))
        unless(on_diagonal)(functools.partial(f, 32))

    def solve(inv_out, inv_in):
        with scope("wait_swap"):
            wait(part.at[pl.ds(64, 16)], brecv.at[3])
        wide_out = wide(inv_out)
        solved = []
        for e in range(8):
            first = 64 + 16 * (e // 2 % 2) + 8 * (e % 2) + e // 4
            sketch = jnp.concatenate([part[first + 2 * q] for q in range(4)], axis=0)
            solved.append(
                fold(product(wide_out, jnp.concatenate([sketch, sketch], axis=0)))
            )
        return product(jnp.concatenate(solved, axis=0), wide(inv_in))

    def final(a, tt):
        return remote(msg.at[a], fin.at[d * 2 + z], fsend, frecv, 4 * x + a, tt)

    def score(weights, scale):
        with scope("wait_share"):
            for r in range(2):
                wait(qall.at[pl.ds(0, 3)], qrecv.at[r])
        queries = qall[...]
        rows = []
        for e in range(8):
            rows.append(
                jnp.sum(queries * weights[e * HALF : (e + 1) * HALF][None], axis=1)
            )
        sums = exact(jnp.concatenate(rows, axis=0), jnp.ones((BLOCK, BLOCK), F32))
        row = lax.broadcasted_iota(jnp.int32, (HALF, BLOCK), 0)
        lane = lax.broadcasted_iota(jnp.int32, (HALF, BLOCK), 1)
        query = 8 * z + 2 * rem(row, 4) + rem(div(row, 4), 2)
        sums = jnp.where(lane == rem(d, 8) * 16 + query, sums * scale, 0.0)
        sums = [
            jnp.sum(sums[e * 8 : (e + 1) * 8], axis=0, keepdims=True) for e in range(8)
        ]
        for a in range(4):
            msg[a] = jnp.concatenate(sums[2 * a : 2 * a + 2], axis=0)

        @pl.loop(0, 8)
        def _(j):
            tt = rem(t + 6 + j, 8)
            for a in range(4):

                @unless(is_me(4 * x + a, tt))
                def _(a=a):
                    final(a, tt).start()

        @pl.when(on_diagonal)
        def _():
            fin[d * 2 + z] = msg[rem(d, 4)]

    def do(name, f, *args):
        with scope(name):
            return f(*args)

    @pl.loop(0, 6)
    def _(four):
        do("project", project, four)

        @pl.when(four == 0)
        def _():
            do("barrier_wait", everyone_is_here)
            phase1(0)

        @pl.when(four == 2)
        def _():
            phase1(1)

        @pl.when(four == 3)
        def _():
            do("phase2_0", phase2, 0)

        @pl.when(four == 5)
        def _():
            phase1(2)

    do("train_finish", train_finish)
    do("phase2_1", phase2, 1)
    do("sketches_out", sketches_out)
    do("moments_over_dp", moments_over_dp)
    do("phase2_2", phase2, 2)
    do("share_1", share_sketch, 1)
    do("sketches_across", sketches_across)
    do("moments_back", moments_back)
    do("share_2", share_sketch, 2)
    inv_out, inv_in = do("inverses", inverses)
    weights = do("solve", solve, inv_out, inv_in)
    train_positions, query_positions = tin.shape[1], qin.shape[1]
    scale = 1.0 / (RANK * math.sqrt(train_positions * query_positions))
    do("score", score, weights, scale)

    with scope("drain"):
        wait(acc.at[pl.ds(0, 21)], send)
        pl.when(leads)(lambda: wait(part.at[pl.ds(0, 29)], msend))
        unless(leads)(lambda: wait(part.at[pl.ds(0, 8)], msend))
        wait(part.at[pl.ds(0, 40)], bsend)
        wait(qall.at[pl.ds(0, 6)], qsend)
    with scope("final_wait"):
        diagonal_or_not(lambda n: wait(fin.at[pl.ds(0, n)], frecv))
    with scope("final_drain"):
        diagonal_or_not(lambda n: wait(fin.at[pl.ds(0, n)], fsend))
    low, high = fin[0], fin[16]
    for j in range(1, 16):
        low = low + fin[j]
        high = high + fin[j + 16]
    out_ref[:, :BLOCK] = low
    out_ref[:, BLOCK:] = high


def on_device(tin, tgr, tlen, qin, qgr, qlen, pin, pout):
    hbm = pl.BlockSpec(memory_space=pltpu.HBM)
    features, units = pin.shape[0], pout.shape[1]
    dma = pltpu.SemaphoreType.DMA
    return pl.pallas_call(
        kernel,
        out_shape=jax.ShapeDtypeStruct((tin.shape[0], DP * qin.shape[0]), F32),
        in_specs=[hbm] * 8,
        out_specs=pl.BlockSpec(memory_space=pltpu.VMEM),
        scratch_shapes=[
            pltpu.SMEM(tlen.shape, jnp.int32),
            pltpu.SMEM(qlen.shape, jnp.int32),
            pltpu.VMEM((24 * BLOCK, features), BF16),
            pltpu.VMEM((2, 24 * BLOCK, units), BF16),
            pltpu.VMEM((2, BLOCK, features), BF16),
            pltpu.VMEM((2, BLOCK, units), BF16),
            pltpu.VMEM((24, HALF + BLOCK, BLOCK), F32),
            pltpu.VMEM((3, 3, HALF, BLOCK), F32),
            pltpu.VMEM((3, 3, HALF + BLOCK, BLOCK), F32),
            pltpu.VMEM((3, 3, HALF + BLOCK, BLOCK), F32),
            pltpu.VMEM((96, 16, BLOCK), F32),
            pltpu.VMEM((16, BLOCK), F32),
            pltpu.VMEM((16, BLOCK), F32),
            pltpu.VMEM((8, HALF, BLOCK), F32),
            pltpu.VMEM((4, 2, BLOCK), F32),
            pltpu.VMEM((32, 2, BLOCK), F32),
            dma((4,)), dma((2,)), dma((2,)),
            dma, dma((3, 3)), dma((3,)), dma, dma((3,)), dma, dma((4,)), dma, dma((2,)), dma, dma,
        ],
        compiler_params=pltpu.CompilerParams(
            collective_id=0, has_side_effects=True, vmem_limit_bytes=56 * 1024 * 1024
        ),
    )(tlen, qlen, tin, tgr, qin, qgr, pin.T, pout.transpose(0, 2, 1))


def solution(mesh):
    placed = (
        P("dp", None, "tensor"),
        P("dp", None, None, "tensor"),
        P("dp"),
        P("dp", None, "tensor"),
        P("dp", None, None, "tensor"),
        P("dp"),
        P("tensor", None),
        P(None, "tensor", None),
    )
    return jax.shard_map(
        on_device, mesh=mesh, in_specs=placed, out_specs=P("dp", None), check_vma=False
    )
```
